32 devices in a mesh: dp: 16 (over z, x, core), tensor: 2 (over y).
Axes of the slice: x: 2, y: 2, z: 4, core: 2. Of those that a mesh axis runs over, the one named last changes fastest.
Arguments:
- tokens: bfloat16 [8192, 1024], P('dp'), may hold values from -6 to 6
- cotangent: bfloat16 [8192, 1024], P('dp'), may hold values from -6 to 6
- segment: int32 [8192], P('dp'), may hold values from 0 to 7, never falling along the last dimension, each value on 1 to 6144 neighbouring positions
- variate: int32 [8192], P('dp'), may hold values from 0 to 3
- time: int32 [8192], P('dp'), may hold values from 0 to 4095
- w_qkv: bfloat16 [3, 1024, 1024], P(None, None, 'tensor'), may hold values from -0.1875 to 0.1875
- w_out: bfloat16 [1024, 1024], P('tensor'), may hold values from -2 to 2
- w_gateup: bfloat16 [2, 1024, 2816], P(None, None, 'tensor'), may hold values from -0.1875 to 0.1875
- w_down: bfloat16 [2816, 1024], P('tensor'), may hold values from -0.109375 to 0.109375
- attn_gain: float32 [1024], replicated, may hold values from 0.5 to 1.5
- mlp_gain: float32 [1024], replicated, may hold values from 0.5 to 1.5
- query_gain: float32 [64], replicated, may hold values from 0.5 to 1.5
- key_gain: float32 [64], replicated, may hold values from 0.5 to 1.5
- var_bias: float32 [2, 16], P(None, 'tensor'), may hold values from -4 to 4
Outputs:
- output: bfloat16 [8192, 1024], P('dp', 'tensor')
- grad_input: float32 [8192, 1024], P('dp', 'tensor')
- grad_qkv: float32 [3, 1024, 1024], P(None, None, 'tensor')
- grad_out: float32 [1024, 1024], P('tensor')
- grad_gateup: float32 [2, 1024, 2816], P(None, None, 'tensor')
- grad_down: float32 [2816, 1024], P('tensor')
- grad_attn_gain: float32 [1024], replicated
- grad_mlp_gain: float32 [1024], replicated
- grad_query_gain: float32 [64], replicated
- grad_key_gain: float32 [64], replicated
- grad_var_bias: float32 [2, 16], P(None, 'tensor')
The draws below stay inside these ranges and needn't reach their ends.
Inputs may be any that keep to these rules, and one draw needn't show every extreme that they name: `segment`: document numbers never fall along the tokens; all documents lie in the one packed sequence of 8192 tokens, each with at most 6144 tokens.
All inputs are finite; a program needn't handle non-finite values.
Results may differ from the reference program's by a relative error of at most 0.022.
Values may be sent and summed in bfloat16 or wider, within the bound.
A program may use at most 256 MiB of HBM per device.

```python
import math
import jax
import jax.numpy as jnp
import numpy as np
from jax import lax

D = 1024
HEADS = 16
HD = 64
FF = 2816
TOKENS = 8192
SEQ_LEN = 8192
DOCS = 8


def touch_ends(entries, rng, least, high):
    place = [jax.random.randint(jax.random.fold_in(rng, axis), (), 0, length) for axis, length in enumerate(entries.shape)]
    main_axis = entries.shape.index(max(entries.shape))
    neighbour = place[:main_axis] + [(place[main_axis] + 1) % entries.shape[main_axis]] + place[main_axis + 1:]
    return entries.at[tuple(place)].set(least).at[tuple(neighbour)].set(high)


def level_of(key, dims, cuts, low, largest):
    def one(dim, blocks):
        steps = jax.random.uniform(jax.random.fold_in(jax.random.fold_in(key, 6), dim), (blocks,), jnp.float32, low / len(cuts), largest / len(cuts))
        return jnp.repeat(jnp.exp(steps), dims[dim] // blocks).reshape((-1,) + (1,) * (len(dims) - dim - 1))

    factor_of = one(*cuts[0])
    for cut in cuts[1:]:
        factor_of = factor_of * one(*cut)
    return factor_of


def split_up(number_of, total, bound, lean):
    loads = [(1 << 20) // math.isqrt(standing ** lean) + 1 for standing in range(2, number_of + 1)]
    rest, given = total - bound - (number_of - 1), [1] * (number_of - 1)
    while rest > 0:
        free = [i for i in range(number_of - 1) if given[i] < bound]
        whole, budget = sum([loads[i] for i in free]), rest
        for i in free:
            addition = min(bound - given[i], max(1, budget * loads[i] // whole), rest)
            given[i] = given[i] + addition
            rest = rest - addition
    return np.array([bound] + given)


def ragged_sizes(stream_key, number_of, total, reach, slope):
    if number_of == 2:
        one = jax.random.randint(stream_key, (), max(1, total - reach), min(reach, total - 1) + 1)
        return jnp.stack([one, total - one])
    lengths = jnp.asarray(split_up(number_of, total, reach, slope), jnp.int32)
    twos = (number_of - 1) // 2
    source_of, taker = lengths[1:1 + 2 * twos:2], lengths[2:2 + 2 * twos:2]
    margin = jnp.minimum(source_of - 1, reach - taker)
    passed = jax.random.randint(jax.random.fold_in(stream_key, 1), (twos,), 0, 1 << 20) % (margin + 1)
    lengths = lengths.at[1:1 + 2 * twos:2].set(source_of - passed).at[2:2 + 2 * twos:2].set(taker + passed)
    return lengths[jax.random.permutation(jax.random.fold_in(stream_key, 2), number_of)]


def gaussian(stream_key, dims, width, limit, split=(), held_as=jnp.bfloat16):
    array = width * jax.random.normal(stream_key, dims, jnp.float32)
    if split:
        array = array * level_of(stream_key, dims, split, -0.22, 0.18)
    return jnp.clip(array, -limit, limit).astype(held_as)


def setup_inputs(seed: int = 0) -> dict:
    key_of = jax.random.split(jax.random.key(seed), 15)
    return {
        "tokens": gaussian(key_of[0], (TOKENS, D), 1.0, 6.0, ((0, 16),)),
        "cotangent": gaussian(key_of[1], (TOKENS, D), 1.0, 6.0, ((0, 16),)),
        "segment": jnp.searchsorted(jnp.cumsum(ragged_sizes(key_of[2], DOCS, TOKENS, SEQ_LEN * 3 // 4, 2)), jnp.arange(TOKENS), side="right").astype(jnp.int32),
        "variate": touch_ends(jax.random.randint(key_of[3], (TOKENS,), 0, 4), jax.random.fold_in(key_of[3], 1), 0, 3).astype(jnp.int32),
        "time": touch_ends(jax.random.randint(key_of[4], (TOKENS,), 0, 4096), jax.random.fold_in(key_of[4], 1), 0, 4095).astype(jnp.int32),
        "w_qkv": gaussian(key_of[5], (3, D, D), D ** -0.5, 0.1875, ((2, 2),)),
        "w_out": gaussian(key_of[6], (D, D), (D // 128) ** -0.5, 2.0, ((0, 2),)),
        "w_gateup": gaussian(key_of[7], (2, D, FF), D ** -0.5, 0.1875, ((2, 2),)),
        "w_down": gaussian(key_of[8], (FF, D), FF ** -0.5, 0.109375, ((0, 2),)),
        "attn_gain": jnp.clip(1.0 + 0.1 * jax.random.normal(key_of[9], (D,), jnp.float32), 0.5, 1.5),
        "mlp_gain": jnp.clip(1.0 + 0.1 * jax.random.normal(key_of[10], (D,), jnp.float32), 0.5, 1.5),
        "query_gain": jnp.clip(1.0 + 0.1 * jax.random.normal(key_of[11], (HD,), jnp.float32), 0.5, 1.5),
        "key_gain": jnp.clip(1.0 + 0.1 * jax.random.normal(key_of[12], (HD,), jnp.float32), 0.5, 1.5),
        "var_bias": gaussian(key_of[13], (2, HEADS), 1.0, 4.0, ((1, 2),), jnp.float32),
    }


EPSILON = 1e-05
MASKED = -1e+30
HIGHEST = lax.Precision.HIGHEST

@jax.custom_vjp
def low(v):
    return lax.optimization_barrier(v.astype(jnp.bfloat16)).astype(jnp.float32)

@jax.custom_vjp
def low_back(v):
    return v

def low_keep(v):
    return (low(v), None)

def low_pass(kept, grad):
    return (grad,)

def back_keep(v):
    return (v, None)

def back_low(kept, grad):
    return (low(grad),)
low.defvjp(low_keep, low_pass)
low_back.defvjp(back_keep, back_low)

def rotary(values, times):
    half_dim = values.shape[-1] // 2
    inverse = 10000.0 ** (-2.0 * jnp.arange(half_dim, dtype=jnp.float32) / values.shape[-1])
    angles = times.astype(jnp.float32)[:, None] * inverse[None, :]
    cosine = jnp.cos(angles)[:, None, :]
    sine_table = jnp.sin(angles)[:, None, :]
    first_half = values[..., :half_dim]
    second_half = values[..., half_dim:]
    return jnp.concatenate([first_half * cosine - second_half * sine_table, second_half * cosine + first_half * sine_table], axis=-1)

def head_norm(values, gain):
    scale_row = lax.rsqrt(lax.optimization_barrier(jnp.mean(values * values, axis=-1, keepdims=True)) + EPSILON)
    return values * scale_row * gain

def layer_sequence(inputs, seg_ids, var_ids, time_ids, qkv_weight, out_weight, gateup_weight, down_weight, gain_attn, gain_mlp, gain_query, gain_key, bias_table):
    length = inputs.shape[0]
    scale_one = lax.rsqrt(lax.optimization_barrier(jnp.mean(inputs * inputs, axis=1, keepdims=True)) + EPSILON)
    normed_one = low(inputs * scale_one * gain_attn)
    projected = low_back(jnp.einsum('td,kde->kte', normed_one, qkv_weight, precision=HIGHEST))
    projected = projected.reshape(3, length, HEADS, HD)
    queries = low(rotary(head_norm(projected[0], gain_query), time_ids))
    keys_all = low(rotary(head_norm(projected[1], gain_key), time_ids))
    values_all = low(projected[2])
    block_rows = min(512, length)

    def attend(row_start):
        query_block = lax.dynamic_slice_in_dim(queries, row_start, block_rows, 0)
        seg_block = lax.dynamic_slice_in_dim(seg_ids, row_start, block_rows, 0)
        var_block = lax.dynamic_slice_in_dim(var_ids, row_start, block_rows, 0)
        raw_scores = jnp.einsum('thd,uhd->htu', query_block, keys_all, precision=HIGHEST) * HD ** (-0.5)
        same_var = (var_block[:, None] == var_ids[None, :])[None]
        biased = raw_scores + jnp.where(same_var, bias_table[0][:, None, None], bias_table[1][:, None, None])
        allowed = (seg_block[:, None] == seg_ids[None, :])[None]
        scores = low_back(jnp.where(allowed, biased, MASKED))
        row_peak = lax.optimization_barrier(jnp.max(scores, axis=2, keepdims=True))
        exponent = jnp.exp(scores - row_peak)
        probs = exponent / lax.optimization_barrier(jnp.sum(exponent, axis=2, keepdims=True))
        mixed = jnp.einsum('htu,uhd->thd', low(probs), values_all, precision=HIGHEST)
        return low(low_back(mixed))
    starts = jnp.arange(0, length, block_rows).astype(jnp.int32)
    heads_out = lax.map(jax.checkpoint(attend), starts).reshape(length, HEADS * HD)
    attn_out = low_back(jnp.dot(heads_out, out_weight, precision=HIGHEST, preferred_element_type=jnp.float32))
    middle = inputs + attn_out
    scale_two = lax.rsqrt(lax.optimization_barrier(jnp.mean(middle * middle, axis=1, keepdims=True)) + EPSILON)
    normed_two = low(middle * scale_two * gain_mlp)
    gate_up = low_back(jnp.einsum('td,kdf->ktf', normed_two, gateup_weight, precision=HIGHEST))
    hidden = low(jax.nn.silu(gate_up[0]) * gate_up[1])
    return middle + jnp.dot(hidden, down_weight, precision=HIGHEST, preferred_element_type=jnp.float32)

def reference(tokens, cotangent, segment, variate, time, w_qkv, w_out, w_gateup, w_down, attn_gain, mlp_gain, query_gain, key_gain, var_bias):
    sequences = TOKENS // SEQ_LEN
    seg_rows = segment.reshape(sequences, SEQ_LEN)
    var_rows = variate.reshape(sequences, SEQ_LEN)
    time_rows = time.reshape(sequences, SEQ_LEN)

    def forward(inputs, qkv_weight, out_weight, gateup_weight, down_weight, gain_attn, gain_mlp, gain_query, gain_key, bias_table):

        def one_sequence(carried, pieces):
            rows_seq, seg_part, var_part, time_part = pieces
            result = jax.checkpoint(layer_sequence)(rows_seq, seg_part, var_part, time_part, qkv_weight, out_weight, gateup_weight, down_weight, gain_attn, gain_mlp, gain_query, gain_key, bias_table)
            return (carried, result)
        unused, outputs = lax.scan(one_sequence, jnp.zeros((), jnp.float32), (inputs.reshape(sequences, SEQ_LEN, D), seg_rows, var_rows, time_rows))
        return outputs.reshape(TOKENS, D)
    primals = (tokens.astype(jnp.float32), w_qkv.astype(jnp.float32), w_out.astype(jnp.float32), w_gateup.astype(jnp.float32), w_down.astype(jnp.float32), attn_gain, mlp_gain, query_gain, key_gain, var_bias)
    result, pullback = jax.vjp(forward, *primals)
    grads = pullback(cotangent.astype(jnp.float32))
    return (result.astype(jnp.bfloat16), grads[0], grads[1], grads[2], grads[3], grads[4], grads[5], grads[6], grads[7], grads[8], grads[9])
```

```python
import functools

import jax
import jax.numpy as jnp
from jax import lax
from jax.experimental import pallas as pl
from jax.experimental.pallas import tpu as pltpu
from jax.sharding import PartitionSpec as P

HD = 64
LANES = 128
EPSILON = 1e-05
LOG2E = 1.4426950408889634
FAR = -30000.0
DOCS = 8
VARS = 4
VAR_AT = HD
SEG_AT = VAR_AT + 3 * VARS
ONE_AT = SEG_AT + DOCS
VMEM = 60 * 1024 * 1024


def heads_view(rows):
    return rows.reshape(rows.shape[0], -1, HD)


def rotary_table(times):
    half_dim = HD // 2
    inverse = 10000.0 ** (-2.0 * jnp.arange(half_dim, dtype=jnp.float32) / HD)
    angles = times.astype(jnp.float32)[:, None] * inverse[None, :]
    return (jnp.cos(angles)[:, None, :], jnp.sin(angles)[:, None, :])


def rotate(values, cosine, sine_table):
    half_dim = values.shape[-1] // 2
    first_half = values[..., :half_dim]
    second_half = values[..., half_dim:]
    return jnp.concatenate(
        [
            first_half * cosine - second_half * sine_table,
            second_half * cosine + first_half * sine_table,
        ],
        axis=-1,
    )


def rotate_back(grads_in, cosine, sine_table):
    return rotate(grads_in, cosine, -sine_table)


def split_three(x):
    high = lax.reduce_precision(x, 8, 7)
    rest = x - high
    mid = lax.reduce_precision(rest, 8, 7)
    return [part.astype(jnp.bfloat16) for part in (high, mid, rest - mid)]


def forward_kernel(lo_ref, hi_ref, q_ref, k_ref, v_ref, o_ref, acc_ref, *, rows, ranks, heads):
    block = pl.program_id(0)
    acc_ref[...] = jnp.zeros_like(acc_ref)
    query = q_ref[...]

    def step(index, carry):
        place = lax.rem(index, ranks) * heads + index // ranks
        span = pl.ds(pl.multiple_of(place * rows, rows), rows)
        scores = lax.dot_general(
            query, k_ref[span, :], (((1,), (1,)), ((), ())), preferred_element_type=jnp.float32
        )
        probs = jnp.exp2(scores).astype(jnp.bfloat16)
        acc_ref[...] += jnp.dot(probs, v_ref[span, :], preferred_element_type=jnp.float32)
        return carry

    lax.fori_loop(lo_ref[block], hi_ref[block], step, 0)
    total = acc_ref[...]
    row_sum = total[:, HD : HD + 1]
    lane = lax.broadcasted_iota(jnp.int32, total.shape, 1)
    o_ref[...] = jnp.where(lane < HD, total / row_sum, jnp.log2(row_sum))


def forward_attention(lo, hi, query, key, value, rows, ranks, heads):
    blocks = query.shape[0] // rows
    whole = pl.BlockSpec(memory_space=pltpu.VMEM)
    return pl.pallas_call(
        functools.partial(forward_kernel, rows=rows, ranks=ranks, heads=heads),
        out_shape=jax.ShapeDtypeStruct(query.shape, jnp.float32),
        grid_spec=pltpu.PrefetchScalarGridSpec(
            num_scalar_prefetch=2,
            grid=(blocks,),
            in_specs=[pl.BlockSpec((rows, LANES), lambda i, *_: (i, 0)), whole, whole],
            out_specs=pl.BlockSpec((rows, LANES), lambda i, *_: (i, 0)),
            scratch_shapes=[pltpu.VMEM((rows, LANES), jnp.float32)],
        ),
        compiler_params=pltpu.CompilerParams(vmem_limit_bytes=VMEM),
    )(lo, hi, query, key, value)


def backward_kernel(
    lo_ref, hi_ref, k_ref, v_ref, q_ref, g_ref, dk_ref, dv_ref, dq_ref, *, rows
):
    @pl.when(pl.program_id(0) == 0)
    def start():
        dq_ref[...] = jnp.zeros_like(dq_ref)

    dk_ref[...] = jnp.zeros_like(dk_ref)
    dv_ref[...] = jnp.zeros_like(dv_ref)
    key = k_ref[...]
    value = v_ref[...]

    def step(index, carry):
        span = pl.ds(pl.multiple_of(index * rows, rows), rows)
        query = q_ref[span, :]
        grad = g_ref[span, :]
        scores = lax.dot_general(
            key, query, (((1,), (1,)), ((), ())), preferred_element_type=jnp.float32
        )
        grad_probs = lax.dot_general(
            value, grad, (((1,), (1,)), ((), ())), preferred_element_type=jnp.float32
        )
        probs = jnp.exp2(scores)
        grad_scores = (probs * grad_probs).astype(jnp.bfloat16)
        dv_ref[...] += jnp.dot(
            probs.astype(jnp.bfloat16), grad, preferred_element_type=jnp.float32
        )
        dk_ref[...] += jnp.dot(grad_scores, query, preferred_element_type=jnp.float32)
        dq_ref[span, :] += lax.dot_general(
            grad_scores, key, (((0,), (0,)), ((), ())), preferred_element_type=jnp.float32
        )
        return carry

    block = pl.program_id(0)
    lax.fori_loop(lo_ref[block], hi_ref[block], step, 0)


def backward_attention(lo, hi, key, value, query, grad, rows, ranks, heads):
    blocks = key.shape[0] // rows
    whole = pl.BlockSpec(memory_space=pltpu.VMEM)

    part = pl.BlockSpec((rows, LANES), lambda i, *_: (i, 0))
    return pl.pallas_call(
        functools.partial(backward_kernel, rows=rows),
        out_shape=(
            jax.ShapeDtypeStruct(key.shape, jnp.float32),
            jax.ShapeDtypeStruct(key.shape, jnp.float32),
            jax.ShapeDtypeStruct(query.shape, jnp.float32),
        ),
        grid_spec=pltpu.PrefetchScalarGridSpec(
            num_scalar_prefetch=2,
            grid=(blocks,),
            in_specs=[part, part, whole, whole],
            out_specs=(part, part, whole),
            scratch_shapes=[],
        ),
        compiler_params=pltpu.CompilerParams(vmem_limit_bytes=VMEM),
    )(lo, hi, key, value, query, grad)


def shards(
    tokens,
    cotangent,
    segment,
    variate,
    time,
    w_qkv,
    w_out,
    w_gateup,
    w_down,
    attn_gain,
    mlp_gain,
    query_gain,
    key_gain,
    var_bias,
):
    low = jnp.bfloat16
    wide = jnp.float32
    rows = tokens.shape[0]
    local_width = w_qkv.shape[2]
    heads = local_width // HD
    dp = lax.axis_size("dp")
    tensor = lax.axis_size("tensor")
    ranks = dp // heads
    head_groups = [[h * ranks + j for h in range(heads)] for j in range(ranks)]
    rank_groups = [[h * ranks + j for j in range(ranks)] for h in range(heads)]
    place = lax.axis_index("dp")
    head_here = place // ranks
    rank_here = lax.rem(place, ranks)
    width_share = tokens.shape[1] // tensor
    tensor_start = lax.axis_index("tensor") * width_share

    def to_heads(x):
        return lax.all_to_all(x, "dp", 0, 0, axis_index_groups=head_groups, tiled=True)

    def tensor_sum(x):
        if tensor == 2:
            return x + lax.ppermute(x.astype(low), "tensor", [(0, 1), (1, 0)]).astype(wide)
        return lax.psum(x.astype(low), "tensor").astype(wide)

    def tensor_share(x):
        mine = lax.dynamic_slice_in_dim(x, tensor_start, width_share, 1)
        if tensor == 2:
            other = lax.dynamic_slice_in_dim(x, width_share - tensor_start, width_share, 1)
            return mine + lax.ppermute(other.astype(low), "tensor", [(0, 1), (1, 0)]).astype(wide)
        return lax.psum_scatter(x, "tensor", scatter_dimension=1, tiled=True)

    inputs = tokens.astype(wide)
    scale_one = lax.rsqrt(jnp.mean(inputs * inputs, axis=1, keepdims=True) + EPSILON)
    unit_one = inputs * scale_one
    normed_one = (unit_one * attn_gain).astype(low)
    projected = jnp.einsum("td,kde->kte", normed_one, w_qkv, preferred_element_type=wide)
    cosine, sine_table = rotary_table(time)
    raw_query = heads_view(projected[0])
    raw_key = heads_view(projected[1])
    query_scale = lax.rsqrt(jnp.mean(raw_query * raw_query, axis=-1, keepdims=True) + EPSILON)
    key_scale = lax.rsqrt(jnp.mean(raw_key * raw_key, axis=-1, keepdims=True) + EPSILON)
    unit_query = raw_query * query_scale
    unit_key = raw_key * key_scale
    query_rows = rotate(unit_query * (query_gain * (LOG2E * HD**-0.5)), cosine, sine_table)
    key_rows = rotate(unit_key * key_gain, cosine, sine_table)
    packed = jnp.concatenate(
        [query_rows.astype(low), key_rows.astype(low), heads_view(projected[2]).astype(low)], axis=-1
    ).transpose(1, 0, 2)
    all_ids = lax.all_gather(jnp.stack([segment, variate]), "dp", axis=0, tiled=False)
    landed = to_heads(packed)
    gathered = lax.all_gather(
        landed[:, :, HD:], "dp", axis=0, axis_index_groups=rank_groups, tiled=False
    )

    ids = all_ids.reshape(heads, ranks, 2, rows).transpose(1, 0, 2, 3)
    segs = ids[:, :, 0]
    variates = ids[:, :, 1]
    own_segs = lax.dynamic_index_in_dim(segs, rank_here, 0, False)
    own_vars = lax.dynamic_index_in_dim(variates, rank_here, 0, False)
    all_rows = dp * rows
    own_rows = heads * rows

    def hot(values, count):
        return values.reshape(-1, 1) == jnp.arange(count, dtype=jnp.int32)[None, :]

    bias_here = lax.dynamic_index_in_dim(var_bias, head_here, 1, False)
    bias_step = split_three(jnp.broadcast_to((bias_here[0] - bias_here[1]) * LOG2E, (1, 1)))
    own_hot = hot(own_vars, VARS)
    query_head = landed[:, :, :HD].reshape(own_rows, HD)
    query_features = [jnp.where(own_hot, part, 0).astype(low) for part in bias_step] + [
        hot(own_segs, DOCS).astype(low)
    ]
    fill = jnp.zeros((own_rows, LANES - ONE_AT), low)
    query_op = jnp.concatenate([query_head] + query_features + [fill], axis=1)
    key_hot = hot(variates, VARS).astype(low)
    key_op = jnp.concatenate(
        [
            gathered[..., :HD].reshape(all_rows, HD),
            key_hot,
            key_hot,
            key_hot,
            jnp.where(hot(segs, DOCS), 0.0, FAR).astype(low),
            jnp.ones((all_rows, 3), low),
            jnp.zeros((all_rows, LANES - ONE_AT - 3), low),
        ],
        axis=1,
    )
    value_op = jnp.concatenate(
        [
            gathered[..., HD:].reshape(all_rows, HD),
            jnp.ones((all_rows, 3), low),
            jnp.zeros((all_rows, LANES - HD - 3), low),
        ],
        axis=1,
    )
    block_first = all_ids[:, 0, 0]
    block_last = all_ids[:, 0, -1]
    own_first = own_segs[:, 0]
    own_last = own_segs[:, -1]
    count = lambda hits, axis: jnp.sum(hits.astype(jnp.int32), axis=axis)
    key_lo = count(block_last[None, :] < own_first[:, None], 1)
    key_hi = count(block_first[None, :] <= own_last[:, None], 1)
    place_first = segs[:, :, 0].reshape(-1)
    place_last = segs[:, :, -1].reshape(-1)
    query_lo = count(own_last[None, :] < place_first[:, None], 1)
    query_hi = count(own_first[None, :] <= place_last[:, None], 1)

    mixed = forward_attention(key_lo, key_hi, query_op, key_op, value_op, rows, ranks, heads)
    exact_out = mixed[:, :HD]
    log_total = mixed[:, HD : HD + 1]

    def to_tokens(x):
        return lax.all_to_all(x, "dp", 0, 0, axis_index_groups=head_groups, tiled=True)

    heads_out = (
        to_tokens(exact_out.astype(low).reshape(heads, rows, HD))
        .transpose(1, 0, 2)
        .reshape(rows, local_width)
    )
    attn_total = tensor_sum(jnp.dot(heads_out, w_out, preferred_element_type=wide))
    middle = inputs + attn_total
    scale_two = lax.rsqrt(jnp.mean(middle * middle, axis=1, keepdims=True) + EPSILON)
    unit_two = middle * scale_two
    normed_two = (unit_two * mlp_gain).astype(low)
    gate_up = jnp.einsum("td,kdf->ktf", normed_two, w_gateup, preferred_element_type=wide)
    gate_vals = gate_up[0]
    up_vals = gate_up[1]
    sig_gate = jax.nn.sigmoid(gate_vals)
    act_gate = gate_vals * sig_gate
    hidden = (act_gate * up_vals).astype(low)
    mlp_part = jnp.dot(hidden, w_down, preferred_element_type=wide)
    mlp_share = tensor_share(mlp_part)
    output = (lax.dynamic_slice_in_dim(middle, tensor_start, width_share, 1) + mlp_share).astype(low)
    grad_hidden = jnp.einsum("te,fe->tf", cotangent, w_down, preferred_element_type=wide)
    grad_down = jnp.einsum("tf,te->fe", hidden, cotangent, preferred_element_type=wide)
    grad_gate = grad_hidden * up_vals * sig_gate * (1.0 + gate_vals * (1.0 - sig_gate))
    grad_up = grad_hidden * act_gate
    grad_gu = jnp.stack([grad_gate, grad_up]).astype(low)
    grad_gateup = jnp.einsum("td,ktf->kdf", normed_two, grad_gu, preferred_element_type=wide)
    grad_normed_two = jnp.einsum("ktf,kdf->td", grad_gu, w_gateup, preferred_element_type=wide)
    mlp_gain_part = jnp.sum(grad_normed_two * unit_two, axis=0)
    scaled_two = grad_normed_two * mlp_gain
    middle_part = scale_two * (
        scaled_two - unit_two * jnp.mean(scaled_two * unit_two, axis=1, keepdims=True)
    )
    grad_middle = cotangent.astype(wide) + tensor_sum(middle_part)
    grad_middle_low = grad_middle.astype(low)
    grad_out = jnp.einsum("tc,td->cd", heads_out, grad_middle_low, preferred_element_type=wide)
    grad_heads = jnp.einsum(
        "td,cd->tc", grad_middle_low, w_out, preferred_element_type=wide
    ).astype(low)
    grad_landed = to_heads(heads_view(grad_heads).transpose(1, 0, 2)).reshape(own_rows, HD)
    row_delta = jnp.sum(grad_landed.astype(wide) * exact_out, axis=1, keepdims=True)
    grad_op = jnp.concatenate(
        [grad_landed] + split_three(-row_delta) + [jnp.zeros((own_rows, LANES - HD - 3), low)],
        axis=1,
    )
    query_back = jnp.concatenate(
        [query_op[:, :ONE_AT]]
        + split_three(-log_total)
        + [jnp.zeros((own_rows, LANES - ONE_AT - 3), low)],
        axis=1,
    )
    key_full, value_full, query_full = backward_attention(
        query_lo, query_hi, key_op, value_op, query_back, grad_op, rows, ranks, heads
    )
    by_variate = query_full[:, VAR_AT : VAR_AT + VARS]
    same_sum = jnp.sum(jnp.where(own_hot, by_variate, 0.0))
    other_sum = jnp.sum(jnp.where(own_hot, 0.0, by_variate))
    bias_part = jnp.stack([same_sum, other_sum])[:, None] * (
        jnp.arange(heads, dtype=jnp.int32)[None, :] == head_here
    ).astype(wide)

    key_value = jnp.concatenate([key_full[:, :HD], value_full[:, :HD]], axis=1).astype(low)
    key_value = lax.psum_scatter(
        key_value.reshape(ranks, heads, rows, 2 * HD),
        "dp",
        scatter_dimension=0,
        axis_index_groups=rank_groups,
        tiled=False,
    )
    back_packed = jnp.concatenate(
        [query_full[:, :HD].astype(low).reshape(heads, rows, HD), key_value], axis=-1
    )
    back_landed = to_tokens(back_packed).transpose(1, 0, 2).astype(wide)
    back_query = rotate_back(back_landed[..., :HD] * HD ** (-0.5), cosine, sine_table)
    back_key = rotate_back(back_landed[..., HD : 2 * HD] * (1.0 / LOG2E), cosine, sine_table)
    grad_value = back_landed[..., 2 * HD :].reshape(rows, local_width)
    query_gain_part = jnp.sum(back_query * unit_query, axis=(0, 1))
    key_gain_part = jnp.sum(back_key * unit_key, axis=(0, 1))
    scaled_query = back_query * query_gain
    scaled_key = back_key * key_gain
    grad_raw_query = query_scale * (
        scaled_query - unit_query * jnp.mean(scaled_query * unit_query, axis=-1, keepdims=True)
    )
    grad_raw_key = key_scale * (
        scaled_key - unit_key * jnp.mean(scaled_key * unit_key, axis=-1, keepdims=True)
    )
    grad_projected = jnp.stack(
        [
            grad_raw_query.reshape(rows, local_width),
            grad_raw_key.reshape(rows, local_width),
            grad_value,
        ]
    ).astype(low)
    grad_qkv = jnp.einsum("td,kte->kde", normed_one, grad_projected, preferred_element_type=wide)
    grad_normed_one = jnp.einsum("kte,kde->td", grad_projected, w_qkv, preferred_element_type=wide)
    attn_gain_part = jnp.sum(grad_normed_one * unit_one, axis=0)
    scaled_one = grad_normed_one * attn_gain
    input_part = scale_one * (
        scaled_one - unit_one * jnp.mean(scaled_one * unit_one, axis=1, keepdims=True)
    )
    grad_input = lax.dynamic_slice_in_dim(grad_middle, tensor_start, width_share, 1) + tensor_share(
        input_part
    )
    gain_sums = lax.psum(
        (attn_gain_part, mlp_gain_part, query_gain_part, key_gain_part), ("dp", "tensor")
    )
    bias_sum = lax.psum(bias_part, "dp")
    early = lax.psum((grad_out.astype(low), grad_gateup.astype(low), grad_down.astype(low)), "dp")
    late = lax.psum(grad_qkv.astype(low), "dp")
    return (
        output,
        grad_input,
        late.astype(wide),
        early[0].astype(wide),
        early[1].astype(wide),
        early[2].astype(wide),
        gain_sums[0],
        gain_sums[1],
        gain_sums[2],
        gain_sums[3],
        bias_sum,
    )


def solution(mesh):
    placed = (
        P("dp", None),
        P("dp", None),
        P("dp"),
        P("dp"),
        P("dp"),
        P(None, None, "tensor"),
        P("tensor", None),
        P(None, None, "tensor"),
        P("tensor", None),
        P(),
        P(),
        P(),
        P(),
        P(None, "tensor"),
    )
    return jax.shard_map(
        shards,
        mesh=mesh,
        in_specs=placed,
        out_specs=(
            P("dp", "tensor"),
            P("dp", "tensor"),
            P(None, None, "tensor"),
            P("tensor", None),
            P(None, None, "tensor"),
            P("tensor", None),
            P(),
            P(),
            P(),
            P(),
            P(None, "tensor"),
        ),
        check_vma=False,
    )
```

```python
import functools

import jax
import jax.numpy as jnp
from jax import lax
from jax.experimental import pallas as pl
from jax.experimental.pallas import tpu as pltpu
from jax.sharding import PartitionSpec as P

HD = 64
LANES = 128
IDS = 16
EPSILON = 1e-05
LOG2E = 1.4426950408889634
FAR = -30000.0
DOCS = 8
VARS = 4
VAR_AT = HD
SEG_AT = VAR_AT + 3 * VARS
ONE_AT = SEG_AT + DOCS
VMEM = 60 * 1024 * 1024
MESH = pl.DeviceIdType.MESH
WHOLE = pl.BlockSpec(memory_space=pltpu.VMEM)
SCALARS = pl.BlockSpec(memory_space=pltpu.SMEM)
ANYWHERE = pl.BlockSpec(memory_space=pl.ANY)
wide = jnp.float32
low = jnp.bfloat16


def params(**more):
    return pltpu.CompilerParams(vmem_limit_bytes=VMEM, **more)


def lanes_of(x):
    return lax.broadcasted_iota(jnp.int32, x.shape, x.ndim - 1)


def dot_nt(a, b):
    return lax.dot_general(a, b, (((1,), (1,)), ((), ())), preferred_element_type=wide)


def dot_tn(a, b):
    return lax.dot_general(a, b, (((0,), (0,)), ((), ())), preferred_element_type=wide)


def dot_nn(a, b):
    return jnp.dot(a, b, preferred_element_type=wide)


def left_pair(a, b):
    return jnp.where(lanes_of(a) < HD, a, pltpu.roll(b, HD, 1))


def right_pair(a, b):
    return jnp.where(lanes_of(a) < HD, pltpu.roll(a, HD, 1), b)


def swap_halves(x):
    return jnp.where(
        lanes_of(x) % HD < HD // 2,
        pltpu.roll(x, LANES - HD // 2, 1),
        pltpu.roll(x, HD // 2, 1),
    )


def head_mean(x):
    row = lax.broadcasted_iota(jnp.int32, (LANES, LANES), 0) // HD
    column = lax.broadcasted_iota(jnp.int32, (LANES, LANES), 1) // HD
    mix = jnp.where(row == column, 1.0 / HD, 0.0)
    return jnp.dot(x, mix, precision=lax.Precision.HIGHEST, preferred_element_type=wide)


def features(segs, variates, table):
    index = lax.broadcasted_iota(jnp.int32, (IDS, LANES), 0)
    segs = jnp.broadcast_to(segs, (IDS, LANES)).astype(jnp.int32)
    variates = jnp.broadcast_to(variates, (IDS, LANES)).astype(jnp.int32)
    by_variate = jnp.where(variates == index, 1.0, 0.0)
    by_document = jnp.where(segs == index - VARS, 1.0, 0.0)
    ones = jnp.where(index < VARS, by_variate, jnp.where(index < VARS + DOCS, by_document, 1.0))
    return dot_tn(ones.astype(low), table)


def key_table():
    row = jnp.arange(IDS)[:, None]
    lane = jnp.arange(LANES)[None, :]
    hot = (row < VARS) & (lane >= VAR_AT) & (lane < SEG_AT) & ((lane - VAR_AT) % VARS == row)
    far = (row >= VARS) & (row < VARS + DOCS) & (lane >= SEG_AT) & (lane < ONE_AT)
    far = far & (lane - SEG_AT != row - VARS)
    one = (row == VARS + DOCS) & (lane >= ONE_AT) & (lane < ONE_AT + 3)
    return jnp.where(hot | one, 1.0, jnp.where(far, FAR, 0.0)).astype(low)


def query_table(step):
    row = jnp.arange(IDS)[:, None]
    lane = jnp.arange(LANES)[None, :]
    high = lax.reduce_precision(step, 8, 7)
    mid = lax.reduce_precision(step - high, 8, 7)
    part = (lane - VAR_AT) // VARS
    step = jnp.where(part == 0, high, jnp.where(part == 1, mid, step - high - mid))
    hot = (row < VARS) & (lane >= VAR_AT) & (lane < SEG_AT) & ((lane - VAR_AT) % VARS == row)
    seg = (row >= VARS) & (row < VARS + DOCS) & (lane - SEG_AT == row - VARS)
    return jnp.where(hot, step, jnp.where(seg, 1.0, 0.0)).astype(low)


def project_kernel(
    tokens_ref, w_ref, gain_ref, query_gain_ref, key_gain_ref, cosine_ref, sine_ref, ids_ref,
    message_ref, query_ref, key_ref, normed_ref,
):
    rows = tokens_ref.shape[0]

    @pl.when(pl.program_id(0) == 0)
    def norm():
        x = tokens_ref[...].astype(wide)
        scale = lax.rsqrt(jnp.mean(x * x, axis=1, keepdims=True) + EPSILON)
        normed_ref[...] = (x * scale * gain_ref[...]).astype(low)

    normed = normed_ref[...]

    def turned(raw, gain):
        x = raw * lax.rsqrt(head_mean(raw * raw) + EPSILON) * gain
        return x * cosine_ref[...] + swap_halves(x) * sine_ref[...]

    raw_query = dot_nn(normed, w_ref[0])
    raw_key = dot_nn(normed, w_ref[1])
    value = dot_nn(normed, w_ref[2])
    query_ref[...] = raw_query
    key_ref[...] = raw_key
    query = turned(raw_query, query_gain_ref[...])
    key = turned(raw_key, key_gain_ref[...])
    message_ref[0, :rows] = left_pair(key, value).astype(low)
    message_ref[1, :rows] = right_pair(key, value).astype(low)
    upper, lower = query[: rows // 2], query[rows // 2 :]
    message_ref[0, rows + IDS :] = left_pair(upper, lower).astype(low)
    message_ref[1, rows + IDS :] = right_pair(upper, lower).astype(low)
    message_ref[0, rows : rows + IDS] = ids_ref[...]
    message_ref[1, rows : rows + IDS] = ids_ref[...]


def project(tokens, w_qkv, gain, query_gain, key_gain, cosine, sine, ids):
    rows, depth = tokens.shape
    width = w_qkv.shape[2]
    size = rows + IDS + rows // 2
    column = pl.BlockSpec((rows, LANES), lambda i: (0, i))
    return pl.pallas_call(
        project_kernel,
        grid=(width // LANES,),
        in_specs=[
            WHOLE,
            pl.BlockSpec((3, depth, LANES), lambda i: (0, 0, i)),
            WHOLE, WHOLE, WHOLE, WHOLE, WHOLE, WHOLE,
        ],
        out_specs=(
            pl.BlockSpec((2, size, LANES), lambda i: (i, 0, 0)),
            column, column,
            pl.BlockSpec((rows, depth), lambda i: (0, 0)),
        ),
        out_shape=(
            jax.ShapeDtypeStruct((width // HD, size, LANES), low),
            jax.ShapeDtypeStruct((rows, width), wide),
            jax.ShapeDtypeStruct((rows, width), wide),
            jax.ShapeDtypeStruct((rows, depth), low),
        ),
        compiler_params=params(),
    )(tokens, w_qkv, gain, query_gain, key_gain, cosine, sine, ids)


def walk(begin, end, body, largest):
    count = (end - begin) // LANES
    many = largest // LANES

    def step(index, carry):
        body(begin + index * largest, largest)
        return carry

    lax.fori_loop(0, count // many, step, 0)
    size = many // 2
    while size:
        piece = size * LANES
        at = begin + (count // (2 * size)) * (2 * piece)

        @pl.when((count // size) % 2 == 1)
        def rest(at=at, piece=piece):
            body(at, piece)

        size //= 2


def scalar(x):
    return x[0, 0].astype(jnp.int32)


def run_of(segs, first, last):
    below = jnp.sum(jnp.where(segs < first, 1.0, 0.0), keepdims=True)
    upto = jnp.sum(jnp.where(segs <= last, 1.0, 0.0), keepdims=True)
    return scalar(below) // LANES * LANES, (scalar(upto) + LANES - 1) // LANES * LANES


def forward_kernel(
    rank_ref, kv_ref, query_in_ref, key_table_ref, query_table_ref,
    k_ref, v_ref, q_ref, exact_ref, message_ref, runs_ref, acc_ref, seg_ref,
):
    ranks, heads = kv_ref.shape[:2]
    rows = q_ref.shape[0]
    half = rows // 2
    parts = rows // LANES
    block = pl.program_id(0)
    rank = rank_ref[0]
    filled = lax.broadcasted_iota(jnp.int32, (IDS // 2, LANES), 0) < parts

    @pl.when(block == 0)
    def prepare():
        for rank_at in range(ranks):
            for head_at in range(heads):
                at = head_at * ranks + rank_at
                ids = kv_ref[rank_at, head_at, rows:, :].astype(wide)
                seg_ref[at] = jnp.where(filled, ids[: IDS // 2], DOCS + 1.0)
                for part in range(parts):
                    extra = features(
                        ids[part : part + 1],
                        ids[IDS // 2 + part : IDS // 2 + part + 1],
                        key_table_ref[...],
                    )
                    kv = kv_ref[rank_at, head_at, part * LANES : (part + 1) * LANES].astype(wide)
                    lane = lanes_of(kv)
                    span = pl.ds(at * rows + part * LANES, LANES)
                    k_ref[span, :] = jnp.where(lane < HD, kv, extra).astype(low)
                    one = jnp.where(lane < HD + 3, 1.0, 0.0)
                    v_ref[span, :] = jnp.where(lane < HD, pltpu.roll(kv, HD, 1), one).astype(low)
        own = jnp.stack([seg_ref[head_at * ranks + rank] for head_at in range(heads)])
        own = own.reshape(heads * (IDS // 2), LANES)
        for at in range(ranks * heads):
            segs = seg_ref[at]
            first = jnp.min(segs, keepdims=True)
            last = jnp.max(jnp.where(filled, segs, 0.0), keepdims=True)
            runs_ref[0, at], runs_ref[1, at] = run_of(own, first, last)

    segs = seg_ref[block * ranks + rank]
    first = jnp.min(segs, keepdims=True)
    last = jnp.max(jnp.where(filled, segs, 0.0), keepdims=True)
    begin, end = run_of(seg_ref[...].reshape(ranks * heads * (IDS // 2), LANES), first, last)
    for part in range(parts):
        extra = features(
            kv_ref[rank, block, pl.ds(rows, IDS), :].astype(wide)[part : part + 1],
            kv_ref[rank, block, pl.ds(rows, IDS), :].astype(wide)[
                IDS // 2 + part : IDS // 2 + part + 1
            ],
            query_table_ref[...],
        )
        at = part * LANES
        if at < half:
            head = query_in_ref[0, at : at + LANES, :].astype(wide)
        else:
            head = pltpu.roll(query_in_ref[0, at - half : at - half + LANES, :].astype(wide), HD, 1)
        q_ref[at : at + LANES, :] = jnp.where(lanes_of(head) < HD, head, extra).astype(low)
    acc_ref[...] = jnp.zeros_like(acc_ref)

    def step(start, size):
        span = pl.ds(pl.multiple_of(start, LANES), size)
        probs = jnp.exp2(dot_nt(q_ref[...], k_ref[span, :])).astype(low)
        acc_ref[...] += dot_nn(probs, v_ref[span, :])

    walk(begin, end, step, 1024)
    total = acc_ref[...]
    row_sum = total[:, HD : HD + 1]
    exact = total / row_sum
    exact_ref[...] = jnp.where(lanes_of(total) < HD, exact, jnp.log2(row_sum))
    message_ref[0] = left_pair(exact[:half], exact[half:]).astype(low)


def forward_attention(rank, kv, query, key_table, query_table):
    ranks, heads, size = kv.shape[:3]
    rows = size - IDS
    every = ranks * heads * rows
    part = pl.BlockSpec((rows, LANES), lambda i, *_: (i, 0))
    fold = pl.BlockSpec((1, rows // 2, LANES), lambda i, *_: (i, 0, 0))
    return pl.pallas_call(
        forward_kernel,
        grid_spec=pltpu.PrefetchScalarGridSpec(
            num_scalar_prefetch=1,
            grid=(heads,),
            in_specs=[WHOLE, fold, WHOLE, WHOLE],
            out_specs=(WHOLE, WHOLE, part, part, fold, SCALARS),
            scratch_shapes=[
                pltpu.VMEM((rows, LANES), wide),
                pltpu.VMEM((ranks * heads, IDS // 2, LANES), wide),
            ],
        ),
        out_shape=(
            jax.ShapeDtypeStruct((every, LANES), low),
            jax.ShapeDtypeStruct((every, LANES), low),
            jax.ShapeDtypeStruct((heads * rows, LANES), low),
            jax.ShapeDtypeStruct((heads * rows, LANES), wide),
            jax.ShapeDtypeStruct((heads, rows // 2, LANES), low),
            jax.ShapeDtypeStruct((2, ranks * heads), jnp.int32),
        ),
        compiler_params=params(),
    )(rank, kv, query, key_table, query_table)


def split_lanes(column, lane, at):
    high = column.astype(low).astype(wide)
    mid = (column - high).astype(low).astype(wide)
    parts = jnp.where(lane == at, high, jnp.where(lane == at + 1, mid, column - high - mid))
    return jnp.where(lane < at + 3, parts, 0.0)


def backward_kernel(
    runs_ref, k_ref, v_ref, q_in_ref, exact_ref, grad_in_ref, ids_ref,
    kv_ref, message_ref, bias_ref, q_ref, g_ref, kt_ref, dk_ref, dv_ref, dq_ref,
):
    heads, half = grad_in_ref.shape[:2]
    rows = 2 * half
    block = pl.program_id(0)

    @pl.when(block == 0)
    def prepare():
        dq_ref[...] = jnp.zeros_like(dq_ref)
        for head_at in range(heads):
            folded = grad_in_ref[head_at].astype(wide)
            for side in range(2):
                span = pl.ds(head_at * rows + side * half, half)
                grad = folded if side == 0 else pltpu.roll(folded, HD, 1)
                lane = lanes_of(grad)
                grad = jnp.where(lane < HD, grad, 0.0)
                exact = exact_ref[span, :]
                delta = jnp.sum(grad * exact, axis=1, keepdims=True)
                g_ref[span, :] = jnp.where(lane < HD, grad, split_lanes(-delta, lane, HD)).astype(low)
                query = q_in_ref[span, :].astype(wide)
                total = split_lanes(-exact[:, HD : HD + 1], lane, ONE_AT)
                q_ref[span, :] = jnp.where(lane < ONE_AT, query, total).astype(low)

    dk_ref[...] = jnp.zeros_like(dk_ref)
    dv_ref[...] = jnp.zeros_like(dv_ref)
    key = k_ref[...]
    value = v_ref[...]
    kt_ref[...] = key.astype(wide).T.astype(low)

    def step(start, size):
        span = pl.ds(pl.multiple_of(start, LANES), size)
        query = q_ref[span, :]
        grad = g_ref[span, :]
        probs = jnp.exp2(dot_nt(key, query))
        grad_scores = (probs * dot_nt(value, grad)).astype(low)
        dv_ref[...] += dot_nn(probs.astype(low), grad)
        dk_ref[...] += dot_nn(grad_scores, query)
        dq_ref[:, span] += dot_nn(kt_ref[...], grad_scores)

    walk(runs_ref[0, block], runs_ref[1, block], step, 1024)
    kv_ref[0, 0] = left_pair(dk_ref[...] * (1.0 / LOG2E), dv_ref[...]).astype(low)

    @pl.when(block == pl.num_programs(0) - 1)
    def finish():
        same = jnp.zeros((8, LANES), wide)
        every = jnp.zeros((8, LANES), wide)
        index = lax.broadcasted_iota(jnp.int32, (8, LANES), 0)
        for head_at in range(heads):
            ids = ids_ref[head_at].astype(wide)
            for part in range(rows // LANES):
                at = head_at * rows + part * LANES
                by_variate = jnp.where(index < VARS, dq_ref[VAR_AT : VAR_AT + 8, at : at + LANES], 0.0)
                variates = jnp.broadcast_to(
                    ids[IDS // 2 + part : IDS // 2 + part + 1], (8, LANES)
                ).astype(jnp.int32)
                same = same + jnp.where(variates == index, by_variate, 0.0)
                every = every + by_variate
            span = dq_ref[:, head_at * rows : (head_at + 1) * rows].T * HD**-0.5
            message_ref[head_at] = left_pair(span[:half], span[half:]).astype(low)
        bias_ref[0] = same
        bias_ref[1] = every - same


def backward_attention(runs, key, value, query, exact, grad, ids):
    every = key.shape[0]
    heads, half = grad.shape[:2]
    rows = 2 * half
    ranks = every // (heads * rows)
    part = pl.BlockSpec((rows, LANES), lambda i, *_: (i, 0))
    return pl.pallas_call(
        backward_kernel,
        grid_spec=pltpu.PrefetchScalarGridSpec(
            num_scalar_prefetch=1,
            grid=(ranks * heads,),
            in_specs=[part, part, WHOLE, WHOLE, WHOLE, WHOLE],
            out_specs=(
                pl.BlockSpec((1, 1, rows, LANES), lambda i, *_: (i % ranks, i // ranks, 0, 0)),
                WHOLE,
                WHOLE,
            ),
            scratch_shapes=[
                pltpu.VMEM((heads * rows, LANES), low),
                pltpu.VMEM((heads * rows, LANES), low),
                pltpu.VMEM((LANES, rows), low),
                pltpu.VMEM((rows, LANES), wide),
                pltpu.VMEM((rows, LANES), wide),
                pltpu.VMEM((LANES, heads * rows), wide),
            ],
        ),
        out_shape=(
            jax.ShapeDtypeStruct((ranks, heads, rows, LANES), low),
            jax.ShapeDtypeStruct((heads, half, LANES), low),
            jax.ShapeDtypeStruct((2, 8, LANES), wide),
        ),
        compiler_params=params(),
    )(runs, key, value, query, exact, grad, ids)


def out_kernel(landed_ref, w_ref, heads_ref, part_ref, low_ref):
    half = landed_ref.shape[1]
    for pair in range(landed_ref.shape[0] // 2):
        one = landed_ref[2 * pair].astype(wide)
        two = landed_ref[2 * pair + 1].astype(wide)
        span = pl.ds(pair * LANES, LANES)
        heads_ref[:half, span] = left_pair(one, two).astype(low)
        heads_ref[half:, span] = right_pair(one, two).astype(low)
    part = dot_nn(heads_ref[...], w_ref[...])
    part_ref[...] = part
    low_ref[...] = part.astype(low)


def attention_out(landed, w_out):
    heads, half = landed.shape[:2]
    depth = w_out.shape[1]
    return pl.pallas_call(
        out_kernel,
        in_specs=[WHOLE, WHOLE],
        out_specs=(WHOLE, WHOLE, WHOLE),
        out_shape=(
            jax.ShapeDtypeStruct((2 * half, heads * HD), low),
            jax.ShapeDtypeStruct((2 * half, depth), wide),
            jax.ShapeDtypeStruct((2 * half, depth), low),
        ),
        compiler_params=params(),
    )(landed, w_out)


def grad_heads_kernel(grad_ref, w_ref, message_ref):
    half = message_ref.shape[1]
    for pair in range(message_ref.shape[0] // 2):
        both = dot_nt(grad_ref[...], w_ref[pair * LANES : (pair + 1) * LANES, :])
        message_ref[2 * pair] = left_pair(both[:half], both[half:]).astype(low)
        message_ref[2 * pair + 1] = right_pair(both[:half], both[half:]).astype(low)


def grad_heads_of(grad, w_out):
    return pl.pallas_call(
        grad_heads_kernel,
        in_specs=[WHOLE, WHOLE],
        out_specs=WHOLE,
        out_shape=jax.ShapeDtypeStruct((w_out.shape[0] // HD, grad.shape[0] // 2, LANES), low),
        compiler_params=params(),
    )(grad, w_out)


def unproject_kernel(
    landed_ref, query_ref, key_ref, query_gain_ref, key_gain_ref, cosine_ref, sine_ref,
    grad_ref, gains_ref,
):
    rows = query_ref.shape[0]
    half = rows // 2

    @pl.when(pl.program_id(0) == 0)
    def start():
        gains_ref[...] = jnp.zeros_like(gains_ref)

    def back(turned, raw_ref, gain_ref, at):
        grad = turned * cosine_ref[...] - swap_halves(turned) * sine_ref[...]
        raw = raw_ref[...]
        scale = lax.rsqrt(head_mean(raw * raw) + EPSILON)
        unit = raw * scale
        gains_ref[at : at + 1] += jnp.sum(grad * unit, axis=0, keepdims=True)
        scaled = grad * gain_ref[...]
        return scale * (scaled - unit * head_mean(scaled * unit))

    key_one = landed_ref[0, :rows].astype(wide)
    key_two = landed_ref[1, :rows].astype(wide)
    query_one = landed_ref[0, rows:].astype(wide)
    query_two = landed_ref[1, rows:].astype(wide)
    query = jnp.concatenate(
        [left_pair(query_one, query_two), right_pair(query_one, query_two)], axis=0
    )
    grad_ref[0] = back(query, query_ref, query_gain_ref, 0).astype(low)
    grad_ref[1] = back(left_pair(key_one, key_two), key_ref, key_gain_ref, 1).astype(low)
    grad_ref[2] = right_pair(key_one, key_two).astype(low)


def unproject(landed, raw_query, raw_key, query_gain, key_gain, cosine, sine):
    rows, width = raw_query.shape
    column = pl.BlockSpec((rows, LANES), lambda i: (0, i))
    return pl.pallas_call(
        unproject_kernel,
        grid=(width // LANES,),
        in_specs=[
            pl.BlockSpec((2, rows + rows // 2, LANES), lambda i: (i, 0, 0)),
            column, column, WHOLE, WHOLE, WHOLE, WHOLE,
        ],
        out_specs=(
            pl.BlockSpec((3, rows, LANES), lambda i: (0, 0, i)),
            pl.BlockSpec((8, LANES), lambda i: (0, 0)),
        ),
        out_shape=(
            jax.ShapeDtypeStruct((3, rows, width), low),
            jax.ShapeDtypeStruct((8, LANES), wide),
        ),
        compiler_params=params(),
    )(landed, raw_query, raw_key, query_gain, key_gain, cosine, sine)


def remote(src, dst, send, recv, place):
    return pltpu.make_async_remote_copy(
        src_ref=src, dst_ref=dst, send_sem=send, recv_sem=recv,
        device_id={"dp": place}, device_id_type=MESH,
    )


def greet(heads, ranks, head, rank, with_ranks):
    barrier = pltpu.get_barrier_semaphore()
    for step in range(1, heads):
        place = lax.rem(head + step, heads) * ranks + rank
        pl.semaphore_signal(barrier, inc=1, device_id={"dp": place}, device_id_type=MESH)
    if with_ranks:
        for step in range(1, ranks):
            place = head * ranks + lax.rem(rank + step, ranks)
            pl.semaphore_signal(barrier, inc=1, device_id={"dp": place}, device_id_type=MESH)
    pl.semaphore_wait(barrier, heads - 1 + (ranks - 1 if with_ranks else 0))


def spread_kernel(
    message_ref, kv_ref, query_ref, send_a, recv_a, send_b, recv_b, send_f, recv_f, local, *, ranks
):
    heads = message_ref.shape[0]
    size = kv_ref.shape[2]
    rest = query_ref.shape[1]
    place = lax.axis_index("dp")
    head = place // ranks
    rank = lax.rem(place, ranks)
    greet(heads, ranks, head, rank, True)
    firsts = []
    for step in range(1, heads):
        to = lax.rem(head + step, heads)
        at = to * ranks + rank
        first = remote(
            message_ref.at[to, pl.ds(0, size)], kv_ref.at[rank, head],
            send_a.at[step], recv_a.at[step], at,
        )
        second = remote(
            message_ref.at[to, pl.ds(size, rest)], query_ref.at[head],
            send_b.at[step], recv_b.at[step], at,
        )
        first.start()
        second.start()
        firsts.append((first, second))
    mine = [
        pltpu.make_async_copy(message_ref.at[head, pl.ds(0, size)], kv_ref.at[rank, head], local.at[0]),
        pltpu.make_async_copy(message_ref.at[head, pl.ds(size, rest)], query_ref.at[head], local.at[1]),
    ]
    for copy in mine:
        copy.start()
    onward = []

    def forward(step, source, src):
        for other in range(1, ranks):
            copy = remote(
                src, kv_ref.at[rank, source], send_f.at[step, other], recv_f.at[step, other],
                head * ranks + lax.rem(rank + other, ranks),
            )
            copy.start()
            onward.append(copy)

    forward(0, head, message_ref.at[head, pl.ds(0, size)])
    for step in range(1, heads):
        source = lax.rem(head + heads - step, heads)
        firsts[step - 1][0].wait_recv()
        forward(step, source, kv_ref.at[rank, source])
    for first, second in firsts:
        first.wait_send()
        second.wait()
    for copy in mine + onward:
        copy.wait()


def spread(message, ranks, rows):
    heads, size = message.shape[:2]
    dma = pltpu.SemaphoreType.DMA
    return pl.pallas_call(
        functools.partial(spread_kernel, ranks=ranks),
        in_specs=[ANYWHERE],
        out_specs=(ANYWHERE, ANYWHERE),
        out_shape=(
            jax.ShapeDtypeStruct((ranks, heads, rows + IDS, LANES), low),
            jax.ShapeDtypeStruct((heads, rows // 2, LANES), low),
        ),
        scratch_shapes=[dma((heads,))] * 4 + [dma((heads, ranks))] * 2 + [dma((2,))],
        compiler_params=params(collective_id=0, has_side_effects=True),
    )(message)


def exchange_kernel(message_ref, landed_ref, send, recv, local, *, ranks):
    heads = message_ref.shape[0]
    place = lax.axis_index("dp")
    head = place // ranks
    rank = lax.rem(place, ranks)
    greet(heads, ranks, head, rank, False)
    copies = []
    for step in range(1, heads):
        to = lax.rem(head + step, heads)
        copies.append(
            remote(
                message_ref.at[to], landed_ref.at[head], send.at[step], recv.at[step],
                to * ranks + rank,
            )
        )
        copies[-1].start()
    copies.append(pltpu.make_async_copy(message_ref.at[head], landed_ref.at[head], local))
    copies[-1].start()
    for copy in copies:
        copy.wait()


def exchange(message, ranks, collective_id):
    heads = message.shape[0]
    dma = pltpu.SemaphoreType.DMA
    return pl.pallas_call(
        functools.partial(exchange_kernel, ranks=ranks),
        in_specs=[ANYWHERE],
        out_specs=ANYWHERE,
        out_shape=jax.ShapeDtypeStruct(message.shape, message.dtype),
        scratch_shapes=[dma((heads,)), dma((heads,)), dma],
        compiler_params=params(collective_id=collective_id, has_side_effects=True),
    )(message)


def collect_kernel(
    kv_ref, query_ref, landed_ref, piece_ref, sum_ref,
    send_p, recv_p, send_a, recv_a, send_b, recv_b, local, *, ranks,
):
    heads, rows = kv_ref.shape[1:3]
    half = query_ref.shape[1]
    place = lax.axis_index("dp")
    head = place // ranks
    rank = lax.rem(place, ranks)
    greet(heads, ranks, head, rank, True)
    order = list(range(1, heads)) + [0]
    pieces = {}
    copies = []
    for step in order:
        to = lax.rem(head + step, heads)
        for other in range(1, ranks):
            partner = lax.rem(rank + other, ranks)
            pieces[step, other] = remote(
                kv_ref.at[partner, to], piece_ref.at[other, to],
                send_p.at[step, other], recv_p.at[step, other], head * ranks + partner,
            )
            pieces[step, other].start()
        if step:
            copies.append(
                remote(
                    query_ref.at[to], landed_ref.at[head, pl.ds(rows, half)],
                    send_b.at[step], recv_b.at[step], to * ranks + rank,
                )
            )
        else:
            copies.append(
                pltpu.make_async_copy(
                    query_ref.at[head], landed_ref.at[head, pl.ds(rows, half)], local.at[0]
                )
            )
        copies[-1].start()
    for step in order:
        to = lax.rem(head + step, heads)
        total = kv_ref[rank, to].astype(wide)
        for other in range(1, ranks):
            pieces[step, other].wait_recv()
            total = total + piece_ref[other, to].astype(wide)
        sum_ref[to] = total.astype(low)
        if step:
            copies.append(
                remote(
                    sum_ref.at[to], landed_ref.at[head, pl.ds(0, rows)],
                    send_a.at[step], recv_a.at[step], to * ranks + rank,
                )
            )
        else:
            copies.append(
                pltpu.make_async_copy(
                    sum_ref.at[head], landed_ref.at[head, pl.ds(0, rows)], local.at[1]
                )
            )
        copies[-1].start()
    for piece in pieces.values():
        piece.wait_send()
    for copy in copies:
        copy.wait()


def collect(kv, query):
    ranks, heads, rows = kv.shape[:3]
    dma = pltpu.SemaphoreType.DMA
    return pl.pallas_call(
        functools.partial(collect_kernel, ranks=ranks),
        in_specs=[WHOLE, WHOLE],
        out_specs=ANYWHERE,
        out_shape=jax.ShapeDtypeStruct((heads, rows + rows // 2, LANES), low),
        scratch_shapes=[
            pltpu.VMEM((ranks, heads, rows, LANES), low),
            pltpu.VMEM((heads, rows, LANES), low),
        ]
        + [dma((heads, ranks))] * 2
        + [dma((heads,))] * 4
        + [dma((2,))],
        compiler_params=params(collective_id=3, has_side_effects=True),
    )(kv, query)


def tables(times):
    half = HD // 2
    inverse = 10000.0 ** (-2.0 * jnp.arange(half, dtype=wide) / HD)
    angles = times.astype(wide)[:, None] * inverse[None, :]
    cosine, sine = jnp.cos(angles), jnp.sin(angles)
    return (
        jnp.concatenate([cosine] * (LANES // half), axis=1),
        jnp.concatenate([-sine, sine] * (LANES // HD), axis=1),
    )


def id_rows(x):
    rows = x.reshape(-1, LANES).astype(low)
    return jnp.pad(rows, ((0, IDS // 2 - rows.shape[0]), (0, 0)))


def shards(
    tokens,
    cotangent,
    segment,
    variate,
    time,
    w_qkv,
    w_out,
    w_gateup,
    w_down,
    attn_gain,
    mlp_gain,
    query_gain,
    key_gain,
    var_bias,
):
    rows = tokens.shape[0]
    local_width = w_qkv.shape[2]
    heads = local_width // HD
    dp = lax.axis_size("dp")
    tensor = lax.axis_size("tensor")
    ranks = dp // heads
    place = lax.axis_index("dp")
    head_here = place // ranks
    rank_here = lax.rem(place, ranks)
    width_share = tokens.shape[1] // tensor
    tensor_start = lax.axis_index("tensor") * width_share

    def tensor_sum(x, x_low):
        if tensor == 2:
            return x + lax.ppermute(x_low, "tensor", [(0, 1), (1, 0)]).astype(wide)
        return lax.psum(x_low, "tensor").astype(wide)

    def tensor_share(x):
        mine = lax.dynamic_slice_in_dim(x, tensor_start, width_share, 1)
        if tensor == 2:
            other = lax.dynamic_slice_in_dim(x, width_share - tensor_start, width_share, 1)
            return mine + lax.ppermute(other.astype(low), "tensor", [(0, 1), (1, 0)]).astype(wide)
        return lax.psum_scatter(x, "tensor", scatter_dimension=1, tiled=True)

    cosine, sine = tables(time)
    pair_gain = lambda gain: jnp.concatenate([gain, gain])[None, :]
    ids = jnp.concatenate([id_rows(segment), id_rows(variate)])
    message, raw_query, raw_key, normed_one = project(
        tokens, w_qkv, attn_gain[None, :], pair_gain(query_gain * (LOG2E * HD**-0.5)),
        pair_gain(key_gain), cosine, sine, ids,
    )
    kv, query_in = spread(message, ranks, rows)
    bias_here = lax.dynamic_index_in_dim(var_bias, head_here, 1, False)
    bias_step = (bias_here[0] - bias_here[1]) * LOG2E
    key_op, value_op, query_op, exact, out_message, runs = forward_attention(
        rank_here[None], kv, query_in, key_table(), query_table(bias_step)
    )
    heads_out, attn_part, attn_low = attention_out(exchange(out_message, ranks, 1), w_out)
    inputs = tokens.astype(wide)
    attn_total = tensor_sum(attn_part, attn_low)
    middle = inputs + attn_total
    scale_two = lax.rsqrt(jnp.mean(middle * middle, axis=1, keepdims=True) + EPSILON)
    unit_two = middle * scale_two
    normed_two = (unit_two * mlp_gain).astype(low)
    gate_up = jnp.einsum("td,kdf->ktf", normed_two, w_gateup, preferred_element_type=wide)
    gate_vals = gate_up[0]
    up_vals = gate_up[1]
    sig_gate = jax.nn.sigmoid(gate_vals)
    act_gate = gate_vals * sig_gate
    hidden = (act_gate * up_vals).astype(low)
    mlp_part = jnp.dot(hidden, w_down, preferred_element_type=wide)
    mlp_share = tensor_share(mlp_part)
    output = (lax.dynamic_slice_in_dim(middle, tensor_start, width_share, 1) + mlp_share).astype(low)
    grad_hidden = jnp.einsum("te,fe->tf", cotangent, w_down, preferred_element_type=wide)
    grad_down = jnp.einsum("tf,te->fe", hidden, cotangent, preferred_element_type=wide)
    grad_gate = grad_hidden * up_vals * sig_gate * (1.0 + gate_vals * (1.0 - sig_gate))
    grad_up = grad_hidden * act_gate
    grad_gu = jnp.stack([grad_gate, grad_up]).astype(low)
    grad_gateup = jnp.einsum("td,ktf->kdf", normed_two, grad_gu, preferred_element_type=wide)
    grad_normed_two = jnp.einsum("ktf,kdf->td", grad_gu, w_gateup, preferred_element_type=wide)
    mlp_gain_part = jnp.sum(grad_normed_two * unit_two, axis=0)
    scaled_two = grad_normed_two * mlp_gain
    middle_part = scale_two * (
        scaled_two - unit_two * jnp.mean(scaled_two * unit_two, axis=1, keepdims=True)
    )
    grad_middle = cotangent.astype(wide) + tensor_sum(middle_part, middle_part.astype(low))
    grad_middle_low = grad_middle.astype(low)
    grad_out = jnp.einsum("tc,td->cd", heads_out, grad_middle_low, preferred_element_type=wide)
    grad_landed = exchange(grad_heads_of(grad_middle_low, w_out), ranks, 2)
    own_ids = lax.dynamic_index_in_dim(kv[:, :, rows:], rank_here, 0, False)
    back_kv, back_query, bias_tiles = backward_attention(
        runs, key_op, value_op, query_op, exact, grad_landed, own_ids
    )
    same_sum = jnp.sum(bias_tiles[0])
    other_sum = jnp.sum(bias_tiles[1])
    grad_projected, gain_tile = unproject(
        collect(back_kv, back_query), raw_query, raw_key, pair_gain(query_gain),
        pair_gain(key_gain), cosine, sine,
    )
    query_gain_part = gain_tile[0, :HD] + gain_tile[0, HD:]
    key_gain_part = gain_tile[1, :HD] + gain_tile[1, HD:]
    scale_one = lax.rsqrt(jnp.mean(inputs * inputs, axis=1, keepdims=True) + EPSILON)
    unit_one = inputs * scale_one
    grad_qkv = jnp.einsum("td,kte->kde", normed_one, grad_projected, preferred_element_type=wide)
    grad_normed_one = jnp.einsum("kte,kde->td", grad_projected, w_qkv, preferred_element_type=wide)
    attn_gain_part = jnp.sum(grad_normed_one * unit_one, axis=0)
    scaled_one = grad_normed_one * attn_gain
    input_part = scale_one * (
        scaled_one - unit_one * jnp.mean(scaled_one * unit_one, axis=1, keepdims=True)
    )
    grad_input = lax.dynamic_slice_in_dim(grad_middle, tensor_start, width_share, 1) + tensor_share(
        input_part
    )
    early = lax.psum((grad_gateup.astype(low), grad_down.astype(low)), "dp")
    early, late = lax.optimization_barrier((early, (grad_qkv.astype(low), grad_out.astype(low))))
    late = lax.psum(late, "dp")
    depth = tokens.shape[1]
    head_slot = lax.axis_index("tensor") * heads + head_here
    hit = (jnp.arange(tensor * heads, dtype=jnp.int32) == head_slot).astype(wide)
    small = jnp.concatenate(
        [attn_gain_part, mlp_gain_part, query_gain_part, key_gain_part]
        + [same_sum * hit, other_sum * hit]
    )
    small = lax.psum(small, ("dp", "tensor"))
    gains, biases = small[: 2 * depth + 2 * HD], small[2 * depth + 2 * HD :]
    bias_sum = lax.dynamic_slice_in_dim(
        biases.reshape(2, tensor * heads), lax.axis_index("tensor") * heads, heads, 1
    )
    return (
        output,
        grad_input,
        late[0].astype(wide),
        late[1].astype(wide),
        early[0].astype(wide),
        early[1].astype(wide),
        gains[:depth],
        gains[depth : 2 * depth],
        gains[2 * depth : 2 * depth + HD],
        gains[2 * depth + HD :],
        bias_sum,
    )


def solution(mesh):
    placed = (
        P("dp", None),
        P("dp", None),
        P("dp"),
        P("dp"),
        P("dp"),
        P(None, None, "tensor"),
        P("tensor", None),
        P(None, None, "tensor"),
        P("tensor", None),
        P(),
        P(),
        P(),
        P(),
        P(None, "tensor"),
    )
    return jax.shard_map(
        shards,
        mesh=mesh,
        in_specs=placed,
        out_specs=(
            P("dp", "tensor"),
            P("dp", "tensor"),
            P(None, None, "tensor"),
            P("tensor", None),
            P(None, None, "tensor"),
            P("tensor", None),
            P(),
            P(),
            P(),
            P(),
            P(None, "tensor"),
        ),
        check_vma=False,
    )
```

```python
import functools

import jax
import jax.numpy as jnp
import numpy as np
from jax import lax
from jax.experimental import pallas as pl
from jax.experimental.layout import Layout, with_layout_constraint
from jax.experimental.pallas import tpu as pltpu
from jax.sharding import PartitionSpec as P

HD = 64
LANES = 128
IDS = 16
EPSILON = 1e-05
LOG2E = 1.4426950408889634
FAR = -30000.0
DOCS = 8
VARS = 4
VAR_AT = HD
SEG_AT = VAR_AT + 3 * VARS
ONE_AT = SEG_AT + DOCS
VMEM = 60 * 1024 * 1024
FEWEST = 512
LAGS = (0, 1, 3, 5, 7, 8)
MESH = pl.DeviceIdType.MESH
WHOLE = pl.BlockSpec(memory_space=pltpu.VMEM)
SCALARS = pl.BlockSpec(memory_space=pltpu.SMEM)
ANYWHERE = pl.BlockSpec(memory_space=pl.ANY)
wide = jnp.float32
low = jnp.bfloat16


def params(**more):
    return pltpu.CompilerParams(vmem_limit_bytes=VMEM, **more)


def lanes_of(x):
    return lax.broadcasted_iota(jnp.int32, x.shape, x.ndim - 1)


def dot_nt(a, b):
    return lax.dot_general(a, b, (((1,), (1,)), ((), ())), preferred_element_type=wide)


def dot_tn(a, b):
    return lax.dot_general(a, b, (((0,), (0,)), ((), ())), preferred_element_type=wide)


def dot_nn(a, b):
    return jnp.dot(a, b, preferred_element_type=wide)


def left_pair(a, b):
    return jnp.where(lanes_of(a) < HD, a, pltpu.roll(b, HD, 1))


def right_pair(a, b):
    return jnp.where(lanes_of(a) < HD, pltpu.roll(a, HD, 1), b)


def swap_halves(x):
    return jnp.where(
        lanes_of(x) % HD < HD // 2,
        pltpu.roll(x, LANES - HD // 2, 1),
        pltpu.roll(x, HD // 2, 1),
    )


def head_mean(x):
    row = lax.broadcasted_iota(jnp.int32, (LANES, LANES), 0) // HD
    column = lax.broadcasted_iota(jnp.int32, (LANES, LANES), 1) // HD
    mix = jnp.where(row == column, 1.0 / HD, 0.0).astype(low)
    high = x.astype(low)
    return dot_nn(high, mix) + dot_nn((x - high.astype(wide)).astype(low), mix)


def features(ids, parts, table):
    index = lax.broadcasted_iota(jnp.int32, (IDS, LANES), 0)
    columns = []
    for part in range(parts):
        segs = jnp.broadcast_to(ids[part : part + 1], (IDS, LANES)).astype(jnp.int32)
        at = IDS // 2 + part
        variates = jnp.broadcast_to(ids[at : at + 1], (IDS, LANES)).astype(jnp.int32)
        by_variate = jnp.where(variates == index, 1.0, 0.0)
        by_document = jnp.where(segs == index - VARS, 1.0, 0.0)
        columns.append(
            jnp.where(index < VARS, by_variate, jnp.where(index < VARS + DOCS, by_document, 1.0))
        )
    return dot_tn(jnp.concatenate(columns, axis=1).astype(low), table)


def table_places():
    row = lax.broadcasted_iota(jnp.int32, (IDS, LANES), 0)
    lane = lax.broadcasted_iota(jnp.int32, (IDS, LANES), 1)
    return row, lane


def hot_variates(row, lane, values):
    kept = jnp.where((lane - VAR_AT) % VARS == row, values, 0.0)
    kept = jnp.where(lane < SEG_AT, kept, 0.0)
    kept = jnp.where(lane >= VAR_AT, kept, 0.0)
    return jnp.where(row < VARS, kept, 0.0)


def of_documents(row, lane, values):
    kept = jnp.where(row >= VARS, values, 0.0)
    kept = jnp.where(row < VARS + DOCS, kept, 0.0)
    kept = jnp.where(lane >= SEG_AT, kept, 0.0)
    return jnp.where(lane < ONE_AT, kept, 0.0)


def key_table():
    row, lane = table_places()
    table = hot_variates(row, lane, 1.0)
    table = table + of_documents(row, lane, jnp.where(lane - SEG_AT == row - VARS, 0.0, FAR))
    one = jnp.where(lane >= ONE_AT, jnp.where(lane < ONE_AT + 3, 1.0, 0.0), 0.0)
    return (table + jnp.where(row == VARS + DOCS, one, 0.0)).astype(low)


def query_table(step):
    row, lane = table_places()
    step = jnp.full((IDS, LANES), step, wide)
    high = step.astype(low).astype(wide)
    mid = (step - high).astype(low).astype(wide)
    part = (lane - VAR_AT) // VARS
    step = jnp.where(part == 0, high, jnp.where(part == 1, mid, step - high - mid))
    table = hot_variates(row, lane, step)
    table = table + of_documents(row, lane, jnp.where(lane - SEG_AT == row - VARS, 1.0, 0.0))
    return table.astype(low)


def project_kernel(
    tokens_ref, w_ref, gain_ref, query_gain_ref, key_gain_ref, cosine_ref, sine_ref, ids_ref,
    message_ref, query_ref, key_ref, normed_ref,
):
    rows = tokens_ref.shape[0]

    @pl.when(pl.program_id(0) == 0)
    def norm():
        x = tokens_ref[...].astype(wide)
        scale = lax.rsqrt(jnp.mean(x * x, axis=1, keepdims=True) + EPSILON)
        normed_ref[...] = (x * scale * gain_ref[...]).astype(low)

    normed = normed_ref[...]

    def turned(raw, gain):
        x = raw * lax.rsqrt(head_mean(raw * raw) + EPSILON) * gain
        return x * cosine_ref[...] + swap_halves(x) * sine_ref[...]

    query_ref[...] = dot_nn(normed, w_ref[0])
    key_ref[...] = dot_nn(normed, w_ref[1])
    values = dot_nn(normed, w_ref[2])
    for pair in range(query_ref.shape[1] // LANES):
        span = slice(pair * LANES, (pair + 1) * LANES)
        one, two = 2 * pair, 2 * pair + 1
        query = turned(query_ref[:, span], query_gain_ref[...])
        key = turned(key_ref[:, span], key_gain_ref[...])
        value = values[:, span]
        message_ref[one, :rows] = left_pair(key, value).astype(low)
        message_ref[two, :rows] = right_pair(key, value).astype(low)
        upper, lower = query[: rows // 2], query[rows // 2 :]
        message_ref[one, rows + IDS :] = left_pair(upper, lower).astype(low)
        message_ref[two, rows + IDS :] = right_pair(upper, lower).astype(low)
        message_ref[one, rows : rows + IDS] = ids_ref[...]
        message_ref[two, rows : rows + IDS] = ids_ref[...]


def project(tokens, w_qkv, gain, query_gain, key_gain, cosine, sine, ids):
    rows, depth = tokens.shape
    width = w_qkv.shape[2]
    size = rows + IDS + rows // 2
    wider = LANES * (1 + (width // LANES + 1) % 2)
    column = pl.BlockSpec((rows, wider), lambda i: (0, i))
    return pl.pallas_call(
        project_kernel,
        grid=(width // wider,),
        in_specs=[
            WHOLE,
            pl.BlockSpec((3, depth, wider), lambda i: (0, 0, i)),
            WHOLE, WHOLE, WHOLE, WHOLE, WHOLE, WHOLE,
        ],
        out_specs=(
            pl.BlockSpec((wider // HD, size, LANES), lambda i: (i, 0, 0)),
            column, column,
            pl.BlockSpec((rows, depth), lambda i: (0, 0)),
        ),
        out_shape=(
            jax.ShapeDtypeStruct((width // HD, size, LANES), low),
            jax.ShapeDtypeStruct((rows, width), wide),
            jax.ShapeDtypeStruct((rows, width), wide),
            jax.ShapeDtypeStruct((rows, depth), low),
        ),
        compiler_params=params(),
    )(tokens, w_qkv, gain, query_gain, key_gain, cosine, sine, ids)


def walk(begin, end, body, largest):
    count = (end - begin) // LANES
    many = largest // LANES

    def step(index, carry):
        body(begin + index * largest, largest)
        return carry

    lax.fori_loop(0, count // many, step, 0)
    size = many // 2
    while size:
        piece = size * LANES
        at = begin + (count // (2 * size)) * (2 * piece)

        @pl.when((count // size) % 2 == 1)
        def rest(at=at, piece=piece):
            body(at, piece)

        size //= 2


def scalar(x):
    return x[0, 0].astype(jnp.int32)


def forward_kernel(
    bias_ref, kv_ref, query_in_ref,
    k_ref, v_ref, q_ref, exact_ref, message_ref, runs_ref, acc_ref, seg_ref, upto_ref, keys_ref,
):
    ranks, heads = kv_ref.shape[:2]
    rows = q_ref.shape[0]
    half = rows // 2
    parts = rows // LANES
    block = pl.program_id(0)
    place = lax.axis_index("dp")
    rank = lax.rem(place, ranks)
    head = place // ranks
    filled = lax.broadcasted_iota(jnp.int32, (IDS // 2, LANES), 0) < parts

    @pl.when(block == 0)
    def prepare():
        keys = key_table()
        for rank_at in range(ranks):
            for head_at in range(heads):
                at = head_at * ranks + rank_at
                ids = kv_ref[rank_at, head_at, rows:, :].astype(wide)
                seg_ref[at] = jnp.where(filled, ids[: IDS // 2], DOCS + 1.0)
                extra = features(ids, parts, keys)
                kv = kv_ref[rank_at, head_at, :rows].astype(wide)
                lane = lanes_of(kv)
                span = pl.ds(at * rows, rows)
                k_ref[span, :] = jnp.where(lane < HD, kv, extra).astype(low)
                one = jnp.where(lane < HD + 3, 1.0, 0.0)
                v_ref[span, :] = jnp.where(lane < HD, pltpu.roll(kv, HD, 1), one).astype(low)
        every = seg_ref[...].reshape(ranks * heads * (IDS // 2), LANES)
        own = jnp.stack([seg_ref[head_at * ranks + rank] for head_at in range(heads)])
        own = own.reshape(heads * (IDS // 2), LANES)
        upto_ref[0, 0] = 0
        upto_ref[1, 0] = 0
        for document in range(DOCS):
            for which, segs in ((0, every), (1, own)):
                count = jnp.sum(jnp.where(segs <= document, 1.0, 0.0), keepdims=True)
                upto_ref[which, document + 1] = scalar(count)
        for at in range(ranks * heads):
            segs = seg_ref[at]
            first = scalar(segs[:1, :1])
            last = scalar(segs[parts - 1 : parts, LANES - 1 :])
            keys_ref[0, at] = upto_ref[0, first] // LANES * LANES
            keys_ref[1, at] = (upto_ref[0, last + 1] + LANES - 1) // LANES * LANES
            runs_ref[0, at] = upto_ref[1, first] // LANES * LANES
            runs_ref[1, at] = (upto_ref[1, last + 1] + LANES - 1) // LANES * LANES

    begin = keys_ref[0, block * ranks + rank]
    end = keys_ref[1, block * ranks + rank]
    queries = query_table((bias_ref[0, head] - bias_ref[1, head]) * LOG2E)
    ids = kv_ref[rank, block, pl.ds(rows, IDS), :].astype(wide)
    extra = features(ids, parts, queries)
    folded = query_in_ref[0].astype(wide)
    head_part = jnp.concatenate([folded, pltpu.roll(folded, HD, 1)], axis=0)
    q_ref[...] = jnp.where(lanes_of(extra) < HD, head_part, extra).astype(low)
    acc_ref[...] = jnp.zeros_like(acc_ref)

    def step(start, size):
        span = pl.ds(pl.multiple_of(start, LANES), size)
        probs = jnp.exp2(dot_nt(q_ref[...], k_ref[span, :])).astype(low)
        acc_ref[...] += dot_nn(probs, v_ref[span, :])

    walk(begin, end, step, 2048)
    total = acc_ref[...]
    row_sum = total[:, HD : HD + 1]
    exact = total / row_sum
    exact_ref[...] = jnp.where(lanes_of(total) < HD, exact, jnp.log2(row_sum))
    message_ref[0] = left_pair(exact[:half], exact[half:]).astype(low)


def forward_attention(bias, kv, query):
    ranks, heads, size = kv.shape[:3]
    rows = size - IDS
    every = ranks * heads * rows
    part = pl.BlockSpec((rows, LANES), lambda i: (i, 0))
    fold = pl.BlockSpec((1, rows // 2, LANES), lambda i: (i, 0, 0))
    return pl.pallas_call(
        forward_kernel,
        grid=(heads,),
        in_specs=[SCALARS, WHOLE, fold],
        out_specs=(WHOLE, WHOLE, part, part, fold, SCALARS),
        scratch_shapes=[
            pltpu.VMEM((rows, LANES), wide),
            pltpu.VMEM((ranks * heads, IDS // 2, LANES), wide),
            pltpu.SMEM((2, DOCS + 1), jnp.int32),
            pltpu.SMEM((2, ranks * heads), jnp.int32),
        ],
        out_shape=(
            jax.ShapeDtypeStruct((every, LANES), low),
            jax.ShapeDtypeStruct((every, LANES), low),
            jax.ShapeDtypeStruct((heads * rows, LANES), low),
            jax.ShapeDtypeStruct((heads * rows, LANES), wide),
            jax.ShapeDtypeStruct((heads, rows // 2, LANES), low),
            jax.ShapeDtypeStruct((2, ranks * heads), jnp.int32),
        ),
        compiler_params=params(),
    )(bias, kv, query)


def split_lanes(column, lane, at):
    high = column.astype(low).astype(wide)
    mid = (column - high).astype(low).astype(wide)
    parts = jnp.where(lane == at, high, jnp.where(lane == at + 1, mid, column - high - mid))
    return jnp.where(lane < at + 3, parts, 0.0)


def backward_kernel(
    runs_ref, k_ref, v_ref, q_in_ref, exact_ref, grad_in_ref, ids_ref,
    kv_ref, message_ref, bias_ref, q_ref, g_ref, kt_ref, dk_ref, dv_ref, dq_ref,
):
    heads, half = grad_in_ref.shape[:2]
    rows = 2 * half
    block = pl.program_id(0)

    @pl.when(block == 0)
    def prepare():
        dq_ref[...] = jnp.zeros_like(dq_ref)
        for head_at in range(heads):
            folded = grad_in_ref[head_at].astype(wide)
            for side in range(2):
                span = pl.ds(head_at * rows + side * half, half)
                grad = folded if side == 0 else pltpu.roll(folded, HD, 1)
                lane = lanes_of(grad)
                grad = jnp.where(lane < HD, grad, 0.0)
                exact = exact_ref[span, :]
                delta = jnp.sum(grad * exact, axis=1, keepdims=True)
                g_ref[span, :] = jnp.where(lane < HD, grad, split_lanes(-delta, lane, HD)).astype(low)
                query = q_in_ref[span, :].astype(wide)
                total = split_lanes(-exact[:, HD : HD + 1], lane, ONE_AT)
                q_ref[span, :] = jnp.where(lane < ONE_AT, query, total).astype(low)

    dk_ref[...] = jnp.zeros_like(dk_ref)
    dv_ref[...] = jnp.zeros_like(dv_ref)
    key = k_ref[...]
    value = v_ref[...]
    kt_ref[...] = key.astype(wide).T.astype(low)

    def step(start, size):
        span = pl.ds(pl.multiple_of(start, LANES), size)
        query = q_ref[span, :]
        grad = g_ref[span, :]
        probs = jnp.exp2(dot_nt(key, query))
        grad_scores = (probs * dot_nt(value, grad)).astype(low)
        dv_ref[...] += dot_nn(probs.astype(low), grad)
        dk_ref[...] += dot_nn(grad_scores, query)
        dq_ref[:, span] += dot_nn(kt_ref[...], grad_scores)

    walk(runs_ref[0, block], runs_ref[1, block], step, 2048)
    kv_ref[0, 0] = left_pair(dk_ref[...] * (1.0 / LOG2E), dv_ref[...]).astype(low)

    @pl.when(block == pl.num_programs(0) - 1)
    def finish():
        same = jnp.zeros((8, LANES), wide)
        every = jnp.zeros((8, LANES), wide)
        index = lax.broadcasted_iota(jnp.int32, (8, LANES), 0)
        for head_at in range(heads):
            ids = ids_ref[head_at].astype(wide)
            for part in range(rows // LANES):
                at = head_at * rows + part * LANES
                by_variate = jnp.where(index < VARS, dq_ref[VAR_AT : VAR_AT + 8, at : at + LANES], 0.0)
                variates = jnp.broadcast_to(
                    ids[IDS // 2 + part : IDS // 2 + part + 1], (8, LANES)
                ).astype(jnp.int32)
                same = same + jnp.where(variates == index, by_variate, 0.0)
                every = every + by_variate
            span = dq_ref[:, head_at * rows : (head_at + 1) * rows].T * HD**-0.5
            message_ref[head_at] = left_pair(span[:half], span[half:]).astype(low)
        bias_ref[0] = same
        bias_ref[1] = every - same


def backward_attention(runs, key, value, query, exact, grad, ids):
    every = key.shape[0]
    heads, half = grad.shape[:2]
    rows = 2 * half
    ranks = every // (heads * rows)
    part = pl.BlockSpec((rows, LANES), lambda i, *_: (i, 0))
    return pl.pallas_call(
        backward_kernel,
        grid_spec=pltpu.PrefetchScalarGridSpec(
            num_scalar_prefetch=1,
            grid=(ranks * heads,),
            in_specs=[part, part, WHOLE, WHOLE, WHOLE, WHOLE],
            out_specs=(
                pl.BlockSpec((1, 1, rows, LANES), lambda i, *_: (i % ranks, i // ranks, 0, 0)),
                WHOLE,
                WHOLE,
            ),
            scratch_shapes=[
                pltpu.VMEM((heads * rows, LANES), low),
                pltpu.VMEM((heads * rows, LANES), low),
                pltpu.VMEM((LANES, rows), low),
                pltpu.VMEM((rows, LANES), wide),
                pltpu.VMEM((rows, LANES), wide),
                pltpu.VMEM((LANES, heads * rows), wide),
            ],
        ),
        out_shape=(
            jax.ShapeDtypeStruct((ranks, heads, rows, LANES), low),
            jax.ShapeDtypeStruct((heads, half, LANES), low),
            jax.ShapeDtypeStruct((2, 8, LANES), wide),
        ),
        compiler_params=params(),
    )(runs, key, value, query, exact, grad, ids)


def out_kernel(landed_ref, *refs):
    tensor, heads, half = landed_ref.shape[:3]
    w_refs, (heads_ref, part_ref, other_ref) = refs[:tensor], refs[tensor:]
    for share in range(tensor):
        to_ref = other_ref if share else heads_ref
        for pair in range(heads // 2):
            one = landed_ref[share, 2 * pair].astype(wide)
            two = landed_ref[share, 2 * pair + 1].astype(wide)
            span = pl.ds(pair * LANES, LANES)
            to_ref[:half, span] = left_pair(one, two).astype(low)
            to_ref[half:, span] = right_pair(one, two).astype(low)
        part = dot_nn(to_ref[...], w_refs[share][...])
        if share:
            part_ref[...] += part
        else:
            part_ref[...] = part


def attention_out(landed, w_outs):
    tensor, heads, half = landed.shape[:3]
    depth = w_outs[0].shape[1]
    return pl.pallas_call(
        out_kernel,
        in_specs=[WHOLE] * (1 + tensor),
        out_specs=(WHOLE, WHOLE),
        out_shape=(
            jax.ShapeDtypeStruct((2 * half, heads * HD), low),
            jax.ShapeDtypeStruct((2 * half, depth), wide),
        ),
        scratch_shapes=[pltpu.VMEM((2 * half, heads * HD), low)],
        compiler_params=params(),
    )(landed, *w_outs)


def grad_heads_kernel(grad_ref, w_ref, message_ref):
    half = message_ref.shape[1]
    for pair in range(message_ref.shape[0] // 2):
        both = dot_nt(grad_ref[...], w_ref[pair * LANES : (pair + 1) * LANES, :])
        message_ref[2 * pair] = left_pair(both[:half], both[half:]).astype(low)
        message_ref[2 * pair + 1] = right_pair(both[:half], both[half:]).astype(low)


def grad_heads_of(grad, w_out):
    return pl.pallas_call(
        grad_heads_kernel,
        in_specs=[WHOLE, WHOLE],
        out_specs=WHOLE,
        out_shape=jax.ShapeDtypeStruct((w_out.shape[0] // HD, grad.shape[0] // 2, LANES), low),
        compiler_params=params(),
    )(grad, w_out)


def unproject_kernel(
    landed_ref, query_ref, key_ref, query_gain_ref, key_gain_ref, cosine_ref, sine_ref,
    grad_ref, gains_ref,
):
    rows = query_ref.shape[0]
    half = rows // 2

    @pl.when(pl.program_id(0) == 0)
    def start():
        gains_ref[...] = jnp.zeros_like(gains_ref)

    def back(turned, raw_ref, gain_ref, at):
        grad = turned * cosine_ref[...] - swap_halves(turned) * sine_ref[...]
        raw = raw_ref[...]
        scale = lax.rsqrt(head_mean(raw * raw) + EPSILON)
        unit = raw * scale
        gains_ref[at : at + 1] += jnp.sum(grad * unit, axis=0, keepdims=True)
        scaled = grad * gain_ref[...]
        return scale * (scaled - unit * head_mean(scaled * unit))

    key_one = landed_ref[0, :rows].astype(wide)
    key_two = landed_ref[1, :rows].astype(wide)
    query_one = landed_ref[0, rows:].astype(wide)
    query_two = landed_ref[1, rows:].astype(wide)
    query = jnp.concatenate(
        [left_pair(query_one, query_two), right_pair(query_one, query_two)], axis=0
    )
    grad_ref[0] = back(query, query_ref, query_gain_ref, 0).astype(low)
    grad_ref[1] = back(left_pair(key_one, key_two), key_ref, key_gain_ref, 1).astype(low)
    grad_ref[2] = right_pair(key_one, key_two).astype(low)


def unproject(landed, raw_query, raw_key, query_gain, key_gain, cosine, sine):
    rows, width = raw_query.shape
    column = pl.BlockSpec((rows, LANES), lambda i: (0, i))
    return pl.pallas_call(
        unproject_kernel,
        grid=(width // LANES,),
        in_specs=[
            pl.BlockSpec((2, rows + rows // 2, LANES), lambda i: (i, 0, 0)),
            column, column, WHOLE, WHOLE, WHOLE, WHOLE,
        ],
        out_specs=(
            pl.BlockSpec((3, rows, LANES), lambda i: (0, 0, i)),
            pl.BlockSpec((8, LANES), lambda i: (0, 0)),
        ),
        out_shape=(
            jax.ShapeDtypeStruct((3, rows, width), low),
            jax.ShapeDtypeStruct((8, LANES), wide),
        ),
        compiler_params=params(),
    )(landed, raw_query, raw_key, query_gain, key_gain, cosine, sine)


def remote(src, dst, send, recv, place):
    return pltpu.make_async_remote_copy(
        src_ref=src, dst_ref=dst, send_sem=send, recv_sem=recv,
        device_id={"dp": place}, device_id_type=MESH,
    )


def greet(heads, ranks, head, rank, with_ranks):
    barrier = pltpu.get_barrier_semaphore()
    for step in range(1, heads):
        place = lax.rem(head + step, heads) * ranks + rank
        pl.semaphore_signal(barrier, inc=1, device_id={"dp": place}, device_id_type=MESH)
    if with_ranks:
        for step in range(1, ranks):
            place = head * ranks + lax.rem(rank + step, ranks)
            pl.semaphore_signal(barrier, inc=1, device_id={"dp": place}, device_id_type=MESH)
    pl.semaphore_wait(barrier, heads - 1 + (ranks - 1 if with_ranks else 0))


def spread_kernel(
    message_ref, kv_ref, query_ref, send_a, recv_a, send_b, recv_b, send_f, recv_f, local, *, ranks
):
    heads = message_ref.shape[0]
    size = kv_ref.shape[2]
    rest = query_ref.shape[1]
    place = lax.axis_index("dp")
    head = place // ranks
    rank = lax.rem(place, ranks)
    greet(heads, ranks, head, rank, True)
    firsts = []
    for step in range(1, heads):
        to = lax.rem(head + step, heads)
        at = to * ranks + rank
        first = remote(
            message_ref.at[to, pl.ds(0, size)], kv_ref.at[rank, head],
            send_a.at[step], recv_a.at[step], at,
        )
        second = remote(
            message_ref.at[to, pl.ds(size, rest)], query_ref.at[head],
            send_b.at[step], recv_b.at[step], at,
        )
        first.start()
        second.start()
        firsts.append((first, second))
    mine = [
        pltpu.make_async_copy(message_ref.at[head, pl.ds(0, size)], kv_ref.at[rank, head], local.at[0]),
        pltpu.make_async_copy(message_ref.at[head, pl.ds(size, rest)], query_ref.at[head], local.at[1]),
    ]
    for copy in mine:
        copy.start()
    onward = []

    def forward(step, source, src):
        for other in range(1, ranks):
            copy = remote(
                src, kv_ref.at[rank, source], send_f.at[step, other], recv_f.at[step, other],
                head * ranks + lax.rem(rank + other, ranks),
            )
            copy.start()
            onward.append(copy)

    forward(0, head, message_ref.at[head, pl.ds(0, size)])
    for step in range(1, heads):
        source = lax.rem(head + heads - step, heads)
        firsts[step - 1][0].wait_recv()
        forward(step, source, kv_ref.at[rank, source])
    for first, second in firsts:
        first.wait_send()
        second.wait()
    for copy in mine + onward:
        copy.wait()


def spread(message, ranks, rows):
    heads, size = message.shape[:2]
    dma = pltpu.SemaphoreType.DMA
    return pl.pallas_call(
        functools.partial(spread_kernel, ranks=ranks),
        in_specs=[ANYWHERE],
        out_specs=(ANYWHERE, ANYWHERE),
        out_shape=(
            jax.ShapeDtypeStruct((ranks, heads, rows + IDS, LANES), low),
            jax.ShapeDtypeStruct((heads, rows // 2, LANES), low),
        ),
        scratch_shapes=[dma((heads,))] * 4 + [dma((heads, ranks))] * 2 + [dma((2,))],
        compiler_params=params(collective_id=0, has_side_effects=True),
    )(message)


def exchange_kernel(message_ref, landed_ref, send, recv, local, *, ranks):
    heads = message_ref.shape[0]
    place = lax.axis_index("dp")
    head = place // ranks
    rank = lax.rem(place, ranks)
    greet(heads, ranks, head, rank, False)
    copies = []
    for step in range(1, heads):
        to = lax.rem(head + step, heads)
        copies.append(
            remote(
                message_ref.at[to], landed_ref.at[head], send.at[step], recv.at[step],
                to * ranks + rank,
            )
        )
        copies[-1].start()
    copies.append(pltpu.make_async_copy(message_ref.at[head], landed_ref.at[head], local))
    copies[-1].start()
    for copy in copies:
        copy.wait()


def exchange(message, ranks, collective_id):
    heads = message.shape[0]
    dma = pltpu.SemaphoreType.DMA
    return pl.pallas_call(
        functools.partial(exchange_kernel, ranks=ranks),
        in_specs=[ANYWHERE],
        out_specs=ANYWHERE,
        out_shape=jax.ShapeDtypeStruct(message.shape, message.dtype),
        scratch_shapes=[dma((heads,)), dma((heads,)), dma],
        compiler_params=params(collective_id=collective_id, has_side_effects=True),
    )(message)


def share_out_kernel(message_ref, landed_ref, send, recv, send_t, recv_t, local, *, ranks, tensor):
    heads = message_ref.shape[0]
    place = lax.axis_index("dp")
    side = lax.axis_index("tensor")
    head = place // ranks
    rank = lax.rem(place, ranks)
    barrier = pltpu.get_barrier_semaphore()
    for step in range(1, tensor):
        to = lax.rem(side + step, tensor)
        pl.semaphore_signal(barrier, inc=1, device_id={"tensor": to}, device_id_type=MESH)
    for step in range(1, heads):
        to = lax.rem(head + step, heads) * ranks + rank
        pl.semaphore_signal(barrier, inc=1, device_id={"dp": to}, device_id_type=MESH)
    pl.semaphore_wait(barrier, heads + tensor - 2)
    copies = []
    for step in range(1, heads):
        to = lax.rem(head + step, heads)
        copies.append(
            remote(
                message_ref.at[to], landed_ref.at[0, head], send.at[step], recv.at[step],
                to * ranks + rank,
            )
        )
        copies[-1].start()
    mine = pltpu.make_async_copy(message_ref.at[head], landed_ref.at[0, head], local)
    mine.start()
    onward = []

    def relay(step, source, src):
        for other in range(1, tensor):
            copy = pltpu.make_async_remote_copy(
                src_ref=src, dst_ref=landed_ref.at[tensor - other, source],
                send_sem=send_t.at[step, other], recv_sem=recv_t.at[step, other],
                device_id={"tensor": lax.rem(side + other, tensor)}, device_id_type=MESH,
            )
            copy.start()
            onward.append(copy)

    relay(0, head, message_ref.at[head])
    for step in range(1, heads):
        source = lax.rem(head + heads - step, heads)
        copies[step - 1].wait_recv()
        relay(step, source, landed_ref.at[0, source])
    for copy in copies:
        copy.wait_send()
    mine.wait()
    for copy in onward:
        copy.wait()


def share_out(message, ranks, tensor):
    heads = message.shape[0]
    dma = pltpu.SemaphoreType.DMA
    return pl.pallas_call(
        functools.partial(share_out_kernel, ranks=ranks, tensor=tensor),
        in_specs=[ANYWHERE],
        out_specs=ANYWHERE,
        out_shape=jax.ShapeDtypeStruct((tensor,) + message.shape, message.dtype),
        scratch_shapes=[dma((heads,))] * 2 + [dma((heads, tensor))] * 2 + [dma],
        compiler_params=params(collective_id=1, has_side_effects=True),
    )(message)


def total_kernel(*refs, arrays, chunks, zs, tensor):
    ins, refs = refs[: arrays + 1], refs[arrays + 1 :]
    outs, refs = refs[: arrays + 1], refs[arrays + 1 :]
    count = len(chunks)
    scratch, refs = refs[: 5 * count], refs[5 * count :]
    near_ref, far_ref, line_ref, side_ref, send, recv, send_z, recv_z, send_s, recv_s = refs
    place = lax.axis_index("dp")
    side = lax.axis_index("tensor")
    core = lax.rem(place, 2)
    x = lax.rem(place // 2, 2)
    z = place // 4
    base = place - core
    core_mate = base + 1 - core
    x_mate = z * 4 + (1 - x) * 2 + core
    z_mates = [lax.rem(z + step, zs) * 4 + x * 2 + core for step in range(1, zs)]

    barrier = pltpu.get_barrier_semaphore()
    for to in [core_mate, x_mate] + z_mates:
        pl.semaphore_signal(barrier, inc=1, device_id={"dp": to}, device_id_type=MESH)
    for step in range(1, tensor):
        to = lax.rem(side + step, tensor)
        pl.semaphore_signal(barrier, inc=1, device_id={"tensor": to}, device_id_type=MESH)
    pl.semaphore_wait(barrier, zs + tensor)
    sent = []
    waits = {}

    def rows_at(at, size):
        return pl.ds(pl.multiple_of(at, 16), size)

    def pieces(chunk):
        index, lead, begin, size = chunks[chunk]
        source = ins[index] if lead is None else ins[index].at[lead]
        target = outs[index] if lead is None else outs[index].at[lead]
        source, target = (ref.at[pl.ds(begin, size)] for ref in (source, target))
        return source, target, size, scratch[5 * chunk : 5 * chunk + 5]

    def go(copy, key):
        copy.start()
        sent.append(copy)
        waits.setdefault(key, []).append(copy)

    def arrived(key):
        for copy in waits[key]:
            copy.wait_recv()

    def halve_core(chunk):
        source, _, size, (first, _, _, _, _) = pieces(chunk)
        go(
            remote(
                source.at[rows_at((1 - core) * (size // 2), size // 2)], first,
                send.at[chunk, 0], recv.at[chunk, 0], core_mate,
            ),
            (chunk, 0),
        )

    def halve_x(chunk):
        source, _, size, (first, half, second, _, _) = pieces(chunk)
        arrived((chunk, 0))
        mine = source[rows_at(core * (size // 2), size // 2), :].astype(wide)
        half[...] = (mine + first[...].astype(wide)).astype(low)
        go(
            remote(
                half.at[rows_at((1 - x) * (size // 4), size // 4)], second,
                send.at[chunk, 1], recv.at[chunk, 1], x_mate,
            ),
            (chunk, 1),
        )

    def part_z(chunk):
        _, _, size, (_, half, second, quarter, third) = pieces(chunk)
        arrived((chunk, 1))
        mine = half[rows_at(x * (size // 4), size // 4), :].astype(wide)
        quarter[...] = (mine + second[...].astype(wide)).astype(low)
        part = size // (4 * zs)
        for step in range(1, zs):
            to = lax.rem(z + step, zs)
            go(
                remote(
                    quarter.at[rows_at(to * part, part)], third.at[step],
                    send_z.at[chunk, 0, step], recv_z.at[chunk, 0, step], z_mates[step - 1],
                ),
                (chunk, 2),
            )

    def spread_z(chunk):
        _, target, size, (_, _, _, quarter, third) = pieces(chunk)
        arrived((chunk, 2))
        part = size // (4 * zs)
        total = quarter[rows_at(z * part, part), :].astype(wide)
        for step in range(1, zs):
            total = total + third[step].astype(wide)
        span = rows_at(core * (size // 2) + x * (size // 4) + z * part, part)
        target[span, :] = total.astype(low)
        for step in range(1, zs):
            go(
                remote(
                    target.at[span], target.at[span],
                    send_z.at[chunk, 1, step], recv_z.at[chunk, 1, step], z_mates[step - 1],
                ),
                (chunk, 3),
            )

    def spread_x(chunk):
        _, target, size, _ = pieces(chunk)
        arrived((chunk, 3))
        span = rows_at(core * (size // 2) + x * (size // 4), size // 4)
        go(
            remote(target.at[span], target.at[span], send.at[chunk, 2], recv.at[chunk, 2], x_mate),
            (chunk, 4),
        )

    def spread_core(chunk):
        _, target, size, _ = pieces(chunk)
        arrived((chunk, 4))
        span = rows_at(core * (size // 2), size // 2)
        go(
            remote(target.at[span], target.at[span], send.at[chunk, 3], recv.at[chunk, 3], core_mate),
            (chunk, 5),
        )

    small = ins[arrays]

    def small_core():
        near_ref[0] = small[...]
        go(remote(near_ref.at[0], near_ref.at[1], send_s.at[0, 0], recv_s.at[0, 0], core_mate), "c")

    def small_x():
        arrived("c")
        far_ref[0] = near_ref[0] + near_ref[1]
        go(remote(far_ref.at[0], far_ref.at[1], send_s.at[1, 0], recv_s.at[1, 0], x_mate), "x")

    def small_z():
        arrived("x")
        line_ref[z] = far_ref[0] + far_ref[1]
        for step in range(1, zs):
            go(
                remote(
                    line_ref.at[z], line_ref.at[z], send_s.at[2, step], recv_s.at[2, step],
                    z_mates[step - 1],
                ),
                "z",
            )

    def small_side():
        arrived("z")
        total = line_ref[0]
        for at in range(1, zs):
            total = total + line_ref[at]
        side_ref[side] = total
        for step in range(1, tensor):
            copy = pltpu.make_async_remote_copy(
                src_ref=side_ref.at[side], dst_ref=side_ref.at[side],
                send_sem=send_s.at[3, step], recv_sem=recv_s.at[3, step],
                device_id={"tensor": lax.rem(side + step, tensor)}, device_id_type=MESH,
            )
            go(copy, "s")

    def small_end():
        if tensor > 1:
            arrived("s")
        total = side_ref[0]
        for at in range(1, tensor):
            total = total + side_ref[at]
        outs[arrays][...] = total

    stages = [halve_core, halve_x, part_z, spread_z, spread_x, spread_core]
    smalls = [small_core, small_x, small_z, small_side, small_end]
    for tick in range(max(count + LAGS[-1], len(smalls))):
        for stage in range(len(stages)):
            if 0 <= tick - LAGS[stage] < count:
                stages[stage](tick - LAGS[stage])
        if tick < len(smalls):
            smalls[tick]()
    for chunk in range(count):
        arrived((chunk, 5))
    for copy in sent:
        copy.wait_send()


def total_sums(arrays, small, dp, tensor):
    zs = dp // 4
    chunks = []
    scratch = []
    for index, array in enumerate(arrays):
        leads = [None] if array.ndim == 2 else list(range(array.shape[0]))
        size, width = array.shape[-2:]
        total, size = size, min(size, max(64 * zs, FEWEST))
        for lead, begin in [(a, b) for a in leads for b in range(0, total, size)]:
            chunks.append((index, lead, begin, size))
            scratch += [
                pltpu.VMEM((size // 2, width), low),
                pltpu.VMEM((size // 2, width), low),
                pltpu.VMEM((size // 4, width), low),
                pltpu.VMEM((size // 4, width), low),
                pltpu.VMEM((zs, size // (4 * zs), width), low),
            ]
    dma = pltpu.SemaphoreType.DMA
    count = len(chunks)
    return pl.pallas_call(
        functools.partial(
            total_kernel, arrays=len(arrays), chunks=tuple(chunks), zs=zs, tensor=tensor
        ),
        in_specs=[WHOLE] * (len(arrays) + 1),
        out_specs=(WHOLE,) * (len(arrays) + 1),
        out_shape=tuple(jax.ShapeDtypeStruct(a.shape, a.dtype) for a in [*arrays, small]),
        scratch_shapes=scratch
        + [
            pltpu.VMEM((2,) + small.shape, wide),
            pltpu.VMEM((2,) + small.shape, wide),
            pltpu.VMEM((zs,) + small.shape, wide),
            pltpu.VMEM((tensor,) + small.shape, wide),
        ]
        + [dma((count, 4))] * 2
        + [dma((count, 2, zs))] * 2
        + [dma((4, max(zs, tensor)))] * 2,
        compiler_params=params(collective_id=4, has_side_effects=True),
    )(*arrays, small)


def collect_kernel(
    kv_ref, query_ref, landed_ref, piece_ref, sum_ref,
    send_p, recv_p, send_a, recv_a, send_b, recv_b, local, *, ranks,
):
    heads, rows = kv_ref.shape[1:3]
    half = query_ref.shape[1]
    place = lax.axis_index("dp")
    head = place // ranks
    rank = lax.rem(place, ranks)
    greet(heads, ranks, head, rank, True)
    order = list(range(1, heads)) + [0]
    pieces = {}
    copies = []
    for step in order:
        to = lax.rem(head + step, heads)
        for other in range(1, ranks):
            partner = lax.rem(rank + other, ranks)
            pieces[step, other] = remote(
                kv_ref.at[partner, to], piece_ref.at[other, to],
                send_p.at[step, other], recv_p.at[step, other], head * ranks + partner,
            )
            pieces[step, other].start()
        if step:
            copies.append(
                remote(
                    query_ref.at[to], landed_ref.at[head, pl.ds(rows, half)],
                    send_b.at[step], recv_b.at[step], to * ranks + rank,
                )
            )
        else:
            copies.append(
                pltpu.make_async_copy(
                    query_ref.at[head], landed_ref.at[head, pl.ds(rows, half)], local.at[0]
                )
            )
        copies[-1].start()
    for step in order:
        to = lax.rem(head + step, heads)
        total = kv_ref[rank, to].astype(wide)
        for other in range(1, ranks):
            pieces[step, other].wait_recv()
            total = total + piece_ref[other, to].astype(wide)
        sum_ref[to] = total.astype(low)
        if step:
            copies.append(
                remote(
                    sum_ref.at[to], landed_ref.at[head, pl.ds(0, rows)],
                    send_a.at[step], recv_a.at[step], to * ranks + rank,
                )
            )
        else:
            copies.append(
                pltpu.make_async_copy(
                    sum_ref.at[head], landed_ref.at[head, pl.ds(0, rows)], local.at[1]
                )
            )
        copies[-1].start()
    for piece in pieces.values():
        piece.wait_send()
    for copy in copies:
        copy.wait()


def collect(kv, query):
    ranks, heads, rows = kv.shape[:3]
    dma = pltpu.SemaphoreType.DMA
    return pl.pallas_call(
        functools.partial(collect_kernel, ranks=ranks),
        in_specs=[WHOLE, WHOLE],
        out_specs=ANYWHERE,
        out_shape=jax.ShapeDtypeStruct((heads, rows + rows // 2, LANES), low),
        scratch_shapes=[
            pltpu.VMEM((ranks, heads, rows, LANES), low),
            pltpu.VMEM((heads, rows, LANES), low),
        ]
        + [dma((heads, ranks))] * 2
        + [dma((heads,))] * 4
        + [dma((2,))],
        compiler_params=params(collective_id=3, has_side_effects=True),
    )(kv, query)


def tables(times):
    half = HD // 2
    lane = np.arange(LANES)
    inverse = (10000.0 ** (-2.0 * (lane % half) / HD)).astype(np.float32)
    sign = np.where(lane % HD < half, -1.0, 1.0).astype(np.float32)
    angles = times.astype(wide)[:, None] * inverse[None, :]
    return jnp.cos(angles), jnp.sin(angles) * sign[None, :]


def keep_order(x):
    return with_layout_constraint(x, Layout(major_to_minor=tuple(range(x.ndim))))


def id_rows(x):
    rows = x.reshape(-1, LANES).astype(low)
    return jnp.pad(rows, ((0, IDS // 2 - rows.shape[0]), (0, 0)))


def shards(
    tokens,
    cotangent,
    segment,
    variate,
    time,
    w_qkv,
    w_out,
    w_gateup,
    w_down,
    attn_gain,
    mlp_gain,
    query_gain,
    key_gain,
    var_bias,
):
    rows = tokens.shape[0]
    local_width = w_qkv.shape[2]
    heads = local_width // HD
    dp = lax.axis_size("dp")
    tensor = lax.axis_size("tensor")
    ranks = dp // heads
    place = lax.axis_index("dp")
    head_here = place // ranks
    rank_here = lax.rem(place, ranks)
    width_share = tokens.shape[1] // tensor
    tensor_start = lax.axis_index("tensor") * width_share

    def tensor_sum(x, x_low):
        if tensor == 2:
            return x + lax.ppermute(x_low, "tensor", [(0, 1), (1, 0)]).astype(wide)
        return lax.psum(x_low, "tensor").astype(wide)

    def tensor_share(x):
        mine = lax.dynamic_slice_in_dim(x, tensor_start, width_share, 1)
        if tensor == 2:
            other = lax.dynamic_slice_in_dim(x, width_share - tensor_start, width_share, 1)
            return mine + lax.ppermute(other.astype(low), "tensor", [(0, 1), (1, 0)]).astype(wide)
        return lax.psum_scatter(x, "tensor", scatter_dimension=1, tiled=True)

    cosine, sine = tables(time)
    pair_gain = lambda gain: jnp.concatenate([gain, gain])[None, :]
    ids = jnp.concatenate([id_rows(segment), id_rows(variate)])
    w_outs = [w_out] + [
        lax.ppermute(w_out, "tensor", [((i + step) % tensor, i) for i in range(tensor)])
        for step in range(1, tensor)
    ]
    message, raw_query, raw_key, normed_one = project(
        tokens, w_qkv, attn_gain[None, :], pair_gain(query_gain * (LOG2E * HD**-0.5)),
        pair_gain(key_gain), cosine, sine, ids,
    )
    kv, query_in = spread(message, ranks, rows)
    key_op, value_op, query_op, exact, out_message, runs = forward_attention(
        var_bias, kv, query_in
    )
    heads_out, attn_total = attention_out(share_out(out_message, ranks, tensor), w_outs)
    inputs = tokens.astype(wide)
    middle = inputs + attn_total
    scale_two = lax.rsqrt(jnp.mean(middle * middle, axis=1, keepdims=True) + EPSILON)
    unit_two = middle * scale_two
    normed_two = (unit_two * mlp_gain).astype(low)
    gate_up = jnp.einsum("td,kdf->ktf", normed_two, w_gateup, preferred_element_type=wide)
    gate_vals = gate_up[0]
    up_vals = gate_up[1]
    sig_gate = jax.nn.sigmoid(gate_vals)
    act_gate = gate_vals * sig_gate
    hidden = (act_gate * up_vals).astype(low)
    mlp_part = jnp.dot(hidden, w_down, preferred_element_type=wide)
    grad_hidden = jnp.einsum("te,fe->tf", cotangent, w_down, preferred_element_type=wide)
    grad_gate = grad_hidden * up_vals * sig_gate * (1.0 + gate_vals * (1.0 - sig_gate))
    grad_up = grad_hidden * act_gate
    grad_gu = jnp.stack([grad_gate, grad_up]).astype(low)
    grad_normed_two = jnp.einsum("ktf,kdf->td", grad_gu, w_gateup, preferred_element_type=wide)
    mlp_gain_part = jnp.sum(grad_normed_two * unit_two, axis=0)
    scaled_two = grad_normed_two * mlp_gain
    middle_part = scale_two * (
        scaled_two - unit_two * jnp.mean(scaled_two * unit_two, axis=1, keepdims=True)
    )
    middle_low, hidden_late, grad_gu_late = lax.optimization_barrier(
        (middle_part.astype(low), hidden, grad_gu)
    )
    grad_down = jnp.einsum("tf,te->fe", hidden_late, cotangent, preferred_element_type=wide)
    grad_gateup = jnp.einsum("td,ktf->kdf", normed_two, grad_gu_late, preferred_element_type=wide)
    early = (keep_order(grad_gateup.astype(low)), grad_down.astype(low))
    grad_middle = cotangent.astype(wide) + tensor_sum(middle_part, middle_low)
    grad_middle_low = grad_middle.astype(low)
    grad_middle_low, mlp_part = lax.optimization_barrier((grad_middle_low, mlp_part))
    mlp_share = tensor_share(mlp_part)
    output = (lax.dynamic_slice_in_dim(middle, tensor_start, width_share, 1) + mlp_share).astype(low)
    grad_out = jnp.einsum("tc,td->cd", heads_out, grad_middle_low, preferred_element_type=wide)
    early = lax.psum((*early, grad_out.astype(low)), "dp")
    grad_landed = exchange(grad_heads_of(grad_middle_low, w_out), ranks, 2)
    own_ids = lax.dynamic_index_in_dim(kv[:, :, rows:], rank_here, 0, False)
    back_kv, back_query, bias_tiles = backward_attention(
        runs, key_op, value_op, query_op, exact, grad_landed, own_ids
    )
    same_sum = jnp.sum(bias_tiles[0])
    other_sum = jnp.sum(bias_tiles[1])
    grad_projected, gain_tile = unproject(
        collect(back_kv, back_query), raw_query, raw_key, pair_gain(query_gain),
        pair_gain(key_gain), cosine, sine,
    )
    query_gain_part = gain_tile[0, :HD] + gain_tile[0, HD:]
    key_gain_part = gain_tile[1, :HD] + gain_tile[1, HD:]
    scale_one = lax.rsqrt(jnp.mean(inputs * inputs, axis=1, keepdims=True) + EPSILON)
    unit_one = inputs * scale_one
    grad_qkv = jnp.einsum("td,kte->kde", normed_one, grad_projected, preferred_element_type=wide)
    grad_normed_one = jnp.einsum("kte,kde->td", grad_projected, w_qkv, preferred_element_type=wide)
    attn_gain_part = jnp.sum(grad_normed_one * unit_one, axis=0)
    scaled_one = grad_normed_one * attn_gain
    input_part = scale_one * (
        scaled_one - unit_one * jnp.mean(scaled_one * unit_one, axis=1, keepdims=True)
    )
    grad_input = lax.dynamic_slice_in_dim(grad_middle, tensor_start, width_share, 1) + tensor_share(
        input_part
    )
    depth = tokens.shape[1]
    head_slot = lax.axis_index("tensor") * heads + head_here
    hit = (jnp.arange(tensor * heads, dtype=jnp.int32) == head_slot).astype(wide)
    small = jnp.concatenate(
        [attn_gain_part, mlp_gain_part, query_gain_part, key_gain_part]
        + [same_sum * hit, other_sum * hit]
    )
    length = small.shape[0]
    small = jnp.pad(small, (0, -length % (8 * LANES))).reshape(-1, LANES)
    qkv_sum, small = total_sums([grad_qkv.astype(low)], small, dp, tensor)
    small = small.reshape(-1)[:length]
    gains, biases = small[: 2 * depth + 2 * HD], small[2 * depth + 2 * HD :]
    bias_sum = lax.dynamic_slice_in_dim(
        biases.reshape(2, tensor * heads), lax.axis_index("tensor") * heads, heads, 1
    )
    return (
        output,
        grad_input,
        qkv_sum.astype(wide),
        early[2].astype(wide),
        early[0].astype(wide),
        early[1].astype(wide),
        gains[:depth],
        gains[depth : 2 * depth],
        gains[2 * depth : 2 * depth + HD],
        gains[2 * depth + HD :],
        bias_sum,
    )


def solution(mesh):
    placed = (
        P("dp", None),
        P("dp", None),
        P("dp"),
        P("dp"),
        P("dp"),
        P(None, None, "tensor"),
        P("tensor", None),
        P(None, None, "tensor"),
        P("tensor", None),
        P(),
        P(),
        P(),
        P(),
        P(None, "tensor"),
    )
    return jax.shard_map(
        shards,
        mesh=mesh,
        in_specs=placed,
        out_specs=(
            P("dp", "tensor"),
            P("dp", "tensor"),
            P(None, None, "tensor"),
            P("tensor", None),
            P(None, None, "tensor"),
            P("tensor", None),
            P(),
            P(),
            P(),
            P(),
            P(None, "tensor"),
        ),
        check_vma=False,
    )
```

```python
import functools

import jax
import jax.numpy as jnp
import numpy as np
from jax import lax
from jax.experimental import pallas as pl
from jax.experimental.layout import Layout, with_layout_constraint
from jax.experimental.pallas import tpu as pltpu
from jax.sharding import PartitionSpec as P

HD = 64
LANES = 128
IDS = 16
EPSILON = 1e-05
LOG2E = 1.4426950408889634
FAR = -30000.0
DOCS = 8
VARS = 4
VAR_AT = HD
SEG_AT = VAR_AT + 3 * VARS
ONE_AT = SEG_AT + DOCS
VMEM = 60 * 1024 * 1024
FEWEST = 512
LAGS = (0, 1, 3, 5, 7, 8)
MESH = pl.DeviceIdType.MESH
WHOLE = pl.BlockSpec(memory_space=pltpu.VMEM)
SCALARS = pl.BlockSpec(memory_space=pltpu.SMEM)
ANYWHERE = pl.BlockSpec(memory_space=pl.ANY)
wide = jnp.float32
low = jnp.bfloat16


def params(**more):
    return pltpu.CompilerParams(vmem_limit_bytes=VMEM, **more)


def lanes_of(x):
    return lax.broadcasted_iota(jnp.int32, x.shape, x.ndim - 1)


def dot_nt(a, b):
    return lax.dot_general(a, b, (((1,), (1,)), ((), ())), preferred_element_type=wide)


def dot_tn(a, b):
    return lax.dot_general(a, b, (((0,), (0,)), ((), ())), preferred_element_type=wide)


def dot_nn(a, b):
    return jnp.dot(a, b, preferred_element_type=wide)


def left_pair(a, b):
    return jnp.where(lanes_of(a) < HD, a, pltpu.roll(b, HD, 1))


def right_pair(a, b):
    return jnp.where(lanes_of(a) < HD, pltpu.roll(a, HD, 1), b)


def swap_halves(x):
    return jnp.where(
        lanes_of(x) % HD < HD // 2,
        pltpu.roll(x, LANES - HD // 2, 1),
        pltpu.roll(x, HD // 2, 1),
    )


def head_mean(x):
    row = lax.broadcasted_iota(jnp.int32, (LANES, LANES), 0) // HD
    column = lax.broadcasted_iota(jnp.int32, (LANES, LANES), 1) // HD
    mix = jnp.where(row == column, 1.0 / HD, 0.0).astype(low)
    high = x.astype(low)
    return dot_nn(high, mix) + dot_nn((x - high.astype(wide)).astype(low), mix)


def features(ids, parts, table):
    index = lax.broadcasted_iota(jnp.int32, (IDS, LANES), 0)
    columns = []
    for part in range(parts):
        segs = jnp.broadcast_to(ids[part : part + 1], (IDS, LANES)).astype(jnp.int32)
        at = IDS // 2 + part
        variates = jnp.broadcast_to(ids[at : at + 1], (IDS, LANES)).astype(jnp.int32)
        by_variate = jnp.where(variates == index, 1.0, 0.0)
        by_document = jnp.where(segs == index - VARS, 1.0, 0.0)
        columns.append(
            jnp.where(index < VARS, by_variate, jnp.where(index < VARS + DOCS, by_document, 1.0))
        )
    return dot_tn(jnp.concatenate(columns, axis=1).astype(low), table)


def table_places():
    row = lax.broadcasted_iota(jnp.int32, (IDS, LANES), 0)
    lane = lax.broadcasted_iota(jnp.int32, (IDS, LANES), 1)
    return row, lane


def hot_variates(row, lane, values):
    kept = jnp.where((lane - VAR_AT) % VARS == row, values, 0.0)
    kept = jnp.where(lane < SEG_AT, kept, 0.0)
    kept = jnp.where(lane >= VAR_AT, kept, 0.0)
    return jnp.where(row < VARS, kept, 0.0)


def of_documents(row, lane, values):
    kept = jnp.where(row >= VARS, values, 0.0)
    kept = jnp.where(row < VARS + DOCS, kept, 0.0)
    kept = jnp.where(lane >= SEG_AT, kept, 0.0)
    return jnp.where(lane < ONE_AT, kept, 0.0)


def key_table():
    row, lane = table_places()
    table = hot_variates(row, lane, 1.0)
    table = table + of_documents(row, lane, jnp.where(lane - SEG_AT == row - VARS, 0.0, FAR))
    one = jnp.where(lane >= ONE_AT, jnp.where(lane < ONE_AT + 3, 1.0, 0.0), 0.0)
    return (table + jnp.where(row == VARS + DOCS, one, 0.0)).astype(low)


def query_table(step):
    row, lane = table_places()
    step = jnp.full((IDS, LANES), step, wide)
    high = step.astype(low).astype(wide)
    mid = (step - high).astype(low).astype(wide)
    part = (lane - VAR_AT) // VARS
    step = jnp.where(part == 0, high, jnp.where(part == 1, mid, step - high - mid))
    table = hot_variates(row, lane, step)
    table = table + of_documents(row, lane, jnp.where(lane - SEG_AT == row - VARS, 1.0, 0.0))
    return table.astype(low)


def double_gains(pair_ref, query_ref, key_ref):
    for side in range(2):
        span = slice(side * HD, (side + 1) * HD)
        pair_ref[0:1, span] = query_ref[...] * (LOG2E * HD**-0.5)
        pair_ref[1:2, span] = query_ref[...]
        pair_ref[2:3, span] = key_ref[...]


def project_kernel(
    tokens_ref, w_ref, gain_ref, query_gain_ref, key_gain_ref, cosine_ref, sine_ref, segs_ref, vars_ref,
    message_ref, query_ref, key_ref, normed_ref, pair_gain_ref, ids_ref,
):
    rows = tokens_ref.shape[0]
    parts = segs_ref.shape[0]

    @pl.when(pl.program_id(0) == 0)
    def norm():
        x = tokens_ref[...].astype(wide)
        scale = lax.rsqrt(jnp.mean(x * x, axis=1, keepdims=True) + EPSILON)
        normed_ref[...] = (x * scale * gain_ref[...]).astype(low)
        double_gains(pair_gain_ref, query_gain_ref, key_gain_ref)
        ids_ref[...] = jnp.zeros_like(ids_ref)
        ids_ref[:parts, :] = segs_ref[...].astype(wide)
        ids_ref[IDS // 2 : IDS // 2 + parts, :] = vars_ref[...].astype(wide)

    normed = normed_ref[...]

    def turned(raw, gain):
        x = raw * lax.rsqrt(head_mean(raw * raw) + EPSILON) * gain
        return x * cosine_ref[...] + swap_halves(x) * sine_ref[...]

    query_ref[...] = dot_nn(normed, w_ref[0])
    key_ref[...] = dot_nn(normed, w_ref[1])
    values = dot_nn(normed, w_ref[2])
    for pair in range(query_ref.shape[1] // LANES):
        span = slice(pair * LANES, (pair + 1) * LANES)
        one, two = 2 * pair, 2 * pair + 1
        query = turned(query_ref[:, span], pair_gain_ref[0:1])
        key = turned(key_ref[:, span], pair_gain_ref[2:3])
        value = values[:, span]
        message_ref[one, :rows] = left_pair(key, value).astype(low)
        message_ref[two, :rows] = right_pair(key, value).astype(low)
        upper, lower = query[: rows // 2], query[rows // 2 :]
        message_ref[one, rows + IDS :] = left_pair(upper, lower).astype(low)
        message_ref[two, rows + IDS :] = right_pair(upper, lower).astype(low)
        message_ref[one, rows : rows + IDS] = ids_ref[...].astype(low)
        message_ref[two, rows : rows + IDS] = ids_ref[...].astype(low)


def project(tokens, w_qkv, gain, query_gain, key_gain, cosine, sine, segs, variates):
    rows, depth = tokens.shape
    width = w_qkv.shape[2]
    size = rows + IDS + rows // 2
    wider = LANES * (1 + (width // LANES + 1) % 2)
    column = pl.BlockSpec((rows, wider), lambda i: (0, i))
    return pl.pallas_call(
        project_kernel,
        grid=(width // wider,),
        in_specs=[
            WHOLE,
            pl.BlockSpec((3, depth, wider), lambda i: (0, 0, i)),
            WHOLE, WHOLE, WHOLE, WHOLE, WHOLE, WHOLE, WHOLE,
        ],
        out_specs=(
            pl.BlockSpec((wider // HD, size, LANES), lambda i: (i, 0, 0)),
            column, column,
            pl.BlockSpec((rows, depth), lambda i: (0, 0)),
        ),
        out_shape=(
            jax.ShapeDtypeStruct((width // HD, size, LANES), low),
            jax.ShapeDtypeStruct((rows, width), wide),
            jax.ShapeDtypeStruct((rows, width), wide),
            jax.ShapeDtypeStruct((rows, depth), low),
        ),
        scratch_shapes=[pltpu.VMEM((8, LANES), wide), pltpu.VMEM((IDS, LANES), wide)],
        compiler_params=params(),
    )(tokens, w_qkv, gain, query_gain, key_gain, cosine, sine, segs, variates)


def walk(begin, end, body, largest):
    count = (end - begin) // LANES
    many = largest // LANES

    def step(index, carry):
        body(begin + index * largest, largest)
        return carry

    lax.fori_loop(0, count // many, step, 0)
    size = many // 2
    while size:
        piece = size * LANES
        at = begin + (count // (2 * size)) * (2 * piece)

        @pl.when((count // size) % 2 == 1)
        def rest(at=at, piece=piece):
            body(at, piece)

        size //= 2


def scalar(x):
    return x[0, 0].astype(jnp.int32)


def forward_kernel(
    bias_ref, kv_ref, query_in_ref,
    k_ref, v_ref, q_ref, exact_ref, message_ref, runs_ref, acc_ref, seg_ref, upto_ref, keys_ref,
):
    ranks, heads = kv_ref.shape[:2]
    rows = q_ref.shape[0]
    half = rows // 2
    parts = rows // LANES
    block = pl.program_id(0)
    place = lax.axis_index("dp")
    rank = lax.rem(place, ranks)
    head = place // ranks
    filled = lax.broadcasted_iota(jnp.int32, (IDS // 2, LANES), 0) < parts

    @pl.when(block == 0)
    def prepare():
        keys = key_table()
        for rank_at in range(ranks):
            for head_at in range(heads):
                at = head_at * ranks + rank_at
                ids = kv_ref[rank_at, head_at, rows:, :].astype(wide)
                seg_ref[at] = jnp.where(filled, ids[: IDS // 2], DOCS + 1.0)
                extra = features(ids, parts, keys)
                kv = kv_ref[rank_at, head_at, :rows].astype(wide)
                lane = lanes_of(kv)
                span = pl.ds(at * rows, rows)
                k_ref[span, :] = jnp.where(lane < HD, kv, extra).astype(low)
                one = jnp.where(lane < HD + 3, 1.0, 0.0)
                v_ref[span, :] = jnp.where(lane < HD, pltpu.roll(kv, HD, 1), one).astype(low)
        every = seg_ref[...].reshape(ranks * heads * (IDS // 2), LANES)
        own = jnp.stack([seg_ref[head_at * ranks + rank] for head_at in range(heads)])
        own = own.reshape(heads * (IDS // 2), LANES)
        upto_ref[0, 0] = 0
        upto_ref[1, 0] = 0
        for document in range(DOCS):
            for which, segs in ((0, every), (1, own)):
                count = jnp.sum(jnp.where(segs <= document, 1.0, 0.0), keepdims=True)
                upto_ref[which, document + 1] = scalar(count)
        for at in range(ranks * heads):
            segs = seg_ref[at]
            first = scalar(segs[:1, :1])
            last = scalar(segs[parts - 1 : parts, LANES - 1 :])
            keys_ref[0, at] = upto_ref[0, first] // LANES * LANES
            keys_ref[1, at] = (upto_ref[0, last + 1] + LANES - 1) // LANES * LANES
            runs_ref[0, at] = upto_ref[1, first] // LANES * LANES
            runs_ref[1, at] = (upto_ref[1, last + 1] + LANES - 1) // LANES * LANES

    begin = keys_ref[0, block * ranks + rank]
    end = keys_ref[1, block * ranks + rank]
    queries = query_table((bias_ref[0, head] - bias_ref[1, head]) * LOG2E)
    ids = kv_ref[rank, block, pl.ds(rows, IDS), :].astype(wide)
    extra = features(ids, parts, queries)
    folded = query_in_ref[0].astype(wide)
    head_part = jnp.concatenate([folded, pltpu.roll(folded, HD, 1)], axis=0)
    q_ref[...] = jnp.where(lanes_of(extra) < HD, head_part, extra).astype(low)
    acc_ref[...] = jnp.zeros_like(acc_ref)

    def step(start, size):
        span = pl.ds(pl.multiple_of(start, LANES), size)
        probs = jnp.exp2(dot_nt(q_ref[...], k_ref[span, :])).astype(low)
        acc_ref[...] += dot_nn(probs, v_ref[span, :])

    walk(begin, end, step, 2048)
    total = acc_ref[...]
    row_sum = total[:, HD : HD + 1]
    exact = total / row_sum
    exact_ref[...] = jnp.where(lanes_of(total) < HD, exact, jnp.log2(row_sum))
    message_ref[0] = left_pair(exact[:half], exact[half:]).astype(low)


def forward_attention(bias, kv, query):
    ranks, heads, size = kv.shape[:3]
    rows = size - IDS
    every = ranks * heads * rows
    part = pl.BlockSpec((rows, LANES), lambda i: (i, 0))
    fold = pl.BlockSpec((1, rows // 2, LANES), lambda i: (i, 0, 0))
    return pl.pallas_call(
        forward_kernel,
        grid=(heads,),
        in_specs=[SCALARS, WHOLE, fold],
        out_specs=(WHOLE, WHOLE, part, part, fold, SCALARS),
        scratch_shapes=[
            pltpu.VMEM((rows, LANES), wide),
            pltpu.VMEM((ranks * heads, IDS // 2, LANES), wide),
            pltpu.SMEM((2, DOCS + 1), jnp.int32),
            pltpu.SMEM((2, ranks * heads), jnp.int32),
        ],
        out_shape=(
            jax.ShapeDtypeStruct((every, LANES), low),
            jax.ShapeDtypeStruct((every, LANES), low),
            jax.ShapeDtypeStruct((heads * rows, LANES), low),
            jax.ShapeDtypeStruct((heads * rows, LANES), wide),
            jax.ShapeDtypeStruct((heads, rows // 2, LANES), low),
            jax.ShapeDtypeStruct((2, ranks * heads), jnp.int32),
        ),
        compiler_params=params(),
    )(bias, kv, query)


def split_lanes(column, lane, at):
    high = column.astype(low).astype(wide)
    mid = (column - high).astype(low).astype(wide)
    parts = jnp.where(lane == at, high, jnp.where(lane == at + 1, mid, column - high - mid))
    return jnp.where(lane < at + 3, parts, 0.0)


def backward_kernel(
    runs_ref, k_ref, v_ref, q_in_ref, exact_ref, grad_in_ref, ids_ref,
    kv_ref, message_ref, bias_ref, q_ref, g_ref, kt_ref, dk_ref, dv_ref, dq_ref,
):
    heads, half = grad_in_ref.shape[:2]
    rows = 2 * half
    block = pl.program_id(0)

    @pl.when(block == 0)
    def prepare():
        dq_ref[...] = jnp.zeros_like(dq_ref)
        for head_at in range(heads):
            folded = grad_in_ref[head_at].astype(wide)
            for side in range(2):
                span = pl.ds(head_at * rows + side * half, half)
                grad = folded if side == 0 else pltpu.roll(folded, HD, 1)
                lane = lanes_of(grad)
                grad = jnp.where(lane < HD, grad, 0.0)
                exact = exact_ref[span, :]
                delta = jnp.sum(grad * exact, axis=1, keepdims=True)
                g_ref[span, :] = jnp.where(lane < HD, grad, split_lanes(-delta, lane, HD)).astype(low)
                query = q_in_ref[span, :].astype(wide)
                total = split_lanes(-exact[:, HD : HD + 1], lane, ONE_AT)
                q_ref[span, :] = jnp.where(lane < ONE_AT, query, total).astype(low)

    dk_ref[...] = jnp.zeros_like(dk_ref)
    dv_ref[...] = jnp.zeros_like(dv_ref)
    key = k_ref[...]
    value = v_ref[...]
    kt_ref[...] = key.astype(wide).T.astype(low)

    def step(start, size):
        span = pl.ds(pl.multiple_of(start, LANES), size)
        query = q_ref[span, :]
        grad = g_ref[span, :]
        probs = jnp.exp2(dot_nt(key, query))
        grad_scores = (probs * dot_nt(value, grad)).astype(low)
        dv_ref[...] += dot_nn(probs.astype(low), grad)
        dk_ref[...] += dot_nn(grad_scores, query)
        dq_ref[:, span] += dot_nn(kt_ref[...], grad_scores)

    walk(runs_ref[0, block], runs_ref[1, block], step, 2048)
    kv_ref[0, 0] = left_pair(dk_ref[...] * (1.0 / LOG2E), dv_ref[...]).astype(low)

    @pl.when(block == pl.num_programs(0) - 1)
    def finish():
        same = jnp.zeros((8, LANES), wide)
        every = jnp.zeros((8, LANES), wide)
        index = lax.broadcasted_iota(jnp.int32, (8, LANES), 0)
        for head_at in range(heads):
            ids = ids_ref[head_at].astype(wide)
            for part in range(rows // LANES):
                at = head_at * rows + part * LANES
                by_variate = jnp.where(index < VARS, dq_ref[VAR_AT : VAR_AT + 8, at : at + LANES], 0.0)
                variates = jnp.broadcast_to(
                    ids[IDS // 2 + part : IDS // 2 + part + 1], (8, LANES)
                ).astype(jnp.int32)
                same = same + jnp.where(variates == index, by_variate, 0.0)
                every = every + by_variate
            span = dq_ref[:, head_at * rows : (head_at + 1) * rows].T * HD**-0.5
            message_ref[head_at] = left_pair(span[:half], span[half:]).astype(low)
        bias_ref[0] = same
        bias_ref[1] = every - same


def backward_attention(runs, key, value, query, exact, grad, ids):
    every = key.shape[0]
    heads, half = grad.shape[:2]
    rows = 2 * half
    ranks = every // (heads * rows)
    part = pl.BlockSpec((rows, LANES), lambda i, *_: (i, 0))
    return pl.pallas_call(
        backward_kernel,
        grid_spec=pltpu.PrefetchScalarGridSpec(
            num_scalar_prefetch=1,
            grid=(ranks * heads,),
            in_specs=[part, part, WHOLE, WHOLE, WHOLE, WHOLE],
            out_specs=(
                pl.BlockSpec((1, 1, rows, LANES), lambda i, *_: (i % ranks, i // ranks, 0, 0)),
                WHOLE,
                WHOLE,
            ),
            scratch_shapes=[
                pltpu.VMEM((heads * rows, LANES), low),
                pltpu.VMEM((heads * rows, LANES), low),
                pltpu.VMEM((LANES, rows), low),
                pltpu.VMEM((rows, LANES), wide),
                pltpu.VMEM((rows, LANES), wide),
                pltpu.VMEM((LANES, heads * rows), wide),
            ],
        ),
        out_shape=(
            jax.ShapeDtypeStruct((ranks, heads, rows, LANES), low),
            jax.ShapeDtypeStruct((heads, half, LANES), low),
            jax.ShapeDtypeStruct((2, 8, LANES), wide),
        ),
        compiler_params=params(),
    )(runs, key, value, query, exact, grad, ids)


def columns_of(width):
    if width % LANES:
        return [(0, width)]
    return [(at, min(2 * LANES, width - at)) for at in range(0, width, 2 * LANES)]


def mlp_kernel(
    landed_ref, tokens_ref, cotangent_ref, gain_ref, own_out_ref, other_out_ref, gateup_ref, down_ref,
    heads_ref, middle_ref, normed_ref, hidden_ref, grad_gu_ref, part_ref, part_low_ref, gain_part_ref,
    others_ref, gateup_in, down_in, sums_ref, copied,
):
    tensor, heads, half = landed_ref.shape[:3]
    copies = [
        pltpu.make_async_copy(gateup_ref, gateup_in, copied.at[0]),
        pltpu.make_async_copy(down_ref, down_in, copied.at[1]),
    ]
    for copy in copies:
        copy.start()
    for share in range(tensor):
        to_ref = others_ref if share else heads_ref
        for pair in range(heads // 2):
            one = landed_ref[share, 2 * pair].astype(wide)
            two = landed_ref[share, 2 * pair + 1].astype(wide)
            span = pl.ds(pair * LANES, LANES)
            to_ref[:half, span] = left_pair(one, two).astype(low)
            to_ref[half:, span] = right_pair(one, two).astype(low)
        if share:
            middle_ref[...] += dot_nn(to_ref[...], other_out_ref[share - 1])
        else:
            middle_ref[...] = tokens_ref[...].astype(wide) + dot_nn(to_ref[...], own_out_ref[...])

    def unit_and_scale():
        middle = middle_ref[...]
        scale = lax.rsqrt(jnp.mean(middle * middle, axis=1, keepdims=True) + EPSILON)
        return middle * scale, scale

    normed_ref[...] = (unit_and_scale()[0] * gain_ref[...]).astype(low)
    for copy in copies:
        copy.wait()
    sums_ref[...] = jnp.zeros_like(sums_ref)
    for at, size in columns_of(hidden_ref.shape[1]):
        span = slice(at, at + size)
        w_gate = gateup_in[0, :, span]
        w_up = gateup_in[1, :, span]
        gate = dot_nn(normed_ref[...], w_gate)
        up = dot_nn(normed_ref[...], w_up)
        grad = dot_nt(cotangent_ref[...], down_in[span, :])
        sigmoid = 1.0 / (1.0 + jnp.exp(-gate))
        active = gate * sigmoid
        hidden_ref[:, span] = (active * up).astype(low)
        grad_gate = (grad * up * sigmoid * (1.0 + gate * (1.0 - sigmoid))).astype(low)
        grad_up = (grad * active).astype(low)
        grad_gu_ref[0, :, span] = grad_gate
        grad_gu_ref[1, :, span] = grad_up
        sums_ref[...] += dot_nt(grad_gate, w_gate) + dot_nt(grad_up, w_up)
    unit, scale = unit_and_scale()
    sums = sums_ref[...]
    gain_part = jnp.sum(sums * unit, axis=0, keepdims=True)
    for row in range(gain_part_ref.shape[0]):
        gain_part_ref[row : row + 1, :] = gain_part[:, row * LANES : (row + 1) * LANES]
    scaled = sums * gain_ref[...]
    part = scale * (scaled - unit * jnp.mean(scaled * unit, axis=1, keepdims=True))
    part_ref[...] = part
    part_low_ref[...] = part.astype(low)


def out_and_mlp(landed, tokens, cotangent, gain, w_out, w_others, w_gateup, w_down):
    tensor, heads, half = landed.shape[:3]
    rows, depth = tokens.shape
    width, units = heads * HD, w_down.shape[0]
    shape = jax.ShapeDtypeStruct
    return pl.pallas_call(
        mlp_kernel,
        in_specs=[WHOLE] * 6 + [ANYWHERE] * 2,
        out_specs=(WHOLE,) * 8,
        out_shape=(
            shape((rows, width), low),
            shape((rows, depth), wide),
            shape((rows, depth), low),
            shape((rows, units), low),
            shape((2, rows, units), low),
            shape((rows, depth), wide),
            shape((rows, depth), low),
            shape((depth // LANES, LANES), wide),
        ),
        scratch_shapes=[
            pltpu.VMEM((rows, width), low),
            pltpu.VMEM(w_gateup.shape, low),
            pltpu.VMEM(w_down.shape, low),
            pltpu.VMEM((rows, depth), wide),
            pltpu.SemaphoreType.DMA((2,)),
        ],
        compiler_params=params(),
    )(landed, tokens, cotangent, gain, w_out, w_others, w_gateup, w_down)


def grad_heads_kernel(grad_ref, w_ref, message_ref):
    half = message_ref.shape[1]
    for pair in range(message_ref.shape[0] // 2):
        both = dot_nt(grad_ref[...], w_ref[pair * LANES : (pair + 1) * LANES, :])
        message_ref[2 * pair] = left_pair(both[:half], both[half:]).astype(low)
        message_ref[2 * pair + 1] = right_pair(both[:half], both[half:]).astype(low)


def grad_heads_of(grad, w_out):
    return pl.pallas_call(
        grad_heads_kernel,
        in_specs=[WHOLE, WHOLE],
        out_specs=WHOLE,
        out_shape=jax.ShapeDtypeStruct((w_out.shape[0] // HD, grad.shape[0] // 2, LANES), low),
        compiler_params=params(),
    )(grad, w_out)


def tail_kernel(
    landed_ref, query_ref, key_ref, query_gain_ref, key_gain_ref, cosine_ref, sine_ref, tokens_ref, gain_ref,
    normed_ref, w_ref, mlp_gain_ref, bias_ref,
    grad_qkv_ref, input_ref, small_ref, grad_ref, pair_gain_ref, *, every_head,
):
    double_gains(pair_gain_ref, query_gain_ref, key_gain_ref)
    rows, width = query_ref.shape
    depth = tokens_ref.shape[1]

    def back(turned, raw, gain):
        grad = turned * cosine_ref[...] - swap_halves(turned) * sine_ref[...]
        scale = lax.rsqrt(head_mean(raw * raw) + EPSILON)
        unit = raw * scale
        scaled = grad * gain
        part = jnp.sum(grad * unit, axis=0, keepdims=True)
        return (scale * (scaled - unit * head_mean(scaled * unit))).astype(low), part

    query_part = jnp.zeros((1, LANES), wide)
    key_part = jnp.zeros((1, LANES), wide)
    for pair in range(width // LANES):
        span = slice(pair * LANES, (pair + 1) * LANES)
        key_one = landed_ref[2 * pair, :rows].astype(wide)
        key_two = landed_ref[2 * pair + 1, :rows].astype(wide)
        query_one = landed_ref[2 * pair, rows:].astype(wide)
        query_two = landed_ref[2 * pair + 1, rows:].astype(wide)
        query = jnp.concatenate(
            [left_pair(query_one, query_two), right_pair(query_one, query_two)], axis=0
        )
        grad_ref[0, :, span], part = back(query, query_ref[:, span], pair_gain_ref[1:2])
        query_part = query_part + part
        grad_ref[1, :, span], part = back(
            left_pair(key_one, key_two), key_ref[:, span], pair_gain_ref[2:3]
        )
        key_part = key_part + part
        grad_ref[2, :, span] = right_pair(key_one, key_two).astype(low)
    sums = dot_nt(grad_ref[0], w_ref[0]) + dot_nt(grad_ref[1], w_ref[1])
    sums = sums + dot_nt(grad_ref[2], w_ref[2])
    x = tokens_ref[...].astype(wide)
    scale = lax.rsqrt(jnp.mean(x * x, axis=1, keepdims=True) + EPSILON)
    unit = x * scale
    gain_part = jnp.sum(sums * unit, axis=0, keepdims=True)
    scaled = sums * gain_ref[...]
    part = scale * (scaled - unit * jnp.mean(scaled * unit, axis=1, keepdims=True))
    input_ref[...] = part.astype(low)
    for index in range(3):
        grad_qkv_ref[index] = dot_nn(normed_ref[...], grad_ref[index]).astype(low)
    count = depth // LANES
    small_ref[...] = jnp.zeros_like(small_ref)
    for row in range(count):
        small_ref[row : row + 1, :] = gain_part[:, row * LANES : (row + 1) * LANES]
    small_ref[count : 2 * count, :] = mlp_gain_ref[...]
    small_ref[2 * count : 2 * count + 1, :] = query_part
    small_ref[2 * count + 1 : 2 * count + 2, :] = key_part
    head = lax.axis_index("tensor") * (width // HD) + lax.axis_index("dp") // every_head
    lane = lax.broadcasted_iota(jnp.int32, (1, LANES), 1)
    for row in range(2):
        total = jnp.sum(bias_ref[row], keepdims=True)
        at = 2 * count + 2 + row
        small_ref[at : at + 1, :] = jnp.where(lane == head, total, 0.0)


def tail(
    landed, raw_query, raw_key, query_gain, key_gain, cosine, sine, tokens, gain, normed_turned,
    w_qkv, mlp_gain_part, bias_tiles, ranks,
):
    rows, width = raw_query.shape
    depth = tokens.shape[1]
    small = -(-(2 * depth // LANES + 4) // 8) * 8
    return pl.pallas_call(
        functools.partial(tail_kernel, every_head=ranks),
        in_specs=[WHOLE] * 13,
        out_specs=(WHOLE,) * 3,
        out_shape=(
            jax.ShapeDtypeStruct((3, depth, width), low),
            jax.ShapeDtypeStruct((rows, depth), low),
            jax.ShapeDtypeStruct((small, LANES), wide),
        ),
        scratch_shapes=[pltpu.VMEM((3, rows, width), low), pltpu.VMEM((8, LANES), wide)],
        compiler_params=params(),
    )(
        landed, raw_query, raw_key, query_gain, key_gain, cosine, sine, tokens, gain, normed_turned,
        w_qkv, mlp_gain_part, bias_tiles,
    )


def widen_kernel(*refs):
    half = len(refs) // 2
    for source, target in zip(refs[:half], refs[half:]):
        target[...] = source[...].astype(wide)


def widen(arrays):
    steps = 8
    while any(a.shape[0] % (16 * steps) for a in arrays):
        steps //= 2
    specs = [pl.BlockSpec((a.shape[0] // steps, a.shape[1]), lambda i: (i, 0)) for a in arrays]
    return pl.pallas_call(
        widen_kernel,
        grid=(steps,),
        in_specs=specs,
        out_specs=tuple(specs),
        out_shape=tuple(jax.ShapeDtypeStruct(a.shape, wide) for a in arrays),
        compiler_params=params(),
    )(*arrays)


def remote(src, dst, send, recv, place):
    return pltpu.make_async_remote_copy(
        src_ref=src, dst_ref=dst, send_sem=send, recv_sem=recv,
        device_id={"dp": place}, device_id_type=MESH,
    )


def greet(heads, ranks, head, rank, with_ranks, tensor=1):
    barrier = pltpu.get_barrier_semaphore()
    for step in range(1, tensor):
        side = lax.rem(lax.axis_index("tensor") + step, tensor)
        pl.semaphore_signal(barrier, inc=1, device_id={"tensor": side}, device_id_type=MESH)
    for step in range(1, heads):
        place = lax.rem(head + step, heads) * ranks + rank
        pl.semaphore_signal(barrier, inc=1, device_id={"dp": place}, device_id_type=MESH)
    if with_ranks:
        for step in range(1, ranks):
            place = head * ranks + lax.rem(rank + step, ranks)
            pl.semaphore_signal(barrier, inc=1, device_id={"dp": place}, device_id_type=MESH)
    pl.semaphore_wait(barrier, heads + tensor - 2 + (ranks - 1 if with_ranks else 0))


def spread_kernel(
    message_ref, w_ref, kv_ref, query_ref, others_ref,
    send_a, recv_a, send_b, recv_b, send_f, recv_f, send_w, recv_w, local, *, ranks
):
    heads = message_ref.shape[0]
    tensor = others_ref.shape[0] + 1
    side = lax.axis_index("tensor")
    size = kv_ref.shape[2]
    rest = query_ref.shape[1]
    place = lax.axis_index("dp")
    head = place // ranks
    rank = lax.rem(place, ranks)
    greet(heads, ranks, head, rank, True, tensor)
    onward = []
    for step in range(1, tensor):
        copy = pltpu.make_async_remote_copy(
            src_ref=w_ref, dst_ref=others_ref.at[tensor - step - 1],
            send_sem=send_w.at[step], recv_sem=recv_w.at[step],
            device_id={"tensor": lax.rem(side + step, tensor)}, device_id_type=MESH,
        )
        copy.start()
        onward.append(copy)
    firsts = []
    for step in range(1, heads):
        to = lax.rem(head + step, heads)
        at = to * ranks + rank
        first = remote(
            message_ref.at[to, pl.ds(0, size)], kv_ref.at[rank, head],
            send_a.at[step], recv_a.at[step], at,
        )
        second = remote(
            message_ref.at[to, pl.ds(size, rest)], query_ref.at[head],
            send_b.at[step], recv_b.at[step], at,
        )
        first.start()
        second.start()
        firsts.append((first, second))
    mine = [
        pltpu.make_async_copy(message_ref.at[head, pl.ds(0, size)], kv_ref.at[rank, head], local.at[0]),
        pltpu.make_async_copy(message_ref.at[head, pl.ds(size, rest)], query_ref.at[head], local.at[1]),
    ]
    for copy in mine:
        copy.start()

    def forward(step, source, src):
        for other in range(1, ranks):
            copy = remote(
                src, kv_ref.at[rank, source], send_f.at[step, other], recv_f.at[step, other],
                head * ranks + lax.rem(rank + other, ranks),
            )
            copy.start()
            onward.append(copy)

    forward(0, head, message_ref.at[head, pl.ds(0, size)])
    for step in range(1, heads):
        source = lax.rem(head + heads - step, heads)
        firsts[step - 1][0].wait_recv()
        forward(step, source, kv_ref.at[rank, source])
    for first, second in firsts:
        first.wait_send()
        second.wait()
    for copy in mine + onward:
        copy.wait()


def spread(message, w_out, ranks, rows, tensor):
    heads, size = message.shape[:2]
    dma = pltpu.SemaphoreType.DMA
    return pl.pallas_call(
        functools.partial(spread_kernel, ranks=ranks),
        in_specs=[ANYWHERE] * 2,
        out_specs=(ANYWHERE,) * 3,
        out_shape=(
            jax.ShapeDtypeStruct((ranks, heads, rows + IDS, LANES), low),
            jax.ShapeDtypeStruct((heads, rows // 2, LANES), low),
            jax.ShapeDtypeStruct((tensor - 1,) + w_out.shape, low),
        ),
        scratch_shapes=[dma((heads,))] * 4 + [dma((heads, ranks))] * 2 + [dma((tensor,))] * 2 + [dma((2,))],
        compiler_params=params(collective_id=0, has_side_effects=True),
    )(message, w_out)


def send_shares(part_ref, shares_ref, send, recv):
    tensor, _, share = shares_ref.shape
    tensor += 1
    side = lax.axis_index("tensor")
    copies = []
    for step in range(1, tensor):
        to = lax.rem(side + step, tensor)
        copies.append(
            pltpu.make_async_remote_copy(
                src_ref=part_ref.at[:, pl.ds(pl.multiple_of(to * share, LANES), share)],
                dst_ref=shares_ref.at[tensor - step - 1],
                send_sem=send.at[step], recv_sem=recv.at[step],
                device_id={"tensor": to}, device_id_type=MESH,
            )
        )
        copies[-1].start()
    return copies


def exchange_kernel(
    message_ref, part_ref, landed_ref, shares_ref, send, recv, send_t, recv_t, local, *, ranks
):
    heads = message_ref.shape[0]
    place = lax.axis_index("dp")
    head = place // ranks
    rank = lax.rem(place, ranks)
    greet(heads, ranks, head, rank, False, shares_ref.shape[0] + 1)
    copies = []
    for step in range(1, heads):
        to = lax.rem(head + step, heads)
        copies.append(
            remote(
                message_ref.at[to], landed_ref.at[head], send.at[step], recv.at[step],
                to * ranks + rank,
            )
        )
        copies[-1].start()
    copies.append(pltpu.make_async_copy(message_ref.at[head], landed_ref.at[head], local))
    copies[-1].start()
    copies += send_shares(part_ref, shares_ref, send_t, recv_t)
    for copy in copies:
        copy.wait()


def exchange(message, part, ranks, tensor):
    heads = message.shape[0]
    rows, depth = part.shape
    dma = pltpu.SemaphoreType.DMA
    return pl.pallas_call(
        functools.partial(exchange_kernel, ranks=ranks),
        in_specs=[ANYWHERE] * 2,
        out_specs=(ANYWHERE,) * 2,
        out_shape=(
            jax.ShapeDtypeStruct(message.shape, message.dtype),
            jax.ShapeDtypeStruct((tensor - 1, rows, depth // tensor), low),
        ),
        scratch_shapes=[dma((heads,))] * 2 + [dma((tensor,))] * 2 + [dma],
        compiler_params=params(collective_id=2, has_side_effects=True),
    )(message, part)


def share_out_kernel(message_ref, landed_ref, send, recv, send_t, recv_t, local, *, ranks, tensor):
    heads = message_ref.shape[0]
    place = lax.axis_index("dp")
    side = lax.axis_index("tensor")
    head = place // ranks
    rank = lax.rem(place, ranks)
    barrier = pltpu.get_barrier_semaphore()
    for step in range(1, tensor):
        to = lax.rem(side + step, tensor)
        pl.semaphore_signal(barrier, inc=1, device_id={"tensor": to}, device_id_type=MESH)
    for step in range(1, heads):
        to = lax.rem(head + step, heads) * ranks + rank
        pl.semaphore_signal(barrier, inc=1, device_id={"dp": to}, device_id_type=MESH)
    pl.semaphore_wait(barrier, heads + tensor - 2)
    copies = []
    for step in range(1, heads):
        to = lax.rem(head + step, heads)
        copies.append(
            remote(
                message_ref.at[to], landed_ref.at[0, head], send.at[step], recv.at[step],
                to * ranks + rank,
            )
        )
        copies[-1].start()
    mine = pltpu.make_async_copy(message_ref.at[head], landed_ref.at[0, head], local)
    mine.start()
    onward = []

    def relay(step, source, src):
        for other in range(1, tensor):
            copy = pltpu.make_async_remote_copy(
                src_ref=src, dst_ref=landed_ref.at[tensor - other, source],
                send_sem=send_t.at[step, other], recv_sem=recv_t.at[step, other],
                device_id={"tensor": lax.rem(side + other, tensor)}, device_id_type=MESH,
            )
            copy.start()
            onward.append(copy)

    relay(0, head, message_ref.at[head])
    for step in range(1, heads):
        source = lax.rem(head + heads - step, heads)
        copies[step - 1].wait_recv()
        relay(step, source, landed_ref.at[0, source])
    for copy in copies:
        copy.wait_send()
    mine.wait()
    for copy in onward:
        copy.wait()


def share_out(message, ranks, tensor):
    heads = message.shape[0]
    dma = pltpu.SemaphoreType.DMA
    return pl.pallas_call(
        functools.partial(share_out_kernel, ranks=ranks, tensor=tensor),
        in_specs=[ANYWHERE],
        out_specs=ANYWHERE,
        out_shape=jax.ShapeDtypeStruct((tensor,) + message.shape, message.dtype),
        scratch_shapes=[dma((heads,))] * 2 + [dma((heads, tensor))] * 2 + [dma],
        compiler_params=params(collective_id=1, has_side_effects=True),
    )(message)


def total_kernel(*refs, arrays, chunks, zs, tensor):
    ins, part_ref, refs = refs[: arrays + 1], refs[arrays + 1], refs[arrays + 2 :]
    outs, shares_ref, refs = refs[: arrays + 1], refs[arrays + 1], refs[arrays + 2 :]
    count = len(chunks)
    scratch, refs = refs[: 5 * count], refs[5 * count :]
    near_ref, far_ref, line_ref, side_ref, send, recv, send_z, recv_z, send_s, recv_s, send_t, recv_t = refs
    place = lax.axis_index("dp")
    side = lax.axis_index("tensor")
    core = lax.rem(place, 2)
    x = lax.rem(place // 2, 2)
    z = place // 4
    base = place - core
    core_mate = base + 1 - core
    x_mate = z * 4 + (1 - x) * 2 + core
    z_mates = [lax.rem(z + step, zs) * 4 + x * 2 + core for step in range(1, zs)]

    barrier = pltpu.get_barrier_semaphore()
    for to in [core_mate, x_mate] + z_mates:
        pl.semaphore_signal(barrier, inc=1, device_id={"dp": to}, device_id_type=MESH)
    for step in range(1, tensor):
        to = lax.rem(side + step, tensor)
        pl.semaphore_signal(barrier, inc=1, device_id={"tensor": to}, device_id_type=MESH)
    pl.semaphore_wait(barrier, zs + tensor)
    shares = send_shares(part_ref, shares_ref, send_t, recv_t)
    sent = []
    waits = {}

    def rows_at(at, size):
        return pl.ds(pl.multiple_of(at, 16), size)

    def pieces(chunk):
        index, lead, begin, size = chunks[chunk]
        source = ins[index] if lead is None else ins[index].at[lead]
        target = outs[index] if lead is None else outs[index].at[lead]
        source, target = (ref.at[pl.ds(begin, size)] for ref in (source, target))
        return source, target, size, scratch[5 * chunk : 5 * chunk + 5]

    def go(copy, key):
        copy.start()
        sent.append(copy)
        waits.setdefault(key, []).append(copy)

    def arrived(key):
        for copy in waits[key]:
            copy.wait_recv()

    def halve_core(chunk):
        source, _, size, (first, _, _, _, _) = pieces(chunk)
        go(
            remote(
                source.at[rows_at((1 - core) * (size // 2), size // 2)], first,
                send.at[chunk, 0], recv.at[chunk, 0], core_mate,
            ),
            (chunk, 0),
        )

    def halve_x(chunk):
        source, _, size, (first, half, second, _, _) = pieces(chunk)
        arrived((chunk, 0))
        mine = source[rows_at(core * (size // 2), size // 2), :].astype(wide)
        half[...] = (mine + first[...].astype(wide)).astype(low)
        go(
            remote(
                half.at[rows_at((1 - x) * (size // 4), size // 4)], second,
                send.at[chunk, 1], recv.at[chunk, 1], x_mate,
            ),
            (chunk, 1),
        )

    def part_z(chunk):
        _, _, size, (_, half, second, quarter, third) = pieces(chunk)
        arrived((chunk, 1))
        mine = half[rows_at(x * (size // 4), size // 4), :].astype(wide)
        quarter[...] = (mine + second[...].astype(wide)).astype(low)
        part = size // (4 * zs)
        for step in range(1, zs):
            to = lax.rem(z + step, zs)
            go(
                remote(
                    quarter.at[rows_at(to * part, part)], third.at[step],
                    send_z.at[chunk, 0, step], recv_z.at[chunk, 0, step], z_mates[step - 1],
                ),
                (chunk, 2),
            )

    def spread_z(chunk):
        _, target, size, (_, _, _, quarter, third) = pieces(chunk)
        arrived((chunk, 2))
        part = size // (4 * zs)
        total = quarter[rows_at(z * part, part), :].astype(wide)
        for step in range(1, zs):
            total = total + third[step].astype(wide)
        span = rows_at(core * (size // 2) + x * (size // 4) + z * part, part)
        target[span, :] = total.astype(low)
        for step in range(1, zs):
            go(
                remote(
                    target.at[span], target.at[span],
                    send_z.at[chunk, 1, step], recv_z.at[chunk, 1, step], z_mates[step - 1],
                ),
                (chunk, 3),
            )

    def spread_x(chunk):
        _, target, size, _ = pieces(chunk)
        arrived((chunk, 3))
        span = rows_at(core * (size // 2) + x * (size // 4), size // 4)
        go(
            remote(target.at[span], target.at[span], send.at[chunk, 2], recv.at[chunk, 2], x_mate),
            (chunk, 4),
        )

    def spread_core(chunk):
        _, target, size, _ = pieces(chunk)
        arrived((chunk, 4))
        span = rows_at(core * (size // 2), size // 2)
        go(
            remote(target.at[span], target.at[span], send.at[chunk, 3], recv.at[chunk, 3], core_mate),
            (chunk, 5),
        )

    small = ins[arrays]

    def small_core():
        near_ref[0] = small[...]
        go(remote(near_ref.at[0], near_ref.at[1], send_s.at[0, 0], recv_s.at[0, 0], core_mate), "c")

    def small_x():
        arrived("c")
        far_ref[0] = near_ref[0] + near_ref[1]
        go(remote(far_ref.at[0], far_ref.at[1], send_s.at[1, 0], recv_s.at[1, 0], x_mate), "x")

    def small_z():
        arrived("x")
        line_ref[z] = far_ref[0] + far_ref[1]
        for step in range(1, zs):
            go(
                remote(
                    line_ref.at[z], line_ref.at[z], send_s.at[2, step], recv_s.at[2, step],
                    z_mates[step - 1],
                ),
                "z",
            )

    def small_side():
        arrived("z")
        total = line_ref[0]
        for at in range(1, zs):
            total = total + line_ref[at]
        side_ref[side] = total
        for step in range(1, tensor):
            copy = pltpu.make_async_remote_copy(
                src_ref=side_ref.at[side], dst_ref=side_ref.at[side],
                send_sem=send_s.at[3, step], recv_sem=recv_s.at[3, step],
                device_id={"tensor": lax.rem(side + step, tensor)}, device_id_type=MESH,
            )
            go(copy, "s")

    def small_end():
        if tensor > 1:
            arrived("s")
        total = side_ref[0]
        for at in range(1, tensor):
            total = total + side_ref[at]
        outs[arrays][...] = total

    stages = [halve_core, halve_x, part_z, spread_z, spread_x, spread_core]
    smalls = [small_core, small_x, small_z, small_side, small_end]
    for tick in range(max(count + LAGS[-1], len(smalls))):
        for stage in range(len(stages)):
            if 0 <= tick - LAGS[stage] < count:
                stages[stage](tick - LAGS[stage])
        if tick < len(smalls):
            smalls[tick]()
    for chunk in range(count):
        arrived((chunk, 5))
    for copy in sent:
        copy.wait_send()
    for copy in shares:
        copy.wait()


def total_sums(arrays, small, part, dp, tensor):
    zs = dp // 4
    chunks = []
    scratch = []
    for index, array in enumerate(arrays):
        leads = [None] if array.ndim == 2 else list(range(array.shape[0]))
        size, width = array.shape[-2:]
        total, size = size, min(size, max(64 * zs, FEWEST))
        for lead, begin in [(a, b) for a in leads for b in range(0, total, size)]:
            chunks.append((index, lead, begin, size))
            scratch += [
                pltpu.VMEM((size // 2, width), low),
                pltpu.VMEM((size // 2, width), low),
                pltpu.VMEM((size // 4, width), low),
                pltpu.VMEM((size // 4, width), low),
                pltpu.VMEM((zs, size // (4 * zs), width), low),
            ]
    dma = pltpu.SemaphoreType.DMA
    count = len(chunks)
    return pl.pallas_call(
        functools.partial(
            total_kernel, arrays=len(arrays), chunks=tuple(chunks), zs=zs, tensor=tensor
        ),
        in_specs=[WHOLE] * (len(arrays) + 1) + [ANYWHERE],
        out_specs=(WHOLE,) * (len(arrays) + 1) + (ANYWHERE,),
        out_shape=tuple(jax.ShapeDtypeStruct(a.shape, a.dtype) for a in [*arrays, small])
        + (jax.ShapeDtypeStruct((tensor - 1, part.shape[0], part.shape[1] // tensor), low),),
        scratch_shapes=scratch
        + [
            pltpu.VMEM((2,) + small.shape, wide),
            pltpu.VMEM((2,) + small.shape, wide),
            pltpu.VMEM((zs,) + small.shape, wide),
            pltpu.VMEM((tensor,) + small.shape, wide),
        ]
        + [dma((count, 4))] * 2
        + [dma((count, 2, zs))] * 2
        + [dma((4, max(zs, tensor)))] * 2
        + [dma((tensor,))] * 2,
        compiler_params=params(collective_id=4, has_side_effects=True),
    )(*arrays, small, part)


def collect_kernel(
    kv_ref, query_ref, landed_ref, piece_ref, sum_ref,
    send_p, recv_p, send_a, recv_a, send_b, recv_b, local, *, ranks,
):
    heads, rows = kv_ref.shape[1:3]
    half = query_ref.shape[1]
    place = lax.axis_index("dp")
    head = place // ranks
    rank = lax.rem(place, ranks)
    greet(heads, ranks, head, rank, True)
    order = list(range(1, heads)) + [0]
    pieces = {}
    copies = []
    for step in order:
        to = lax.rem(head + step, heads)
        for other in range(1, ranks):
            partner = lax.rem(rank + other, ranks)
            pieces[step, other] = remote(
                kv_ref.at[partner, to], piece_ref.at[other, to],
                send_p.at[step, other], recv_p.at[step, other], head * ranks + partner,
            )
            pieces[step, other].start()
        if step:
            copies.append(
                remote(
                    query_ref.at[to], landed_ref.at[head, pl.ds(rows, half)],
                    send_b.at[step], recv_b.at[step], to * ranks + rank,
                )
            )
        else:
            copies.append(
                pltpu.make_async_copy(
                    query_ref.at[head], landed_ref.at[head, pl.ds(rows, half)], local.at[0]
                )
            )
        copies[-1].start()
    for step in order:
        to = lax.rem(head + step, heads)
        total = kv_ref[rank, to].astype(wide)
        for other in range(1, ranks):
            pieces[step, other].wait_recv()
            total = total + piece_ref[other, to].astype(wide)
        sum_ref[to] = total.astype(low)
        if step:
            copies.append(
                remote(
                    sum_ref.at[to], landed_ref.at[head, pl.ds(0, rows)],
                    send_a.at[step], recv_a.at[step], to * ranks + rank,
                )
            )
        else:
            copies.append(
                pltpu.make_async_copy(
                    sum_ref.at[head], landed_ref.at[head, pl.ds(0, rows)], local.at[1]
                )
            )
        copies[-1].start()
    for piece in pieces.values():
        piece.wait_send()
    for copy in copies:
        copy.wait()


def collect(kv, query):
    ranks, heads, rows = kv.shape[:3]
    dma = pltpu.SemaphoreType.DMA
    return pl.pallas_call(
        functools.partial(collect_kernel, ranks=ranks),
        in_specs=[WHOLE, WHOLE],
        out_specs=ANYWHERE,
        out_shape=jax.ShapeDtypeStruct((heads, rows + rows // 2, LANES), low),
        scratch_shapes=[
            pltpu.VMEM((ranks, heads, rows, LANES), low),
            pltpu.VMEM((heads, rows, LANES), low),
        ]
        + [dma((heads, ranks))] * 2
        + [dma((heads,))] * 4
        + [dma((2,))],
        compiler_params=params(collective_id=3, has_side_effects=True),
    )(kv, query)


def tables(times):
    half = HD // 2
    lane = np.arange(LANES)
    inverse = (10000.0 ** (-2.0 * (lane % half) / HD)).astype(np.float32)
    sign = np.where(lane % HD < half, -1.0, 1.0).astype(np.float32)
    angles = times.astype(wide)[:, None] * inverse[None, :]
    return jnp.cos(angles), jnp.sin(angles) * sign[None, :]


def keep_order(x):
    return with_layout_constraint(x, Layout(major_to_minor=tuple(range(x.ndim))))


def id_rows(x):
    rows = x.reshape(-1, LANES).astype(low)
    return jnp.pad(rows, ((0, IDS // 2 - rows.shape[0]), (0, 0)))


def shards(
    tokens,
    cotangent,
    segment,
    variate,
    time,
    w_qkv,
    w_out,
    w_gateup,
    w_down,
    attn_gain,
    mlp_gain,
    query_gain,
    key_gain,
    var_bias,
):
    rows = tokens.shape[0]
    local_width = w_qkv.shape[2]
    heads = local_width // HD
    dp = lax.axis_size("dp")
    tensor = lax.axis_size("tensor")
    ranks = dp // heads
    place = lax.axis_index("dp")
    rank_here = lax.rem(place, ranks)
    width_share = tokens.shape[1] // tensor
    tensor_start = lax.axis_index("tensor") * width_share

    def tensor_sum(x, x_low):
        if tensor == 2:
            return x + lax.ppermute(x_low, "tensor", [(0, 1), (1, 0)]).astype(wide)
        return lax.psum(x_low, "tensor").astype(wide)

    def share_of(x):
        return lax.dynamic_slice_in_dim(x, tensor_start, width_share, 1).astype(wide)

    def share_sum(x, others):
        return share_of(x) + jnp.sum(others.astype(wide), axis=0)

    depth = tokens.shape[1]
    cosine, sine = tables(time)
    message, raw_query, raw_key, normed_one = project(
        tokens, w_qkv, attn_gain[None, :], query_gain[None, :], key_gain[None, :], cosine, sine,
        segment.reshape(-1, LANES), variate.reshape(-1, LANES),
    )
    kv, query_in, w_others = spread(message, w_out, ranks, rows, tensor)
    key_op, value_op, query_op, exact, out_message, runs = forward_attention(var_bias, kv, query_in)
    landed = share_out(out_message, ranks, tensor)
    heads_out, middle, normed_two, hidden, grad_gu, middle_part, middle_low, mlp_gain_part = out_and_mlp(
        landed, tokens, cotangent, mlp_gain[None, :], w_out, w_others, w_gateup, w_down
    )
    grad_down = jnp.einsum("tf,te->fe", hidden, cotangent, preferred_element_type=wide)
    grad_gateup = jnp.einsum("td,ktf->kdf", normed_two, grad_gu, preferred_element_type=wide)
    early = (keep_order(grad_gateup.astype(low)), grad_down.astype(low))
    mlp_part = jnp.dot(hidden, w_down, preferred_element_type=wide).astype(low)
    normed_turned = normed_one.T
    grad_middle = cotangent.astype(wide) + tensor_sum(middle_part, middle_low)
    grad_middle_low = grad_middle.astype(low)
    grad_middle_low, mlp_part, normed_turned = lax.optimization_barrier(
        (grad_middle_low, mlp_part, normed_turned)
    )
    grad_out = jnp.einsum("tc,td->cd", heads_out, grad_middle_low, preferred_element_type=wide)
    early = lax.psum((*early, grad_out.astype(low)), "dp")
    out_sum = early[2]
    grad_landed, mlp_others = exchange(
        grad_heads_of(grad_middle_low, w_out), mlp_part, ranks, tensor
    )
    output = (share_of(middle) + share_sum(mlp_part, mlp_others)).astype(low)
    own_ids = lax.dynamic_index_in_dim(kv[:, :, rows:], rank_here, 0, False)
    back_kv, back_query, bias_tiles = backward_attention(
        runs, key_op, value_op, query_op, exact, grad_landed, own_ids
    )
    grad_qkv, input_part, small = tail(
        collect(back_kv, back_query), raw_query, raw_key, query_gain[None, :], key_gain[None, :],
        cosine, sine, tokens, attn_gain[None, :], normed_turned, w_qkv, mlp_gain_part, bias_tiles, ranks,
    )
    qkv_sum, small, input_others = total_sums([grad_qkv], small, input_part, dp, tensor)
    grad_input = share_of(grad_middle) + share_sum(input_part, input_others)
    flat = lambda x: x.reshape(-1, x.shape[-1])
    qkv_wide, out_wide, gateup_wide, down_wide = widen(
        [flat(qkv_sum), out_sum, flat(early[0]), early[1]]
    )
    count = 2 * depth // LANES
    gains = small[:count].reshape(2, depth)
    head_gains = small[count : count + 2, :HD] + small[count : count + 2, HD:]
    bias_sum = lax.dynamic_slice_in_dim(
        small[count + 2 : count + 4], lax.axis_index("tensor") * heads, heads, 1
    )
    return (
        output,
        grad_input,
        qkv_wide.reshape(w_qkv.shape),
        out_wide,
        gateup_wide.reshape(w_gateup.shape),
        down_wide,
        gains[0],
        gains[1],
        head_gains[0],
        head_gains[1],
        bias_sum,
    )


def solution(mesh):
    placed = (
        P("dp", None),
        P("dp", None),
        P("dp"),
        P("dp"),
        P("dp"),
        P(None, None, "tensor"),
        P("tensor", None),
        P(None, None, "tensor"),
        P("tensor", None),
        P(),
        P(),
        P(),
        P(),
        P(None, "tensor"),
    )
    return jax.shard_map(
        shards,
        mesh=mesh,
        in_specs=placed,
        out_specs=(
            P("dp", "tensor"),
            P("dp", "tensor"),
            P(None, None, "tensor"),
            P("tensor", None),
            P(None, None, "tensor"),
            P("tensor", None),
            P(),
            P(),
            P(),
            P(),
            P(None, "tensor"),
        ),
        check_vma=False,
    )
```

```python
import functools

import jax
import jax.numpy as jnp
import numpy as np
from jax import lax
from jax.experimental import pallas as pl
from jax.experimental.layout import Layout, with_layout_constraint
from jax.experimental.pallas import tpu as pltpu
from jax.sharding import PartitionSpec as P

HD = 64
LANES = 128
IDS = 16
EPSILON = 1e-05
LOG2E = 1.4426950408889634
FAR = -30000.0
DOCS = 8
VARS = 4
VAR_AT = HD
SEG_AT = VAR_AT + 3 * VARS
ONE_AT = SEG_AT + DOCS
VMEM = 60 * 1024 * 1024
FEWEST = 512
LAGS = (0, 1, 3, 5, 7, 8)
MESH = pl.DeviceIdType.MESH
WHOLE = pl.BlockSpec(memory_space=pltpu.VMEM)
SCALARS = pl.BlockSpec(memory_space=pltpu.SMEM)
ANYWHERE = pl.BlockSpec(memory_space=pl.ANY)
wide = jnp.float32
low = jnp.bfloat16


def params(**more):
    return pltpu.CompilerParams(vmem_limit_bytes=VMEM, **more)


def lanes_of(x):
    return lax.broadcasted_iota(jnp.int32, x.shape, x.ndim - 1)


def dot_nt(a, b):
    return lax.dot_general(a, b, (((1,), (1,)), ((), ())), preferred_element_type=wide)


def dot_tn(a, b):
    return lax.dot_general(a, b, (((0,), (0,)), ((), ())), preferred_element_type=wide)


def dot_nn(a, b):
    return jnp.dot(a, b, preferred_element_type=wide)


def left_pair(a, b):
    return jnp.where(lanes_of(a) < HD, a, pltpu.roll(b, HD, 1))


def right_pair(a, b):
    return jnp.where(lanes_of(a) < HD, pltpu.roll(a, HD, 1), b)


def swap_halves(x):
    return jnp.where(
        lanes_of(x) % HD < HD // 2,
        pltpu.roll(x, LANES - HD // 2, 1),
        pltpu.roll(x, HD // 2, 1),
    )


def head_mean(x):
    row = lax.broadcasted_iota(jnp.int32, (LANES, LANES), 0) // HD
    column = lax.broadcasted_iota(jnp.int32, (LANES, LANES), 1) // HD
    mix = jnp.where(row == column, 1.0 / HD, 0.0).astype(low)
    high = x.astype(low)
    return dot_nn(high, mix) + dot_nn((x - high.astype(wide)).astype(low), mix)


def features(ids, parts, table):
    index = lax.broadcasted_iota(jnp.int32, (IDS, LANES), 0)
    columns = []
    for part in range(parts):
        segs = jnp.broadcast_to(ids[part : part + 1], (IDS, LANES)).astype(jnp.int32)
        at = IDS // 2 + part
        variates = jnp.broadcast_to(ids[at : at + 1], (IDS, LANES)).astype(jnp.int32)
        by_variate = jnp.where(variates == index, 1.0, 0.0)
        by_document = jnp.where(segs == index - VARS, 1.0, 0.0)
        columns.append(
            jnp.where(index < VARS, by_variate, jnp.where(index < VARS + DOCS, by_document, 1.0))
        )
    return dot_tn(jnp.concatenate(columns, axis=1).astype(low), table)


def table_places():
    row = lax.broadcasted_iota(jnp.int32, (IDS, LANES), 0)
    lane = lax.broadcasted_iota(jnp.int32, (IDS, LANES), 1)
    return row, lane


def hot_variates(row, lane, values):
    kept = jnp.where((lane - VAR_AT) % VARS == row, values, 0.0)
    kept = jnp.where(lane < SEG_AT, kept, 0.0)
    kept = jnp.where(lane >= VAR_AT, kept, 0.0)
    return jnp.where(row < VARS, kept, 0.0)


def of_documents(row, lane, values):
    kept = jnp.where(row >= VARS, values, 0.0)
    kept = jnp.where(row < VARS + DOCS, kept, 0.0)
    kept = jnp.where(lane >= SEG_AT, kept, 0.0)
    return jnp.where(lane < ONE_AT, kept, 0.0)


def key_table():
    row, lane = table_places()
    table = hot_variates(row, lane, 1.0)
    table = table + of_documents(row, lane, jnp.where(lane - SEG_AT == row - VARS, 0.0, FAR))
    one = jnp.where(lane >= ONE_AT, jnp.where(lane < ONE_AT + 3, 1.0, 0.0), 0.0)
    return (table + jnp.where(row == VARS + DOCS, one, 0.0)).astype(low)


def query_table(step):
    row, lane = table_places()
    step = jnp.full((IDS, LANES), step, wide)
    high = step.astype(low).astype(wide)
    mid = (step - high).astype(low).astype(wide)
    part = (lane - VAR_AT) // VARS
    step = jnp.where(part == 0, high, jnp.where(part == 1, mid, step - high - mid))
    table = hot_variates(row, lane, step)
    table = table + of_documents(row, lane, jnp.where(lane - SEG_AT == row - VARS, 1.0, 0.0))
    return table.astype(low)


def double_gains(pair_ref, query_ref, key_ref):
    for side in range(2):
        span = slice(side * HD, (side + 1) * HD)
        pair_ref[0:1, span] = query_ref[...] * (LOG2E * HD**-0.5)
        pair_ref[1:2, span] = query_ref[...]
        pair_ref[2:3, span] = key_ref[...]


def project_kernel(
    tokens_ref, w_ref, gain_ref, query_gain_ref, key_gain_ref, cosine_ref, sine_ref, segs_ref, vars_ref,
    message_ref, query_ref, key_ref, normed_ref, pair_gain_ref, ids_ref,
):
    rows = tokens_ref.shape[0]
    parts = segs_ref.shape[0]

    @pl.when(pl.program_id(0) == 0)
    def norm():
        x = tokens_ref[...].astype(wide)
        scale = lax.rsqrt(jnp.mean(x * x, axis=1, keepdims=True) + EPSILON)
        normed_ref[...] = (x * scale * gain_ref[...]).astype(low)
        double_gains(pair_gain_ref, query_gain_ref, key_gain_ref)
        ids_ref[...] = jnp.zeros_like(ids_ref)
        ids_ref[:parts, :] = segs_ref[...].astype(wide)
        ids_ref[IDS // 2 : IDS // 2 + parts, :] = vars_ref[...].astype(wide)

    normed = normed_ref[...]

    def turned(raw, gain):
        x = raw * lax.rsqrt(head_mean(raw * raw) + EPSILON) * gain
        return x * cosine_ref[...] + swap_halves(x) * sine_ref[...]

    query_ref[...] = dot_nn(normed, w_ref[0])
    key_ref[...] = dot_nn(normed, w_ref[1])
    values = dot_nn(normed, w_ref[2])
    for pair in range(query_ref.shape[1] // LANES):
        span = slice(pair * LANES, (pair + 1) * LANES)
        one, two = 2 * pair, 2 * pair + 1
        query = turned(query_ref[:, span], pair_gain_ref[0:1])
        key = turned(key_ref[:, span], pair_gain_ref[2:3])
        value = values[:, span]
        message_ref[one, :rows] = left_pair(key, value).astype(low)
        message_ref[two, :rows] = right_pair(key, value).astype(low)
        upper, lower = query[: rows // 2], query[rows // 2 :]
        message_ref[one, rows + IDS :] = left_pair(upper, lower).astype(low)
        message_ref[two, rows + IDS :] = right_pair(upper, lower).astype(low)
        message_ref[one, rows : rows + IDS] = ids_ref[...].astype(low)
        message_ref[two, rows : rows + IDS] = ids_ref[...].astype(low)


def project(tokens, w_qkv, gain, query_gain, key_gain, cosine, sine, segs, variates):
    rows, depth = tokens.shape
    width = w_qkv.shape[2]
    size = rows + IDS + rows // 2
    wider = LANES * (1 + (width // LANES + 1) % 2)
    column = pl.BlockSpec((rows, wider), lambda i: (0, i))
    return pl.pallas_call(
        project_kernel,
        grid=(width // wider,),
        in_specs=[
            WHOLE,
            pl.BlockSpec((3, depth, wider), lambda i: (0, 0, i)),
            WHOLE, WHOLE, WHOLE, WHOLE, WHOLE, WHOLE, WHOLE,
        ],
        out_specs=(
            pl.BlockSpec((wider // HD, size, LANES), lambda i: (i, 0, 0)),
            column, column,
            pl.BlockSpec((rows, depth), lambda i: (0, 0)),
        ),
        out_shape=(
            jax.ShapeDtypeStruct((width // HD, size, LANES), low),
            jax.ShapeDtypeStruct((rows, width), wide),
            jax.ShapeDtypeStruct((rows, width), wide),
            jax.ShapeDtypeStruct((rows, depth), low),
        ),
        scratch_shapes=[pltpu.VMEM((8, LANES), wide), pltpu.VMEM((IDS, LANES), wide)],
        compiler_params=params(),
    )(tokens, w_qkv, gain, query_gain, key_gain, cosine, sine, segs, variates)


def walk(begin, end, body, largest):
    count = (end - begin) // LANES
    many = largest // LANES

    def step(index, carry):
        body(begin + index * largest, largest)
        return carry

    lax.fori_loop(0, count // many, step, 0)
    size = many // 2
    while size:
        piece = size * LANES
        at = begin + (count // (2 * size)) * (2 * piece)

        @pl.when((count // size) % 2 == 1)
        def rest(at=at, piece=piece):
            body(at, piece)

        size //= 2


def scalar(x):
    return x[0, 0].astype(jnp.int32)


def forward_kernel(
    bias_ref, kv_ref, query_in_ref,
    k_ref, v_ref, q_ref, exact_ref, message_ref, runs_ref, acc_ref, seg_ref, upto_ref, keys_ref,
):
    ranks, heads = kv_ref.shape[:2]
    rows = q_ref.shape[0]
    half = rows // 2
    parts = rows // LANES
    block = pl.program_id(0)
    place = lax.axis_index("dp")
    rank = lax.rem(place, ranks)
    head = place // ranks
    filled = lax.broadcasted_iota(jnp.int32, (IDS // 2, LANES), 0) < parts

    @pl.when(block == 0)
    def prepare():
        keys = key_table()
        for rank_at in range(ranks):
            for head_at in range(heads):
                at = head_at * ranks + rank_at
                ids = kv_ref[rank_at, head_at, rows:, :].astype(wide)
                seg_ref[at] = jnp.where(filled, ids[: IDS // 2], DOCS + 1.0)
                extra = features(ids, parts, keys)
                kv = kv_ref[rank_at, head_at, :rows].astype(wide)
                lane = lanes_of(kv)
                span = pl.ds(at * rows, rows)
                k_ref[span, :] = jnp.where(lane < HD, kv, extra).astype(low)
                one = jnp.where(lane < HD + 3, 1.0, 0.0)
                v_ref[span, :] = jnp.where(lane < HD, pltpu.roll(kv, HD, 1), one).astype(low)
        every = seg_ref[...].reshape(ranks * heads * (IDS // 2), LANES)
        own = jnp.stack([seg_ref[head_at * ranks + rank] for head_at in range(heads)])
        own = own.reshape(heads * (IDS // 2), LANES)
        upto_ref[0, 0] = 0
        upto_ref[1, 0] = 0
        for document in range(DOCS):
            for which, segs in ((0, every), (1, own)):
                count = jnp.sum(jnp.where(segs <= document, 1.0, 0.0), keepdims=True)
                upto_ref[which, document + 1] = scalar(count)
        for at in range(ranks * heads):
            segs = seg_ref[at]
            first = scalar(segs[:1, :1])
            last = scalar(segs[parts - 1 : parts, LANES - 1 :])
            keys_ref[0, at] = upto_ref[0, first] // LANES * LANES
            keys_ref[1, at] = (upto_ref[0, last + 1] + LANES - 1) // LANES * LANES
            runs_ref[0, at] = upto_ref[1, first] // LANES * LANES
            runs_ref[1, at] = (upto_ref[1, last + 1] + LANES - 1) // LANES * LANES

    begin = keys_ref[0, block * ranks + rank]
    end = keys_ref[1, block * ranks + rank]
    queries = query_table((bias_ref[0, head] - bias_ref[1, head]) * LOG2E)
    ids = kv_ref[rank, block, pl.ds(rows, IDS), :].astype(wide)
    extra = features(ids, parts, queries)
    folded = query_in_ref[0].astype(wide)
    head_part = jnp.concatenate([folded, pltpu.roll(folded, HD, 1)], axis=0)
    q_ref[...] = jnp.where(lanes_of(extra) < HD, head_part, extra).astype(low)
    acc_ref[...] = jnp.zeros_like(acc_ref)

    def step(start, size):
        span = pl.ds(pl.multiple_of(start, LANES), size)
        probs = jnp.exp2(dot_nt(q_ref[...], k_ref[span, :])).astype(low)
        acc_ref[...] += dot_nn(probs, v_ref[span, :])

    walk(begin, end, step, 4096)
    total = acc_ref[...]
    row_sum = total[:, HD : HD + 1]
    exact = total / row_sum
    exact_ref[...] = jnp.where(lanes_of(total) < HD, exact, jnp.log2(row_sum))
    message_ref[0] = left_pair(exact[:half], exact[half:]).astype(low)


def forward_attention(bias, kv, query):
    ranks, heads, size = kv.shape[:3]
    rows = size - IDS
    every = ranks * heads * rows
    part = pl.BlockSpec((rows, LANES), lambda i: (i, 0))
    fold = pl.BlockSpec((1, rows // 2, LANES), lambda i: (i, 0, 0))
    return pl.pallas_call(
        forward_kernel,
        grid=(heads,),
        in_specs=[SCALARS, WHOLE, fold],
        out_specs=(WHOLE, WHOLE, part, part, fold, SCALARS),
        scratch_shapes=[
            pltpu.VMEM((rows, LANES), wide),
            pltpu.VMEM((ranks * heads, IDS // 2, LANES), wide),
            pltpu.SMEM((2, DOCS + 1), jnp.int32),
            pltpu.SMEM((2, ranks * heads), jnp.int32),
        ],
        out_shape=(
            jax.ShapeDtypeStruct((every, LANES), low),
            jax.ShapeDtypeStruct((every, LANES), low),
            jax.ShapeDtypeStruct((heads * rows, LANES), low),
            jax.ShapeDtypeStruct((heads * rows, LANES), wide),
            jax.ShapeDtypeStruct((heads, rows // 2, LANES), low),
            jax.ShapeDtypeStruct((2, ranks * heads), jnp.int32),
        ),
        compiler_params=params(),
    )(bias, kv, query)


def split_lanes(column, lane, at):
    high = column.astype(low).astype(wide)
    mid = (column - high).astype(low).astype(wide)
    parts = jnp.where(lane == at, high, jnp.where(lane == at + 1, mid, column - high - mid))
    return jnp.where(lane < at + 3, parts, 0.0)


def backward_kernel(
    runs_ref, k_ref, v_ref, q_in_ref, exact_ref, grad_in_ref, ids_ref,
    kv_ref, message_ref, bias_ref, q_ref, g_ref, kt_ref, dk_ref, dv_ref, dq_ref,
):
    heads, half = grad_in_ref.shape[:2]
    rows = 2 * half
    block = pl.program_id(0)

    @pl.when(block == 0)
    def prepare():
        dq_ref[...] = jnp.zeros_like(dq_ref)
        for head_at in range(heads):
            folded = grad_in_ref[head_at].astype(wide)
            for side in range(2):
                span = pl.ds(head_at * rows + side * half, half)
                grad = folded if side == 0 else pltpu.roll(folded, HD, 1)
                lane = lanes_of(grad)
                grad = jnp.where(lane < HD, grad, 0.0)
                exact = exact_ref[span, :]
                delta = jnp.sum(grad * exact, axis=1, keepdims=True)
                g_ref[span, :] = jnp.where(lane < HD, grad, split_lanes(-delta, lane, HD)).astype(low)
                query = q_in_ref[span, :].astype(wide)
                total = split_lanes(-exact[:, HD : HD + 1], lane, ONE_AT)
                q_ref[span, :] = jnp.where(lane < ONE_AT, query, total).astype(low)

    dk_ref[...] = jnp.zeros_like(dk_ref)
    dv_ref[...] = jnp.zeros_like(dv_ref)
    key = k_ref[...]
    value = v_ref[...]
    kt_ref[...] = key.astype(wide).T.astype(low)

    def step(start, size):
        span = pl.ds(pl.multiple_of(start, LANES), size)
        query = q_ref[span, :]
        grad = g_ref[span, :]
        probs = jnp.exp2(dot_nt(key, query))
        grad_scores = (probs * dot_nt(value, grad)).astype(low)
        dv_ref[...] += dot_nn(probs.astype(low), grad)
        dk_ref[...] += dot_nn(grad_scores, query)
        dq_ref[:, span] += dot_nn(kt_ref[...], grad_scores)

    walk(runs_ref[0, block], runs_ref[1, block], step, 2048)
    kv_ref[0, 0] = left_pair(dk_ref[...] * (1.0 / LOG2E), dv_ref[...]).astype(low)

    @pl.when(block == pl.num_programs(0) - 1)
    def finish():
        same = jnp.zeros((8, LANES), wide)
        every = jnp.zeros((8, LANES), wide)
        index = lax.broadcasted_iota(jnp.int32, (8, LANES), 0)
        for head_at in range(heads):
            ids = ids_ref[head_at].astype(wide)
            for part in range(rows // LANES):
                at = head_at * rows + part * LANES
                by_variate = jnp.where(index < VARS, dq_ref[VAR_AT : VAR_AT + 8, at : at + LANES], 0.0)
                variates = jnp.broadcast_to(
                    ids[IDS // 2 + part : IDS // 2 + part + 1], (8, LANES)
                ).astype(jnp.int32)
                same = same + jnp.where(variates == index, by_variate, 0.0)
                every = every + by_variate
            span = dq_ref[:, head_at * rows : (head_at + 1) * rows].T * HD**-0.5
            message_ref[head_at] = left_pair(span[:half], span[half:]).astype(low)
        bias_ref[0] = same
        bias_ref[1] = every - same


def backward_attention(runs, key, value, query, exact, grad, ids):
    every = key.shape[0]
    heads, half = grad.shape[:2]
    rows = 2 * half
    ranks = every // (heads * rows)
    part = pl.BlockSpec((rows, LANES), lambda i, *_: (i, 0))
    return pl.pallas_call(
        backward_kernel,
        grid_spec=pltpu.PrefetchScalarGridSpec(
            num_scalar_prefetch=1,
            grid=(ranks * heads,),
            in_specs=[part, part, WHOLE, WHOLE, WHOLE, WHOLE],
            out_specs=(
                pl.BlockSpec((1, 1, rows, LANES), lambda i, *_: (i % ranks, i // ranks, 0, 0)),
                WHOLE,
                WHOLE,
            ),
            scratch_shapes=[
                pltpu.VMEM((heads * rows, LANES), low),
                pltpu.VMEM((heads * rows, LANES), low),
                pltpu.VMEM((LANES, rows), low),
                pltpu.VMEM((rows, LANES), wide),
                pltpu.VMEM((rows, LANES), wide),
                pltpu.VMEM((LANES, heads * rows), wide),
            ],
        ),
        out_shape=(
            jax.ShapeDtypeStruct((ranks, heads, rows, LANES), low),
            jax.ShapeDtypeStruct((heads, half, LANES), low),
            jax.ShapeDtypeStruct((2, 8, LANES), wide),
        ),
        compiler_params=params(),
    )(runs, key, value, query, exact, grad, ids)


def columns_of(width):
    if width % LANES:
        return [(0, width)]
    return [(at, min(2 * LANES, width - at)) for at in range(0, width, 2 * LANES)]


def mlp_kernel(
    landed_ref, tokens_ref, cotangent_ref, gain_ref, own_out_ref, other_out_ref, gateup_ref, down_ref,
    heads_ref, middle_ref, normed_ref, hidden_ref, grad_gu_ref, part_ref, part_low_ref, gain_part_ref,
    others_ref, gateup_in, down_in, sums_ref, copied,
):
    tensor, heads, half = landed_ref.shape[:3]
    copies = [
        pltpu.make_async_copy(gateup_ref, gateup_in, copied.at[0]),
        pltpu.make_async_copy(down_ref, down_in, copied.at[1]),
    ]
    for copy in copies:
        copy.start()
    for share in range(tensor):
        to_ref = others_ref if share else heads_ref
        for pair in range(heads // 2):
            one = landed_ref[share, 2 * pair].astype(wide)
            two = landed_ref[share, 2 * pair + 1].astype(wide)
            span = pl.ds(pair * LANES, LANES)
            to_ref[:half, span] = left_pair(one, two).astype(low)
            to_ref[half:, span] = right_pair(one, two).astype(low)
        if share:
            middle_ref[...] += dot_nn(to_ref[...], other_out_ref[share - 1])
        else:
            middle_ref[...] = tokens_ref[...].astype(wide) + dot_nn(to_ref[...], own_out_ref[...])

    def unit_and_scale():
        middle = middle_ref[...]
        scale = lax.rsqrt(jnp.mean(middle * middle, axis=1, keepdims=True) + EPSILON)
        return middle * scale, scale

    normed_ref[...] = (unit_and_scale()[0] * gain_ref[...]).astype(low)
    for copy in copies:
        copy.wait()
    sums_ref[...] = jnp.zeros_like(sums_ref)
    for at, size in columns_of(hidden_ref.shape[1]):
        span = slice(at, at + size)
        w_gate = gateup_in[0, :, span]
        w_up = gateup_in[1, :, span]
        gate = dot_nn(normed_ref[...], w_gate)
        up = dot_nn(normed_ref[...], w_up)
        grad = dot_nt(cotangent_ref[...], down_in[span, :])
        sigmoid = 1.0 / (1.0 + jnp.exp(-gate))
        active = gate * sigmoid
        hidden_ref[:, span] = (active * up).astype(low)
        grad_gate = (grad * up * sigmoid * (1.0 + gate * (1.0 - sigmoid))).astype(low)
        grad_up = (grad * active).astype(low)
        grad_gu_ref[0, :, span] = grad_gate
        grad_gu_ref[1, :, span] = grad_up
        sums_ref[...] += dot_nt(grad_gate, w_gate) + dot_nt(grad_up, w_up)
    unit, scale = unit_and_scale()
    sums = sums_ref[...]
    gain_part = jnp.sum(sums * unit, axis=0, keepdims=True)
    for row in range(gain_part_ref.shape[0]):
        gain_part_ref[row : row + 1, :] = gain_part[:, row * LANES : (row + 1) * LANES]
    scaled = sums * gain_ref[...]
    part = scale * (scaled - unit * jnp.mean(scaled * unit, axis=1, keepdims=True))
    part_ref[...] = part
    part_low_ref[...] = part.astype(low)


def out_and_mlp(landed, tokens, cotangent, gain, w_out, w_others, w_gateup, w_down):
    tensor, heads, half = landed.shape[:3]
    rows, depth = tokens.shape
    width, units = heads * HD, w_down.shape[0]
    shape = jax.ShapeDtypeStruct
    return pl.pallas_call(
        mlp_kernel,
        in_specs=[WHOLE] * 6 + [ANYWHERE] * 2,
        out_specs=(WHOLE,) * 8,
        out_shape=(
            shape((rows, width), low),
            shape((rows, depth), wide),
            shape((rows, depth), low),
            shape((rows, units), low),
            shape((2, rows, units), low),
            shape((rows, depth), wide),
            shape((rows, depth), low),
            shape((depth // LANES, LANES), wide),
        ),
        scratch_shapes=[
            pltpu.VMEM((rows, width), low),
            pltpu.VMEM(w_gateup.shape, low),
            pltpu.VMEM(w_down.shape, low),
            pltpu.VMEM((rows, depth), wide),
            pltpu.SemaphoreType.DMA((2,)),
        ],
        compiler_params=params(),
    )(landed, tokens, cotangent, gain, w_out, w_others, w_gateup, w_down)


def grad_heads_kernel(grad_ref, w_ref, message_ref):
    half = message_ref.shape[1]
    for pair in range(message_ref.shape[0] // 2):
        both = dot_nt(grad_ref[...], w_ref[pair * LANES : (pair + 1) * LANES, :])
        message_ref[2 * pair] = left_pair(both[:half], both[half:]).astype(low)
        message_ref[2 * pair + 1] = right_pair(both[:half], both[half:]).astype(low)


def grad_heads_of(grad, w_out):
    return pl.pallas_call(
        grad_heads_kernel,
        in_specs=[WHOLE, WHOLE],
        out_specs=WHOLE,
        out_shape=jax.ShapeDtypeStruct((w_out.shape[0] // HD, grad.shape[0] // 2, LANES), low),
        compiler_params=params(),
    )(grad, w_out)


def tail_kernel(
    landed_ref, query_ref, key_ref, query_gain_ref, key_gain_ref, cosine_ref, sine_ref, tokens_ref, gain_ref,
    normed_ref, w_ref, mlp_gain_ref, bias_ref,
    grad_qkv_ref, input_ref, small_ref, grad_ref, pair_gain_ref, *, every_head,
):
    double_gains(pair_gain_ref, query_gain_ref, key_gain_ref)
    rows, width = query_ref.shape
    depth = tokens_ref.shape[1]

    def back(turned, raw, gain):
        grad = turned * cosine_ref[...] - swap_halves(turned) * sine_ref[...]
        scale = lax.rsqrt(head_mean(raw * raw) + EPSILON)
        unit = raw * scale
        scaled = grad * gain
        part = jnp.sum(grad * unit, axis=0, keepdims=True)
        return (scale * (scaled - unit * head_mean(scaled * unit))).astype(low), part

    query_part = jnp.zeros((1, LANES), wide)
    key_part = jnp.zeros((1, LANES), wide)
    for pair in range(width // LANES):
        span = slice(pair * LANES, (pair + 1) * LANES)
        key_one = landed_ref[2 * pair, :rows].astype(wide)
        key_two = landed_ref[2 * pair + 1, :rows].astype(wide)
        query_one = landed_ref[2 * pair, rows:].astype(wide)
        query_two = landed_ref[2 * pair + 1, rows:].astype(wide)
        query = jnp.concatenate(
            [left_pair(query_one, query_two), right_pair(query_one, query_two)], axis=0
        )
        grad_ref[0, :, span], part = back(query, query_ref[:, span], pair_gain_ref[1:2])
        query_part = query_part + part
        grad_ref[1, :, span], part = back(
            left_pair(key_one, key_two), key_ref[:, span], pair_gain_ref[2:3]
        )
        key_part = key_part + part
        grad_ref[2, :, span] = right_pair(key_one, key_two).astype(low)
    sums = dot_nt(grad_ref[0], w_ref[0]) + dot_nt(grad_ref[1], w_ref[1])
    sums = sums + dot_nt(grad_ref[2], w_ref[2])
    x = tokens_ref[...].astype(wide)
    scale = lax.rsqrt(jnp.mean(x * x, axis=1, keepdims=True) + EPSILON)
    unit = x * scale
    gain_part = jnp.sum(sums * unit, axis=0, keepdims=True)
    scaled = sums * gain_ref[...]
    part = scale * (scaled - unit * jnp.mean(scaled * unit, axis=1, keepdims=True))
    input_ref[...] = part.astype(low)
    for index in range(3):
        grad_qkv_ref[index] = dot_nn(normed_ref[...], grad_ref[index]).astype(low)
    count = depth // LANES
    small_ref[...] = jnp.zeros_like(small_ref)
    for row in range(count):
        small_ref[row : row + 1, :] = gain_part[:, row * LANES : (row + 1) * LANES]
    small_ref[count : 2 * count, :] = mlp_gain_ref[...]
    small_ref[2 * count : 2 * count + 1, :] = query_part
    small_ref[2 * count + 1 : 2 * count + 2, :] = key_part
    head = lax.axis_index("tensor") * (width // HD) + lax.axis_index("dp") // every_head
    lane = lax.broadcasted_iota(jnp.int32, (1, LANES), 1)
    for row in range(2):
        total = jnp.sum(bias_ref[row], keepdims=True)
        at = 2 * count + 2 + row
        small_ref[at : at + 1, :] = jnp.where(lane == head, total, 0.0)


def tail(
    landed, raw_query, raw_key, query_gain, key_gain, cosine, sine, tokens, gain, normed_turned,
    w_qkv, mlp_gain_part, bias_tiles, ranks,
):
    rows, width = raw_query.shape
    depth = tokens.shape[1]
    small = -(-(2 * depth // LANES + 4) // 8) * 8
    return pl.pallas_call(
        functools.partial(tail_kernel, every_head=ranks),
        in_specs=[WHOLE] * 13,
        out_specs=(WHOLE,) * 3,
        out_shape=(
            jax.ShapeDtypeStruct((3, depth, width), low),
            jax.ShapeDtypeStruct((rows, depth), low),
            jax.ShapeDtypeStruct((small, LANES), wide),
        ),
        scratch_shapes=[pltpu.VMEM((3, rows, width), low), pltpu.VMEM((8, LANES), wide)],
        compiler_params=params(),
    )(
        landed, raw_query, raw_key, query_gain, key_gain, cosine, sine, tokens, gain, normed_turned,
        w_qkv, mlp_gain_part, bias_tiles,
    )


def widen_kernel(*refs):
    half = len(refs) // 2
    for source, target in zip(refs[:half], refs[half:]):
        target[...] = source[...].astype(wide)


def widen(arrays):
    steps = 8
    while any(a.shape[0] % (16 * steps) for a in arrays):
        steps //= 2
    specs = [pl.BlockSpec((a.shape[0] // steps, a.shape[1]), lambda i: (i, 0)) for a in arrays]
    return pl.pallas_call(
        widen_kernel,
        grid=(steps,),
        in_specs=specs,
        out_specs=tuple(specs),
        out_shape=tuple(jax.ShapeDtypeStruct(a.shape, wide) for a in arrays),
        compiler_params=params(),
    )(*arrays)


def remote(src, dst, send, recv, place):
    return pltpu.make_async_remote_copy(
        src_ref=src, dst_ref=dst, send_sem=send, recv_sem=recv,
        device_id={"dp": place}, device_id_type=MESH,
    )


def peer(head, step, heads):
    if heads & (heads - 1):
        return lax.rem(head + step, heads)
    to = 0
    bit = 1
    while bit < heads:
        mine = lax.rem(head // bit, 2)
        to = to + bit * (1 - mine if step & bit else mine)
        bit *= 2
    return to


def origin(head, step, heads):
    if heads & (heads - 1):
        return lax.rem(head + heads - step, heads)
    return peer(head, step, heads)


def greet(heads, ranks, head, rank, with_ranks, tensor=1):
    barrier = pltpu.get_barrier_semaphore()
    for step in range(1, tensor):
        side = lax.rem(lax.axis_index("tensor") + step, tensor)
        pl.semaphore_signal(barrier, inc=1, device_id={"tensor": side}, device_id_type=MESH)
    for step in range(1, heads):
        place = peer(head, step, heads) * ranks + rank
        pl.semaphore_signal(barrier, inc=1, device_id={"dp": place}, device_id_type=MESH)
    if with_ranks:
        for step in range(1, ranks):
            place = head * ranks + lax.rem(rank + step, ranks)
            pl.semaphore_signal(barrier, inc=1, device_id={"dp": place}, device_id_type=MESH)
    pl.semaphore_wait(barrier, heads + tensor - 2 + (ranks - 1 if with_ranks else 0))


def spread_kernel(
    message_ref, w_ref, kv_ref, query_ref, others_ref,
    send_a, recv_a, send_b, recv_b, send_f, recv_f, send_w, recv_w, local, *, ranks
):
    heads = message_ref.shape[0]
    tensor = others_ref.shape[0] + 1
    side = lax.axis_index("tensor")
    size = kv_ref.shape[2]
    rest = query_ref.shape[1]
    place = lax.axis_index("dp")
    head = place // ranks
    rank = lax.rem(place, ranks)
    greet(heads, ranks, head, rank, True, tensor)
    onward = []
    for step in range(1, tensor):
        copy = pltpu.make_async_remote_copy(
            src_ref=w_ref, dst_ref=others_ref.at[tensor - step - 1],
            send_sem=send_w.at[step], recv_sem=recv_w.at[step],
            device_id={"tensor": lax.rem(side + step, tensor)}, device_id_type=MESH,
        )
        copy.start()
        onward.append(copy)
    firsts = {}
    for step in reversed(range(1, heads)):
        to = peer(head, step, heads)
        at = to * ranks + rank
        first = remote(
            message_ref.at[to, pl.ds(0, size)], kv_ref.at[rank, head],
            send_a.at[step], recv_a.at[step], at,
        )
        second = remote(
            message_ref.at[to, pl.ds(size, rest)], query_ref.at[head],
            send_b.at[step], recv_b.at[step], at,
        )
        first.start()
        second.start()
        firsts[step] = (first, second)
    mine = [
        pltpu.make_async_copy(message_ref.at[head, pl.ds(0, size)], kv_ref.at[rank, head], local.at[0]),
        pltpu.make_async_copy(message_ref.at[head, pl.ds(size, rest)], query_ref.at[head], local.at[1]),
    ]
    for copy in mine:
        copy.start()

    def forward(step, source, src):
        for other in range(1, ranks):
            copy = remote(
                src, kv_ref.at[rank, source], send_f.at[step, other], recv_f.at[step, other],
                head * ranks + lax.rem(rank + other, ranks),
            )
            copy.start()
            onward.append(copy)

    forward(0, head, message_ref.at[head, pl.ds(0, size)])
    for step in reversed(range(1, heads)):
        source = origin(head, step, heads)
        firsts[step][0].wait_recv()
        forward(step, source, kv_ref.at[rank, source])
    for first, second in firsts.values():
        first.wait_send()
        second.wait()
    for copy in mine + onward:
        copy.wait()


def spread(message, w_out, ranks, rows, tensor):
    heads, size = message.shape[:2]
    dma = pltpu.SemaphoreType.DMA
    return pl.pallas_call(
        functools.partial(spread_kernel, ranks=ranks),
        in_specs=[ANYWHERE] * 2,
        out_specs=(ANYWHERE,) * 3,
        out_shape=(
            jax.ShapeDtypeStruct((ranks, heads, rows + IDS, LANES), low),
            jax.ShapeDtypeStruct((heads, rows // 2, LANES), low),
            jax.ShapeDtypeStruct((tensor - 1,) + w_out.shape, low),
        ),
        scratch_shapes=[dma((heads,))] * 4 + [dma((heads, ranks))] * 2 + [dma((tensor,))] * 2 + [dma((2,))],
        compiler_params=params(collective_id=0, has_side_effects=True),
    )(message, w_out)


def send_shares(part_ref, shares_ref, send, recv):
    tensor, _, share = shares_ref.shape
    tensor += 1
    side = lax.axis_index("tensor")
    copies = []
    for step in range(1, tensor):
        to = lax.rem(side + step, tensor)
        copies.append(
            pltpu.make_async_remote_copy(
                src_ref=part_ref.at[:, pl.ds(pl.multiple_of(to * share, LANES), share)],
                dst_ref=shares_ref.at[tensor - step - 1],
                send_sem=send.at[step], recv_sem=recv.at[step],
                device_id={"tensor": to}, device_id_type=MESH,
            )
        )
        copies[-1].start()
    return copies


def exchange_kernel(
    message_ref, part_ref, landed_ref, shares_ref, send, recv, send_t, recv_t, local, *, ranks
):
    heads = message_ref.shape[0]
    place = lax.axis_index("dp")
    head = place // ranks
    rank = lax.rem(place, ranks)
    greet(heads, ranks, head, rank, False, shares_ref.shape[0] + 1)
    copies = []
    for step in reversed(range(1, heads)):
        to = peer(head, step, heads)
        copies.append(
            remote(
                message_ref.at[to], landed_ref.at[head], send.at[step], recv.at[step],
                to * ranks + rank,
            )
        )
        copies[-1].start()
    copies.append(pltpu.make_async_copy(message_ref.at[head], landed_ref.at[head], local))
    copies[-1].start()
    copies += send_shares(part_ref, shares_ref, send_t, recv_t)
    for copy in copies:
        copy.wait()


def exchange(message, part, ranks, tensor):
    heads = message.shape[0]
    rows, depth = part.shape
    dma = pltpu.SemaphoreType.DMA
    return pl.pallas_call(
        functools.partial(exchange_kernel, ranks=ranks),
        in_specs=[ANYWHERE] * 2,
        out_specs=(ANYWHERE,) * 2,
        out_shape=(
            jax.ShapeDtypeStruct(message.shape, message.dtype),
            jax.ShapeDtypeStruct((tensor - 1, rows, depth // tensor), low),
        ),
        scratch_shapes=[dma((heads,))] * 2 + [dma((tensor,))] * 2 + [dma],
        compiler_params=params(collective_id=2, has_side_effects=True),
    )(message, part)


def share_out_kernel(message_ref, landed_ref, send, recv, send_t, recv_t, local, *, ranks, tensor):
    heads = message_ref.shape[0]
    place = lax.axis_index("dp")
    side = lax.axis_index("tensor")
    head = place // ranks
    rank = lax.rem(place, ranks)
    barrier = pltpu.get_barrier_semaphore()
    for step in range(1, tensor):
        to = lax.rem(side + step, tensor)
        pl.semaphore_signal(barrier, inc=1, device_id={"tensor": to}, device_id_type=MESH)
    for step in range(1, heads):
        to = peer(head, step, heads) * ranks + rank
        pl.semaphore_signal(barrier, inc=1, device_id={"dp": to}, device_id_type=MESH)
    pl.semaphore_wait(barrier, heads + tensor - 2)
    copies = []
    for step in range(1, heads):
        to = peer(head, step, heads)
        copies.append(
            remote(
                message_ref.at[to], landed_ref.at[0, head], send.at[step], recv.at[step],
                to * ranks + rank,
            )
        )
        copies[-1].start()
    mine = pltpu.make_async_copy(message_ref.at[head], landed_ref.at[0, head], local)
    mine.start()
    onward = []

    def relay(step, source, src):
        for other in range(1, tensor):
            copy = pltpu.make_async_remote_copy(
                src_ref=src, dst_ref=landed_ref.at[tensor - other, source],
                send_sem=send_t.at[step, other], recv_sem=recv_t.at[step, other],
                device_id={"tensor": lax.rem(side + other, tensor)}, device_id_type=MESH,
            )
            copy.start()
            onward.append(copy)

    relay(0, head, message_ref.at[head])
    for step in range(1, heads):
        source = origin(head, step, heads)
        copies[step - 1].wait_recv()
        relay(step, source, landed_ref.at[0, source])
    for copy in copies:
        copy.wait_send()
    mine.wait()
    for copy in onward:
        copy.wait()


def share_out(message, ranks, tensor):
    heads = message.shape[0]
    dma = pltpu.SemaphoreType.DMA
    return pl.pallas_call(
        functools.partial(share_out_kernel, ranks=ranks, tensor=tensor),
        in_specs=[ANYWHERE],
        out_specs=ANYWHERE,
        out_shape=jax.ShapeDtypeStruct((tensor,) + message.shape, message.dtype),
        scratch_shapes=[dma((heads,))] * 2 + [dma((heads, tensor))] * 2 + [dma],
        compiler_params=params(collective_id=1, has_side_effects=True),
    )(message)


def total_kernel(*refs, arrays, chunks, zs, tensor):
    ins, part_ref, refs = refs[: arrays + 1], refs[arrays + 1], refs[arrays + 2 :]
    outs, shares_ref, refs = refs[: arrays + 1], refs[arrays + 1], refs[arrays + 2 :]
    count = len(chunks)
    scratch, refs = refs[: 5 * count], refs[5 * count :]
    near_ref, far_ref, line_ref, side_ref, send, recv, send_z, recv_z, send_s, recv_s, send_t, recv_t = refs
    place = lax.axis_index("dp")
    side = lax.axis_index("tensor")
    core = lax.rem(place, 2)
    x = lax.rem(place // 2, 2)
    z = place // 4
    base = place - core
    core_mate = base + 1 - core
    x_mate = z * 4 + (1 - x) * 2 + core
    z_mates = [lax.rem(z + step, zs) * 4 + x * 2 + core for step in range(1, zs)]

    barrier = pltpu.get_barrier_semaphore()
    for to in [core_mate, x_mate] + z_mates:
        pl.semaphore_signal(barrier, inc=1, device_id={"dp": to}, device_id_type=MESH)
    for step in range(1, tensor):
        to = lax.rem(side + step, tensor)
        pl.semaphore_signal(barrier, inc=1, device_id={"tensor": to}, device_id_type=MESH)
    pl.semaphore_wait(barrier, zs + tensor)
    shares = send_shares(part_ref, shares_ref, send_t, recv_t)
    sent = []
    waits = {}

    def rows_at(at, size):
        return pl.ds(pl.multiple_of(at, 16), size)

    def pieces(chunk):
        index, lead, begin, size = chunks[chunk]
        source = ins[index] if lead is None else ins[index].at[lead]
        target = outs[index] if lead is None else outs[index].at[lead]
        source, target = (ref.at[pl.ds(begin, size)] for ref in (source, target))
        return source, target, size, scratch[5 * chunk : 5 * chunk + 5]

    def go(copy, key):
        copy.start()
        sent.append(copy)
        waits.setdefault(key, []).append(copy)

    def arrived(key):
        for copy in waits[key]:
            copy.wait_recv()

    def halve_core(chunk):
        source, _, size, (first, _, _, _, _) = pieces(chunk)
        go(
            remote(
                source.at[rows_at((1 - core) * (size // 2), size // 2)], first,
                send.at[chunk, 0], recv.at[chunk, 0], core_mate,
            ),
            (chunk, 0),
        )

    def halve_x(chunk):
        source, _, size, (first, half, second, _, _) = pieces(chunk)
        arrived((chunk, 0))
        mine = source[rows_at(core * (size // 2), size // 2), :].astype(wide)
        half[...] = (mine + first[...].astype(wide)).astype(low)
        go(
            remote(
                half.at[rows_at((1 - x) * (size // 4), size // 4)], second,
                send.at[chunk, 1], recv.at[chunk, 1], x_mate,
            ),
            (chunk, 1),
        )

    def part_z(chunk):
        _, _, size, (_, half, second, quarter, third) = pieces(chunk)
        arrived((chunk, 1))
        mine = half[rows_at(x * (size // 4), size // 4), :].astype(wide)
        quarter[...] = (mine + second[...].astype(wide)).astype(low)
        part = size // (4 * zs)
        for step in range(1, zs):
            to = lax.rem(z + step, zs)
            go(
                remote(
                    quarter.at[rows_at(to * part, part)], third.at[step],
                    send_z.at[chunk, 0, step], recv_z.at[chunk, 0, step], z_mates[step - 1],
                ),
                (chunk, 2),
            )

    def spread_z(chunk):
        _, target, size, (_, _, _, quarter, third) = pieces(chunk)
        arrived((chunk, 2))
        part = size // (4 * zs)
        total = quarter[rows_at(z * part, part), :].astype(wide)
        for step in range(1, zs):
            total = total + third[step].astype(wide)
        span = rows_at(core * (size // 2) + x * (size // 4) + z * part, part)
        target[span, :] = total.astype(low)
        for step in range(1, zs):
            go(
                remote(
                    target.at[span], target.at[span],
                    send_z.at[chunk, 1, step], recv_z.at[chunk, 1, step], z_mates[step - 1],
                ),
                (chunk, 3),
            )

    def spread_x(chunk):
        _, target, size, _ = pieces(chunk)
        arrived((chunk, 3))
        span = rows_at(core * (size // 2) + x * (size // 4), size // 4)
        go(
            remote(target.at[span], target.at[span], send.at[chunk, 2], recv.at[chunk, 2], x_mate),
            (chunk, 4),
        )

    def spread_core(chunk):
        _, target, size, _ = pieces(chunk)
        arrived((chunk, 4))
        span = rows_at(core * (size // 2), size // 2)
        go(
            remote(target.at[span], target.at[span], send.at[chunk, 3], recv.at[chunk, 3], core_mate),
            (chunk, 5),
        )

    small = ins[arrays]

    def small_core():
        near_ref[0] = small[...]
        go(remote(near_ref.at[0], near_ref.at[1], send_s.at[0, 0], recv_s.at[0, 0], core_mate), "c")

    def small_x():
        arrived("c")
        far_ref[0] = near_ref[0] + near_ref[1]
        go(remote(far_ref.at[0], far_ref.at[1], send_s.at[1, 0], recv_s.at[1, 0], x_mate), "x")

    def small_z():
        arrived("x")
        line_ref[z] = far_ref[0] + far_ref[1]
        for step in range(1, zs):
            go(
                remote(
                    line_ref.at[z], line_ref.at[z], send_s.at[2, step], recv_s.at[2, step],
                    z_mates[step - 1],
                ),
                "z",
            )

    def small_side():
        arrived("z")
        total = line_ref[0]
        for at in range(1, zs):
            total = total + line_ref[at]
        side_ref[side] = total
        for step in range(1, tensor):
            copy = pltpu.make_async_remote_copy(
                src_ref=side_ref.at[side], dst_ref=side_ref.at[side],
                send_sem=send_s.at[3, step], recv_sem=recv_s.at[3, step],
                device_id={"tensor": lax.rem(side + step, tensor)}, device_id_type=MESH,
            )
            go(copy, "s")

    def small_end():
        if tensor > 1:
            arrived("s")
        total = side_ref[0]
        for at in range(1, tensor):
            total = total + side_ref[at]
        outs[arrays][...] = total

    stages = [halve_core, halve_x, part_z, spread_z, spread_x, spread_core]
    smalls = [small_core, small_x, small_z, small_side, small_end]
    for tick in range(max(count + LAGS[-1], len(smalls))):
        for stage in range(len(stages)):
            if 0 <= tick - LAGS[stage] < count:
                stages[stage](tick - LAGS[stage])
        if tick < len(smalls):
            smalls[tick]()
    for chunk in range(count):
        arrived((chunk, 5))
    for copy in sent:
        copy.wait_send()
    for copy in shares:
        copy.wait()


def total_sums(arrays, small, part, dp, tensor):
    zs = dp // 4
    chunks = []
    scratch = []
    for index, array in enumerate(arrays):
        leads = [None] if array.ndim == 2 else list(range(array.shape[0]))
        size, width = array.shape[-2:]
        total, size = size, min(size, max(64 * zs, FEWEST))
        for lead, begin in [(a, b) for a in leads for b in range(0, total, size)]:
            chunks.append((index, lead, begin, size))
            scratch += [
                pltpu.VMEM((size // 2, width), low),
                pltpu.VMEM((size // 2, width), low),
                pltpu.VMEM((size // 4, width), low),
                pltpu.VMEM((size // 4, width), low),
                pltpu.VMEM((zs, size // (4 * zs), width), low),
            ]
    dma = pltpu.SemaphoreType.DMA
    count = len(chunks)
    return pl.pallas_call(
        functools.partial(
            total_kernel, arrays=len(arrays), chunks=tuple(chunks), zs=zs, tensor=tensor
        ),
        in_specs=[WHOLE] * (len(arrays) + 1) + [ANYWHERE],
        out_specs=(WHOLE,) * (len(arrays) + 1) + (ANYWHERE,),
        out_shape=tuple(jax.ShapeDtypeStruct(a.shape, a.dtype) for a in [*arrays, small])
        + (jax.ShapeDtypeStruct((tensor - 1, part.shape[0], part.shape[1] // tensor), low),),
        scratch_shapes=scratch
        + [
            pltpu.VMEM((2,) + small.shape, wide),
            pltpu.VMEM((2,) + small.shape, wide),
            pltpu.VMEM((zs,) + small.shape, wide),
            pltpu.VMEM((tensor,) + small.shape, wide),
        ]
        + [dma((count, 4))] * 2
        + [dma((count, 2, zs))] * 2
        + [dma((4, max(zs, tensor)))] * 2
        + [dma((tensor,))] * 2,
        compiler_params=params(collective_id=4, has_side_effects=True),
    )(*arrays, small, part)


def collect_kernel(
    kv_ref, query_ref, landed_ref, piece_ref, sum_ref,
    send_p, recv_p, send_a, recv_a, send_b, recv_b, local, *, ranks,
):
    heads, rows = kv_ref.shape[1:3]
    half = query_ref.shape[1]
    place = lax.axis_index("dp")
    head = place // ranks
    rank = lax.rem(place, ranks)
    greet(heads, ranks, head, rank, True)
    order = list(reversed(range(heads)))
    pieces = {}
    copies = []
    for step in order:
        to = peer(head, step, heads)
        for other in range(1, ranks):
            partner = lax.rem(rank + other, ranks)
            pieces[step, other] = remote(
                kv_ref.at[partner, to], piece_ref.at[other, to],
                send_p.at[step, other], recv_p.at[step, other], head * ranks + partner,
            )
            pieces[step, other].start()
        if step:
            copies.append(
                remote(
                    query_ref.at[to], landed_ref.at[head, pl.ds(rows, half)],
                    send_b.at[step], recv_b.at[step], to * ranks + rank,
                )
            )
        else:
            copies.append(
                pltpu.make_async_copy(
                    query_ref.at[head], landed_ref.at[head, pl.ds(rows, half)], local.at[0]
                )
            )
        copies[-1].start()
    for step in order:
        to = peer(head, step, heads)
        total = kv_ref[rank, to].astype(wide)
        for other in range(1, ranks):
            pieces[step, other].wait_recv()
            total = total + piece_ref[other, to].astype(wide)
        sum_ref[to] = total.astype(low)
        if step:
            copies.append(
                remote(
                    sum_ref.at[to], landed_ref.at[head, pl.ds(0, rows)],
                    send_a.at[step], recv_a.at[step], to * ranks + rank,
                )
            )
        else:
            copies.append(
                pltpu.make_async_copy(
                    sum_ref.at[head], landed_ref.at[head, pl.ds(0, rows)], local.at[1]
                )
            )
        copies[-1].start()
    for piece in pieces.values():
        piece.wait_send()
    for copy in copies:
        copy.wait()


def collect(kv, query):
    ranks, heads, rows = kv.shape[:3]
    dma = pltpu.SemaphoreType.DMA
    return pl.pallas_call(
        functools.partial(collect_kernel, ranks=ranks),
        in_specs=[WHOLE, WHOLE],
        out_specs=ANYWHERE,
        out_shape=jax.ShapeDtypeStruct((heads, rows + rows // 2, LANES), low),
        scratch_shapes=[
            pltpu.VMEM((ranks, heads, rows, LANES), low),
            pltpu.VMEM((heads, rows, LANES), low),
        ]
        + [dma((heads, ranks))] * 2
        + [dma((heads,))] * 4
        + [dma((2,))],
        compiler_params=params(collective_id=3, has_side_effects=True),
    )(kv, query)


def tables(times):
    half = HD // 2
    lane = np.arange(LANES)
    inverse = (10000.0 ** (-2.0 * (lane % half) / HD)).astype(np.float32)
    sign = np.where(lane % HD < half, -1.0, 1.0).astype(np.float32)
    angles = times.astype(wide)[:, None] * inverse[None, :]
    return jnp.cos(angles), jnp.sin(angles) * sign[None, :]


def keep_order(x):
    return with_layout_constraint(x, Layout(major_to_minor=tuple(range(x.ndim))))


def id_rows(x):
    rows = x.reshape(-1, LANES).astype(low)
    return jnp.pad(rows, ((0, IDS // 2 - rows.shape[0]), (0, 0)))


def shards(
    tokens,
    cotangent,
    segment,
    variate,
    time,
    w_qkv,
    w_out,
    w_gateup,
    w_down,
    attn_gain,
    mlp_gain,
    query_gain,
    key_gain,
    var_bias,
):
    rows = tokens.shape[0]
    local_width = w_qkv.shape[2]
    heads = local_width // HD
    dp = lax.axis_size("dp")
    tensor = lax.axis_size("tensor")
    ranks = dp // heads
    place = lax.axis_index("dp")
    rank_here = lax.rem(place, ranks)
    width_share = tokens.shape[1] // tensor
    tensor_start = lax.axis_index("tensor") * width_share

    def tensor_sum(x, x_low):
        if tensor == 2:
            return x + lax.ppermute(x_low, "tensor", [(0, 1), (1, 0)]).astype(wide)
        return lax.psum(x_low, "tensor").astype(wide)

    def share_of(x):
        return lax.dynamic_slice_in_dim(x, tensor_start, width_share, 1).astype(wide)

    def share_sum(x, others):
        return share_of(x) + jnp.sum(others.astype(wide), axis=0)

    depth = tokens.shape[1]
    cosine, sine = tables(time)
    message, raw_query, raw_key, normed_one = project(
        tokens, w_qkv, attn_gain[None, :], query_gain[None, :], key_gain[None, :], cosine, sine,
        segment.reshape(-1, LANES), variate.reshape(-1, LANES),
    )
    kv, query_in, w_others = spread(message, w_out, ranks, rows, tensor)
    key_op, value_op, query_op, exact, out_message, runs = forward_attention(var_bias, kv, query_in)
    landed = share_out(out_message, ranks, tensor)
    heads_out, middle, normed_two, hidden, grad_gu, middle_part, middle_low, mlp_gain_part = out_and_mlp(
        landed, tokens, cotangent, mlp_gain[None, :], w_out, w_others, w_gateup, w_down
    )
    grad_down = jnp.einsum("tf,te->fe", hidden, cotangent, preferred_element_type=wide)
    grad_gateup = jnp.einsum("td,ktf->kdf", normed_two, grad_gu, preferred_element_type=wide)
    early = (keep_order(grad_gateup.astype(low)), grad_down.astype(low))
    mlp_part = jnp.dot(hidden, w_down, preferred_element_type=wide).astype(low)
    normed_turned = normed_one.T
    grad_middle = cotangent.astype(wide) + tensor_sum(middle_part, middle_low)
    grad_middle_low = grad_middle.astype(low)
    grad_middle_low, mlp_part, normed_turned = lax.optimization_barrier(
        (grad_middle_low, mlp_part, normed_turned)
    )
    grad_out = jnp.einsum("tc,td->cd", heads_out, grad_middle_low, preferred_element_type=wide)
    early = lax.psum((*early, grad_out.astype(low)), "dp")
    out_sum = early[2]
    grad_landed, mlp_others = exchange(
        grad_heads_of(grad_middle_low, w_out), mlp_part, ranks, tensor
    )
    output = (share_of(middle) + share_sum(mlp_part, mlp_others)).astype(low)
    own_ids = lax.dynamic_index_in_dim(kv[:, :, rows:], rank_here, 0, False)
    back_kv, back_query, bias_tiles = backward_attention(
        runs, key_op, value_op, query_op, exact, grad_landed, own_ids
    )
    grad_qkv, input_part, small = tail(
        collect(back_kv, back_query), raw_query, raw_key, query_gain[None, :], key_gain[None, :],
        cosine, sine, tokens, attn_gain[None, :], normed_turned, w_qkv, mlp_gain_part, bias_tiles, ranks,
    )
    qkv_sum, small, input_others = total_sums([grad_qkv], small, input_part, dp, tensor)
    grad_input = share_of(grad_middle) + share_sum(input_part, input_others)
    flat = lambda x: x.reshape(-1, x.shape[-1])
    (qkv_wide,) = widen([flat(qkv_sum)])
    gateup_wide, out_wide, down_wide = widen([flat(early[0]), out_sum, early[1]])
    count = 2 * depth // LANES
    gains = small[:count].reshape(2, depth)
    head_gains = small[count : count + 2, :HD] + small[count : count + 2, HD:]
    bias_sum = lax.dynamic_slice_in_dim(
        small[count + 2 : count + 4], lax.axis_index("tensor") * heads, heads, 1
    )
    return (
        output,
        grad_input,
        qkv_wide.reshape(w_qkv.shape),
        out_wide,
        gateup_wide.reshape(w_gateup.shape),
        down_wide,
        gains[0],
        gains[1],
        head_gains[0],
        head_gains[1],
        bias_sum,
    )


def solution(mesh):
    placed = (
        P("dp", None),
        P("dp", None),
        P("dp"),
        P("dp"),
        P("dp"),
        P(None, None, "tensor"),
        P("tensor", None),
        P(None, None, "tensor"),
        P("tensor", None),
        P(),
        P(),
        P(),
        P(),
        P(None, "tensor"),
    )
    return jax.shard_map(
        shards,
        mesh=mesh,
        in_specs=placed,
        out_specs=(
            P("dp", "tensor"),
            P("dp", "tensor"),
            P(None, None, "tensor"),
            P("tensor", None),
            P(None, None, "tensor"),
            P("tensor", None),
            P(),
            P(),
            P(),
            P(),
            P(None, "tensor"),
        ),
        check_vma=False,
    )
```

```python
import functools

import jax
import jax.numpy as jnp
import numpy as np
from jax import lax
from jax.experimental import pallas as pl
from jax.experimental.layout import Layout, with_layout_constraint
from jax.experimental.pallas import tpu as pltpu
from jax.sharding import PartitionSpec as P

HD = 64
LANES = 128
IDS = 16
EPSILON = 1e-05
LOG2E = 1.4426950408889634
FAR = -30000.0
DOCS = 8
VARS = 4
VAR_AT = HD
SEG_AT = VAR_AT + 3 * VARS
ONE_AT = SEG_AT + DOCS
VMEM = 60 * 1024 * 1024
FEWEST = 512
LAGS = (0, 1, 3, 5, 7, 8)
MESH = pl.DeviceIdType.MESH
WHOLE = pl.BlockSpec(memory_space=pltpu.VMEM)
SCALARS = pl.BlockSpec(memory_space=pltpu.SMEM)
ANYWHERE = pl.BlockSpec(memory_space=pl.ANY)
wide = jnp.float32
low = jnp.bfloat16


def params(**more):
    return pltpu.CompilerParams(vmem_limit_bytes=VMEM, **more)


def lanes_of(x):
    return lax.broadcasted_iota(jnp.int32, x.shape, x.ndim - 1)


def dot_nt(a, b):
    return lax.dot_general(a, b, (((1,), (1,)), ((), ())), preferred_element_type=wide)


def dot_tn(a, b):
    return lax.dot_general(a, b, (((0,), (0,)), ((), ())), preferred_element_type=wide)


def dot_nn(a, b):
    return jnp.dot(a, b, preferred_element_type=wide)


def left_pair(a, b):
    return jnp.where(lanes_of(a) < HD, a, pltpu.roll(b, HD, 1))


def right_pair(a, b):
    return jnp.where(lanes_of(a) < HD, pltpu.roll(a, HD, 1), b)


def swap_halves(x):
    return jnp.where(
        lanes_of(x) % HD < HD // 2,
        pltpu.roll(x, LANES - HD // 2, 1),
        pltpu.roll(x, HD // 2, 1),
    )


def head_mean(x):
    row = lax.broadcasted_iota(jnp.int32, (LANES, LANES), 0) // HD
    column = lax.broadcasted_iota(jnp.int32, (LANES, LANES), 1) // HD
    mix = jnp.where(row == column, 1.0 / HD, 0.0).astype(low)
    high = x.astype(low)
    return dot_nn(high, mix) + dot_nn((x - high.astype(wide)).astype(low), mix)


def features(ids, parts, table):
    index = lax.broadcasted_iota(jnp.int32, (IDS, LANES), 0)
    columns = []
    for part in range(parts):
        segs = jnp.broadcast_to(ids[part : part + 1], (IDS, LANES)).astype(jnp.int32)
        at = IDS // 2 + part
        variates = jnp.broadcast_to(ids[at : at + 1], (IDS, LANES)).astype(jnp.int32)
        by_variate = jnp.where(variates == index, 1.0, 0.0)
        by_document = jnp.where(segs == index - VARS, 1.0, 0.0)
        columns.append(
            jnp.where(index < VARS, by_variate, jnp.where(index < VARS + DOCS, by_document, 1.0))
        )
    return dot_tn(jnp.concatenate(columns, axis=1).astype(low), table)


def table_places():
    row = lax.broadcasted_iota(jnp.int32, (IDS, LANES), 0)
    lane = lax.broadcasted_iota(jnp.int32, (IDS, LANES), 1)
    return row, lane


def hot_variates(row, lane, values):
    kept = jnp.where((lane - VAR_AT) % VARS == row, values, 0.0)
    kept = jnp.where(lane < SEG_AT, kept, 0.0)
    kept = jnp.where(lane >= VAR_AT, kept, 0.0)
    return jnp.where(row < VARS, kept, 0.0)


def of_documents(row, lane, values):
    kept = jnp.where(row >= VARS, values, 0.0)
    kept = jnp.where(row < VARS + DOCS, kept, 0.0)
    kept = jnp.where(lane >= SEG_AT, kept, 0.0)
    return jnp.where(lane < ONE_AT, kept, 0.0)


def key_table():
    row, lane = table_places()
    table = hot_variates(row, lane, 1.0)
    table = table + of_documents(row, lane, jnp.where(lane - SEG_AT == row - VARS, 0.0, FAR))
    one = jnp.where(lane >= ONE_AT, jnp.where(lane < ONE_AT + 3, 1.0, 0.0), 0.0)
    return (table + jnp.where(row == VARS + DOCS, one, 0.0)).astype(low)


def query_table(step):
    row, lane = table_places()
    step = jnp.full((IDS, LANES), step, wide)
    high = step.astype(low).astype(wide)
    mid = (step - high).astype(low).astype(wide)
    part = (lane - VAR_AT) // VARS
    step = jnp.where(part == 0, high, jnp.where(part == 1, mid, step - high - mid))
    table = hot_variates(row, lane, step)
    table = table + of_documents(row, lane, jnp.where(lane - SEG_AT == row - VARS, 1.0, 0.0))
    return table.astype(low)


def double_gains(pair_ref, query_ref, key_ref):
    for side in range(2):
        span = slice(side * HD, (side + 1) * HD)
        pair_ref[0:1, span] = query_ref[...] * (LOG2E * HD**-0.5)
        pair_ref[1:2, span] = query_ref[...]
        pair_ref[2:3, span] = key_ref[...]


def project_kernel(
    tokens_ref, w_ref, gain_ref, query_gain_ref, key_gain_ref, cosine_ref, sine_ref, segs_ref, vars_ref,
    message_ref, query_ref, key_ref, normed_ref, pair_gain_ref, ids_ref,
):
    rows = tokens_ref.shape[0]
    parts = segs_ref.shape[0]

    @pl.when(pl.program_id(0) == 0)
    def norm():
        x = tokens_ref[...].astype(wide)
        scale = lax.rsqrt(jnp.mean(x * x, axis=1, keepdims=True) + EPSILON)
        normed_ref[...] = (x * scale * gain_ref[...]).astype(low)
        double_gains(pair_gain_ref, query_gain_ref, key_gain_ref)
        ids_ref[...] = jnp.zeros_like(ids_ref)
        ids_ref[:parts, :] = segs_ref[...].astype(wide)
        ids_ref[IDS // 2 : IDS // 2 + parts, :] = vars_ref[...].astype(wide)

    normed = normed_ref[...]

    def turned(raw, gain):
        x = raw * lax.rsqrt(head_mean(raw * raw) + EPSILON) * gain
        return x * cosine_ref[...] + swap_halves(x) * sine_ref[...]

    query_ref[...] = dot_nn(normed, w_ref[0])
    key_ref[...] = dot_nn(normed, w_ref[1])
    values = dot_nn(normed, w_ref[2])
    for pair in range(query_ref.shape[1] // LANES):
        span = slice(pair * LANES, (pair + 1) * LANES)
        one, two = 2 * pair, 2 * pair + 1
        query = turned(query_ref[:, span], pair_gain_ref[0:1])
        key = turned(key_ref[:, span], pair_gain_ref[2:3])
        value = values[:, span]
        message_ref[one, :rows] = left_pair(key, value).astype(low)
        message_ref[two, :rows] = right_pair(key, value).astype(low)
        upper, lower = query[: rows // 2], query[rows // 2 :]
        message_ref[one, rows + IDS :] = left_pair(upper, lower).astype(low)
        message_ref[two, rows + IDS :] = right_pair(upper, lower).astype(low)
        message_ref[one, rows : rows + IDS] = ids_ref[...].astype(low)
        message_ref[two, rows : rows + IDS] = ids_ref[...].astype(low)


def project(tokens, w_qkv, gain, query_gain, key_gain, cosine, sine, segs, variates):
    rows, depth = tokens.shape
    width = w_qkv.shape[2]
    size = rows + IDS + rows // 2
    wider = LANES * (1 + (width // LANES + 1) % 2)
    column = pl.BlockSpec((rows, wider), lambda i: (0, i))
    return pl.pallas_call(
        project_kernel,
        grid=(width // wider,),
        in_specs=[
            WHOLE,
            pl.BlockSpec((3, depth, wider), lambda i: (0, 0, i)),
            WHOLE, WHOLE, WHOLE, WHOLE, WHOLE, WHOLE, WHOLE,
        ],
        out_specs=(
            pl.BlockSpec((wider // HD, size, LANES), lambda i: (i, 0, 0)),
            column, column,
            pl.BlockSpec((rows, depth), lambda i: (0, 0)),
        ),
        out_shape=(
            jax.ShapeDtypeStruct((width // HD, size, LANES), low),
            jax.ShapeDtypeStruct((rows, width), wide),
            jax.ShapeDtypeStruct((rows, width), wide),
            jax.ShapeDtypeStruct((rows, depth), low),
        ),
        scratch_shapes=[pltpu.VMEM((8, LANES), wide), pltpu.VMEM((IDS, LANES), wide)],
        compiler_params=params(),
    )(tokens, w_qkv, gain, query_gain, key_gain, cosine, sine, segs, variates)


def walk(begin, end, body, largest):
    count = (end - begin) // LANES
    many = largest // LANES

    def step(index, carry):
        body(begin + index * largest, largest)
        return carry

    lax.fori_loop(0, count // many, step, 0)
    size = many // 2
    while size:
        piece = size * LANES
        at = begin + (count // (2 * size)) * (2 * piece)

        @pl.when((count // size) % 2 == 1)
        def rest(at=at, piece=piece):
            body(at, piece)

        size //= 2


def scalar(x):
    return x[0, 0].astype(jnp.int32)


def forward_kernel(
    bias_ref, kv_ref, query_in_ref,
    k_ref, v_ref, q_ref, exact_ref, message_ref, runs_ref, acc_ref, seg_ref, upto_ref, keys_ref,
):
    ranks, heads = kv_ref.shape[:2]
    rows = q_ref.shape[0]
    half = rows // 2
    parts = rows // LANES
    block = pl.program_id(0)
    place = lax.axis_index("dp")
    rank = lax.rem(place, ranks)
    head = place // ranks
    filled = lax.broadcasted_iota(jnp.int32, (IDS // 2, LANES), 0) < parts

    @pl.when(block == 0)
    def prepare():
        keys = key_table()
        for rank_at in range(ranks):
            for head_at in range(heads):
                at = head_at * ranks + rank_at
                ids = kv_ref[rank_at, head_at, rows:, :].astype(wide)
                seg_ref[at] = jnp.where(filled, ids[: IDS // 2], DOCS + 1.0)
                extra = features(ids, parts, keys)
                kv = kv_ref[rank_at, head_at, :rows].astype(wide)
                lane = lanes_of(kv)
                span = pl.ds(at * rows, rows)
                k_ref[span, :] = jnp.where(lane < HD, kv, extra).astype(low)
                one = jnp.where(lane < HD + 3, 1.0, 0.0)
                v_ref[span, :] = jnp.where(lane < HD, pltpu.roll(kv, HD, 1), one).astype(low)
        every = seg_ref[...].reshape(ranks * heads * (IDS // 2), LANES)
        own = jnp.stack([seg_ref[head_at * ranks + rank] for head_at in range(heads)])
        own = own.reshape(heads * (IDS // 2), LANES)
        upto_ref[0, 0] = 0
        upto_ref[1, 0] = 0
        for document in range(DOCS):
            for which, segs in ((0, every), (1, own)):
                count = jnp.sum(jnp.where(segs <= document, 1.0, 0.0), keepdims=True)
                upto_ref[which, document + 1] = scalar(count)
        for at in range(ranks * heads):
            segs = seg_ref[at]
            first = scalar(segs[:1, :1])
            last = scalar(segs[parts - 1 : parts, LANES - 1 :])
            keys_ref[0, at] = upto_ref[0, first] // LANES * LANES
            keys_ref[1, at] = (upto_ref[0, last + 1] + LANES - 1) // LANES * LANES
            runs_ref[0, at] = upto_ref[1, first] // LANES * LANES
            runs_ref[1, at] = (upto_ref[1, last + 1] + LANES - 1) // LANES * LANES

    begin = keys_ref[0, block * ranks + rank]
    end = keys_ref[1, block * ranks + rank]
    queries = query_table((bias_ref[0, head] - bias_ref[1, head]) * LOG2E)
    ids = kv_ref[rank, block, pl.ds(rows, IDS), :].astype(wide)
    extra = features(ids, parts, queries)
    folded = query_in_ref[0].astype(wide)
    head_part = jnp.concatenate([folded, pltpu.roll(folded, HD, 1)], axis=0)
    q_ref[...] = jnp.where(lanes_of(extra) < HD, head_part, extra).astype(low)
    acc_ref[...] = jnp.zeros_like(acc_ref)

    def step(start, size):
        span = pl.ds(pl.multiple_of(start, LANES), size)
        probs = jnp.exp2(dot_nt(q_ref[...], k_ref[span, :])).astype(low)
        acc_ref[...] += dot_nn(probs, v_ref[span, :])

    walk(begin, end, step, 4096)
    total = acc_ref[...]
    row_sum = total[:, HD : HD + 1]
    exact = total / row_sum
    exact_ref[...] = jnp.where(lanes_of(total) < HD, exact, jnp.log2(row_sum))
    message_ref[0] = left_pair(exact[:half], exact[half:]).astype(low)


def forward_attention(bias, kv, query):
    ranks, heads, size = kv.shape[:3]
    rows = size - IDS
    every = ranks * heads * rows
    part = pl.BlockSpec((rows, LANES), lambda i: (i, 0))
    fold = pl.BlockSpec((1, rows // 2, LANES), lambda i: (i, 0, 0))
    return pl.pallas_call(
        forward_kernel,
        grid=(heads,),
        in_specs=[SCALARS, WHOLE, fold],
        out_specs=(WHOLE, WHOLE, part, part, fold, SCALARS),
        scratch_shapes=[
            pltpu.VMEM((rows, LANES), wide),
            pltpu.VMEM((ranks * heads, IDS // 2, LANES), wide),
            pltpu.SMEM((2, DOCS + 1), jnp.int32),
            pltpu.SMEM((2, ranks * heads), jnp.int32),
        ],
        out_shape=(
            jax.ShapeDtypeStruct((every, LANES), low),
            jax.ShapeDtypeStruct((every, LANES), low),
            jax.ShapeDtypeStruct((heads * rows, LANES), low),
            jax.ShapeDtypeStruct((heads * rows, LANES), wide),
            jax.ShapeDtypeStruct((heads, rows // 2, LANES), low),
            jax.ShapeDtypeStruct((2, ranks * heads), jnp.int32),
        ),
        compiler_params=params(),
    )(bias, kv, query)


def split_lanes(column, lane, at):
    high = column.astype(low).astype(wide)
    mid = (column - high).astype(low).astype(wide)
    parts = jnp.where(lane == at, high, jnp.where(lane == at + 1, mid, column - high - mid))
    return jnp.where(lane < at + 3, parts, 0.0)


def backward_kernel(
    runs_ref, k_ref, v_ref, q_in_ref, exact_ref, grad_in_ref, ids_ref,
    kv_ref, message_ref, bias_ref, q_ref, g_ref, kt_ref, dk_ref, dv_ref, dq_ref,
):
    heads, half = grad_in_ref.shape[:2]
    rows = 2 * half
    block = pl.program_id(0)

    @pl.when(block == 0)
    def prepare():
        dq_ref[...] = jnp.zeros_like(dq_ref)
        for head_at in range(heads):
            folded = grad_in_ref[head_at].astype(wide)
            for side in range(2):
                span = pl.ds(head_at * rows + side * half, half)
                grad = folded if side == 0 else pltpu.roll(folded, HD, 1)
                lane = lanes_of(grad)
                grad = jnp.where(lane < HD, grad, 0.0)
                exact = exact_ref[span, :]
                delta = jnp.sum(grad * exact, axis=1, keepdims=True)
                g_ref[span, :] = jnp.where(lane < HD, grad, split_lanes(-delta, lane, HD)).astype(low)
                query = q_in_ref[span, :].astype(wide)
                total = split_lanes(-exact[:, HD : HD + 1], lane, ONE_AT)
                q_ref[span, :] = jnp.where(lane < ONE_AT, query, total).astype(low)

    dk_ref[...] = jnp.zeros_like(dk_ref)
    dv_ref[...] = jnp.zeros_like(dv_ref)
    key = k_ref[...]
    value = v_ref[...]
    kt_ref[...] = key.astype(wide).T.astype(low)

    def step(start, size):
        span = pl.ds(pl.multiple_of(start, LANES), size)
        query = q_ref[span, :]
        grad = g_ref[span, :]
        probs = jnp.exp2(dot_nt(key, query))
        grad_scores = (probs * dot_nt(value, grad)).astype(low)
        dv_ref[...] += dot_nn(probs.astype(low), grad)
        dk_ref[...] += dot_nn(grad_scores, query)
        dq_ref[:, span] += dot_nn(kt_ref[...], grad_scores)

    walk(runs_ref[0, block], runs_ref[1, block], step, 2048)
    kv_ref[0, 0] = left_pair(dk_ref[...] * (1.0 / LOG2E), dv_ref[...]).astype(low)

    @pl.when(block == pl.num_programs(0) - 1)
    def finish():
        same = jnp.zeros((8, LANES), wide)
        every = jnp.zeros((8, LANES), wide)
        index = lax.broadcasted_iota(jnp.int32, (8, LANES), 0)
        for head_at in range(heads):
            ids = ids_ref[head_at].astype(wide)
            for part in range(rows // LANES):
                at = head_at * rows + part * LANES
                by_variate = jnp.where(index < VARS, dq_ref[VAR_AT : VAR_AT + 8, at : at + LANES], 0.0)
                variates = jnp.broadcast_to(
                    ids[IDS // 2 + part : IDS // 2 + part + 1], (8, LANES)
                ).astype(jnp.int32)
                same = same + jnp.where(variates == index, by_variate, 0.0)
                every = every + by_variate
            span = dq_ref[:, head_at * rows : (head_at + 1) * rows].T * HD**-0.5
            message_ref[head_at] = left_pair(span[:half], span[half:]).astype(low)
        bias_ref[0] = same
        bias_ref[1] = every - same


def backward_attention(runs, key, value, query, exact, grad, ids):
    every = key.shape[0]
    heads, half = grad.shape[:2]
    rows = 2 * half
    ranks = every // (heads * rows)
    part = pl.BlockSpec((rows, LANES), lambda i, *_: (i, 0))
    return pl.pallas_call(
        backward_kernel,
        grid_spec=pltpu.PrefetchScalarGridSpec(
            num_scalar_prefetch=1,
            grid=(ranks * heads,),
            in_specs=[part, part, WHOLE, WHOLE, WHOLE, WHOLE],
            out_specs=(
                pl.BlockSpec((1, 1, rows, LANES), lambda i, *_: (i % ranks, i // ranks, 0, 0)),
                WHOLE,
                WHOLE,
            ),
            scratch_shapes=[
                pltpu.VMEM((heads * rows, LANES), low),
                pltpu.VMEM((heads * rows, LANES), low),
                pltpu.VMEM((LANES, rows), low),
                pltpu.VMEM((rows, LANES), wide),
                pltpu.VMEM((rows, LANES), wide),
                pltpu.VMEM((LANES, heads * rows), wide),
            ],
        ),
        out_shape=(
            jax.ShapeDtypeStruct((ranks, heads, rows, LANES), low),
            jax.ShapeDtypeStruct((heads, half, LANES), low),
            jax.ShapeDtypeStruct((2, 8, LANES), wide),
        ),
        compiler_params=params(),
    )(runs, key, value, query, exact, grad, ids)


def columns_of(width):
    if width % LANES:
        return [(0, width)]
    return [(at, min(4 * LANES, width - at)) for at in range(0, width, 4 * LANES)]


def mlp_kernel(
    landed_ref, tokens_ref, cotangent_ref, gain_ref, own_out_ref, other_out_ref, gateup_ref, down_ref,
    heads_ref, middle_ref, normed_ref, hidden_ref, grad_gu_ref, part_ref, part_low_ref, gain_part_ref,
    others_ref, gateup_in, down_in, sums_ref, copied,
):
    tensor, heads, half = landed_ref.shape[:3]
    copies = [
        pltpu.make_async_copy(gateup_ref, gateup_in, copied.at[0]),
        pltpu.make_async_copy(down_ref, down_in, copied.at[1]),
    ]
    for copy in copies:
        copy.start()
    for share in range(tensor):
        to_ref = others_ref if share else heads_ref
        for pair in range(heads // 2):
            one = landed_ref[share, 2 * pair].astype(wide)
            two = landed_ref[share, 2 * pair + 1].astype(wide)
            span = pl.ds(pair * LANES, LANES)
            to_ref[:half, span] = left_pair(one, two).astype(low)
            to_ref[half:, span] = right_pair(one, two).astype(low)
        if share:
            middle_ref[...] += dot_nn(to_ref[...], other_out_ref[share - 1])
        else:
            middle_ref[...] = tokens_ref[...].astype(wide) + dot_nn(to_ref[...], own_out_ref[...])

    def unit_and_scale():
        middle = middle_ref[...]
        scale = lax.rsqrt(jnp.mean(middle * middle, axis=1, keepdims=True) + EPSILON)
        return middle * scale, scale

    normed_ref[...] = (unit_and_scale()[0] * gain_ref[...]).astype(low)
    for copy in copies:
        copy.wait()
    sums_ref[...] = jnp.zeros_like(sums_ref)
    for at, size in columns_of(hidden_ref.shape[1]):
        span = slice(at, at + size)
        w_gate = gateup_in[0, :, span]
        w_up = gateup_in[1, :, span]
        gate = dot_nn(normed_ref[...], w_gate)
        up = dot_nn(normed_ref[...], w_up)
        grad = dot_nt(cotangent_ref[...], down_in[span, :])
        sigmoid = 1.0 / (1.0 + jnp.exp(-gate))
        active = gate * sigmoid
        hidden_ref[:, span] = (active * up).astype(low)
        grad_gate = (grad * up * sigmoid * (1.0 + gate * (1.0 - sigmoid))).astype(low)
        grad_up = (grad * active).astype(low)
        grad_gu_ref[0, :, span] = grad_gate
        grad_gu_ref[1, :, span] = grad_up
        sums_ref[...] += dot_nt(grad_gate, w_gate) + dot_nt(grad_up, w_up)
    unit, scale = unit_and_scale()
    sums = sums_ref[...]
    gain_part = jnp.sum(sums * unit, axis=0, keepdims=True)
    for row in range(gain_part_ref.shape[0]):
        gain_part_ref[row : row + 1, :] = gain_part[:, row * LANES : (row + 1) * LANES]
    scaled = sums * gain_ref[...]
    part = scale * (scaled - unit * jnp.mean(scaled * unit, axis=1, keepdims=True))
    part_ref[...] = part
    part_low_ref[...] = part.astype(low)


def out_and_mlp(landed, tokens, cotangent, gain, w_out, w_others, w_gateup, w_down):
    tensor, heads, half = landed.shape[:3]
    rows, depth = tokens.shape
    width, units = heads * HD, w_down.shape[0]
    shape = jax.ShapeDtypeStruct
    return pl.pallas_call(
        mlp_kernel,
        in_specs=[WHOLE] * 6 + [ANYWHERE] * 2,
        out_specs=(WHOLE,) * 8,
        out_shape=(
            shape((rows, width), low),
            shape((rows, depth), wide),
            shape((rows, depth), low),
            shape((rows, units), low),
            shape((2, rows, units), low),
            shape((rows, depth), wide),
            shape((rows, depth), low),
            shape((depth // LANES, LANES), wide),
        ),
        scratch_shapes=[
            pltpu.VMEM((rows, width), low),
            pltpu.VMEM(w_gateup.shape, low),
            pltpu.VMEM(w_down.shape, low),
            pltpu.VMEM((rows, depth), wide),
            pltpu.SemaphoreType.DMA((2,)),
        ],
        compiler_params=params(),
    )(landed, tokens, cotangent, gain, w_out, w_others, w_gateup, w_down)


def grad_heads_kernel(grad_ref, w_ref, message_ref):
    half = message_ref.shape[1]
    for pair in range(message_ref.shape[0] // 2):
        both = dot_nt(grad_ref[...], w_ref[pair * LANES : (pair + 1) * LANES, :])
        message_ref[2 * pair] = left_pair(both[:half], both[half:]).astype(low)
        message_ref[2 * pair + 1] = right_pair(both[:half], both[half:]).astype(low)


def grad_heads_of(grad, w_out):
    return pl.pallas_call(
        grad_heads_kernel,
        in_specs=[WHOLE, WHOLE],
        out_specs=WHOLE,
        out_shape=jax.ShapeDtypeStruct((w_out.shape[0] // HD, grad.shape[0] // 2, LANES), low),
        compiler_params=params(),
    )(grad, w_out)


def tail_kernel(
    landed_ref, query_ref, key_ref, query_gain_ref, key_gain_ref, cosine_ref, sine_ref, tokens_ref, gain_ref,
    normed_ref, w_ref, mlp_gain_ref, bias_ref,
    grad_qkv_ref, input_ref, small_ref, grad_ref, pair_gain_ref, *, every_head,
):
    double_gains(pair_gain_ref, query_gain_ref, key_gain_ref)
    rows, width = query_ref.shape
    depth = tokens_ref.shape[1]

    def back(turned, raw, gain):
        grad = turned * cosine_ref[...] - swap_halves(turned) * sine_ref[...]
        scale = lax.rsqrt(head_mean(raw * raw) + EPSILON)
        unit = raw * scale
        scaled = grad * gain
        part = jnp.sum(grad * unit, axis=0, keepdims=True)
        return (scale * (scaled - unit * head_mean(scaled * unit))).astype(low), part

    query_part = jnp.zeros((1, LANES), wide)
    key_part = jnp.zeros((1, LANES), wide)
    for pair in range(width // LANES):
        span = slice(pair * LANES, (pair + 1) * LANES)
        key_one = landed_ref[2 * pair, :rows].astype(wide)
        key_two = landed_ref[2 * pair + 1, :rows].astype(wide)
        query_one = landed_ref[2 * pair, rows:].astype(wide)
        query_two = landed_ref[2 * pair + 1, rows:].astype(wide)
        query = jnp.concatenate(
            [left_pair(query_one, query_two), right_pair(query_one, query_two)], axis=0
        )
        grad_ref[0, :, span], part = back(query, query_ref[:, span], pair_gain_ref[1:2])
        query_part = query_part + part
        grad_ref[1, :, span], part = back(
            left_pair(key_one, key_two), key_ref[:, span], pair_gain_ref[2:3]
        )
        key_part = key_part + part
        grad_ref[2, :, span] = right_pair(key_one, key_two).astype(low)
    sums = dot_nt(grad_ref[0], w_ref[0]) + dot_nt(grad_ref[1], w_ref[1])
    sums = sums + dot_nt(grad_ref[2], w_ref[2])
    x = tokens_ref[...].astype(wide)
    scale = lax.rsqrt(jnp.mean(x * x, axis=1, keepdims=True) + EPSILON)
    unit = x * scale
    gain_part = jnp.sum(sums * unit, axis=0, keepdims=True)
    scaled = sums * gain_ref[...]
    part = scale * (scaled - unit * jnp.mean(scaled * unit, axis=1, keepdims=True))
    input_ref[...] = part.astype(low)
    for index in range(3):
        grad_qkv_ref[index] = dot_nn(normed_ref[...], grad_ref[index]).astype(low)
    count = depth // LANES
    small_ref[...] = jnp.zeros_like(small_ref)
    for row in range(count):
        small_ref[row : row + 1, :] = gain_part[:, row * LANES : (row + 1) * LANES]
    small_ref[count : 2 * count, :] = mlp_gain_ref[...]
    small_ref[2 * count : 2 * count + 1, :] = query_part
    small_ref[2 * count + 1 : 2 * count + 2, :] = key_part
    head = lax.axis_index("tensor") * (width // HD) + lax.axis_index("dp") // every_head
    lane = lax.broadcasted_iota(jnp.int32, (1, LANES), 1)
    for row in range(2):
        total = jnp.sum(bias_ref[row], keepdims=True)
        at = 2 * count + 2 + row
        small_ref[at : at + 1, :] = jnp.where(lane == head, total, 0.0)


def tail(
    landed, raw_query, raw_key, query_gain, key_gain, cosine, sine, tokens, gain, normed_turned,
    w_qkv, mlp_gain_part, bias_tiles, ranks,
):
    rows, width = raw_query.shape
    depth = tokens.shape[1]
    small = -(-(2 * depth // LANES + 4) // 8) * 8
    return pl.pallas_call(
        functools.partial(tail_kernel, every_head=ranks),
        in_specs=[WHOLE] * 13,
        out_specs=(WHOLE,) * 3,
        out_shape=(
            jax.ShapeDtypeStruct((3, depth, width), low),
            jax.ShapeDtypeStruct((rows, depth), low),
            jax.ShapeDtypeStruct((small, LANES), wide),
        ),
        scratch_shapes=[pltpu.VMEM((3, rows, width), low), pltpu.VMEM((8, LANES), wide)],
        compiler_params=params(),
    )(
        landed, raw_query, raw_key, query_gain, key_gain, cosine, sine, tokens, gain, normed_turned,
        w_qkv, mlp_gain_part, bias_tiles,
    )


def widen_kernel(*refs):
    half = len(refs) // 2
    for source, target in zip(refs[:half], refs[half:]):
        target[...] = source[...].astype(wide)


def widen(arrays):
    steps = 8
    while any(a.shape[0] % (16 * steps) for a in arrays):
        steps //= 2
    specs = [pl.BlockSpec((a.shape[0] // steps, a.shape[1]), lambda i: (i, 0)) for a in arrays]
    return pl.pallas_call(
        widen_kernel,
        grid=(steps,),
        in_specs=specs,
        out_specs=tuple(specs),
        out_shape=tuple(jax.ShapeDtypeStruct(a.shape, wide) for a in arrays),
        compiler_params=params(),
    )(*arrays)


def remote(src, dst, send, recv, place):
    return pltpu.make_async_remote_copy(
        src_ref=src, dst_ref=dst, send_sem=send, recv_sem=recv,
        device_id={"dp": place}, device_id_type=MESH,
    )


def peer(head, step, heads):
    if heads & (heads - 1):
        return lax.rem(head + step, heads)
    to = 0
    bit = 1
    while bit < heads:
        mine = lax.rem(head // bit, 2)
        to = to + bit * (1 - mine if step & bit else mine)
        bit *= 2
    return to


def origin(head, step, heads):
    if heads & (heads - 1):
        return lax.rem(head + heads - step, heads)
    return peer(head, step, heads)


def greet(heads, ranks, head, rank, with_ranks, tensor=1):
    barrier = pltpu.get_barrier_semaphore()
    for step in range(1, tensor):
        side = lax.rem(lax.axis_index("tensor") + step, tensor)
        pl.semaphore_signal(barrier, inc=1, device_id={"tensor": side}, device_id_type=MESH)
    for step in range(1, heads):
        place = peer(head, step, heads) * ranks + rank
        pl.semaphore_signal(barrier, inc=1, device_id={"dp": place}, device_id_type=MESH)
    if with_ranks:
        for step in range(1, ranks):
            place = head * ranks + lax.rem(rank + step, ranks)
            pl.semaphore_signal(barrier, inc=1, device_id={"dp": place}, device_id_type=MESH)
    pl.semaphore_wait(barrier, heads + tensor - 2 + (ranks - 1 if with_ranks else 0))


def spread_kernel(
    message_ref, w_ref, kv_ref, query_ref, others_ref,
    send_a, recv_a, send_b, recv_b, send_f, recv_f, send_w, recv_w, local, *, ranks
):
    heads = message_ref.shape[0]
    tensor = others_ref.shape[0] + 1
    side = lax.axis_index("tensor")
    size = kv_ref.shape[2]
    rest = query_ref.shape[1]
    place = lax.axis_index("dp")
    head = place // ranks
    rank = lax.rem(place, ranks)
    greet(heads, ranks, head, rank, True, tensor)
    onward = []
    for step in range(1, tensor):
        copy = pltpu.make_async_remote_copy(
            src_ref=w_ref, dst_ref=others_ref.at[tensor - step - 1],
            send_sem=send_w.at[step], recv_sem=recv_w.at[step],
            device_id={"tensor": lax.rem(side + step, tensor)}, device_id_type=MESH,
        )
        copy.start()
        onward.append(copy)
    firsts = {}
    for step in reversed(range(1, heads)):
        to = peer(head, step, heads)
        at = to * ranks + rank
        first = remote(
            message_ref.at[to, pl.ds(0, size)], kv_ref.at[rank, head],
            send_a.at[step], recv_a.at[step], at,
        )
        second = remote(
            message_ref.at[to, pl.ds(size, rest)], query_ref.at[head],
            send_b.at[step], recv_b.at[step], at,
        )
        first.start()
        second.start()
        firsts[step] = (first, second)
    mine = [
        pltpu.make_async_copy(message_ref.at[head, pl.ds(0, size)], kv_ref.at[rank, head], local.at[0]),
        pltpu.make_async_copy(message_ref.at[head, pl.ds(size, rest)], query_ref.at[head], local.at[1]),
    ]
    for copy in mine:
        copy.start()

    def forward(step, source, src):
        for other in range(1, ranks):
            copy = remote(
                src, kv_ref.at[rank, source], send_f.at[step, other], recv_f.at[step, other],
                head * ranks + lax.rem(rank + other, ranks),
            )
            copy.start()
            onward.append(copy)

    forward(0, head, message_ref.at[head, pl.ds(0, size)])
    for step in reversed(range(1, heads)):
        source = origin(head, step, heads)
        firsts[step][0].wait_recv()
        forward(step, source, kv_ref.at[rank, source])
    for first, second in firsts.values():
        first.wait_send()
        second.wait()
    for copy in mine + onward:
        copy.wait()


def spread(message, w_out, ranks, rows, tensor):
    heads, size = message.shape[:2]
    dma = pltpu.SemaphoreType.DMA
    return pl.pallas_call(
        functools.partial(spread_kernel, ranks=ranks),
        in_specs=[ANYWHERE] * 2,
        out_specs=(ANYWHERE,) * 3,
        out_shape=(
            jax.ShapeDtypeStruct((ranks, heads, rows + IDS, LANES), low),
            jax.ShapeDtypeStruct((heads, rows // 2, LANES), low),
            jax.ShapeDtypeStruct((tensor - 1,) + w_out.shape, low),
        ),
        scratch_shapes=[dma((heads,))] * 4 + [dma((heads, ranks))] * 2 + [dma((tensor,))] * 2 + [dma((2,))],
        compiler_params=params(collective_id=0, has_side_effects=True),
    )(message, w_out)


def send_shares(part_ref, shares_ref, send, recv):
    tensor, _, share = shares_ref.shape
    tensor += 1
    side = lax.axis_index("tensor")
    copies = []
    for step in range(1, tensor):
        to = lax.rem(side + step, tensor)
        copies.append(
            pltpu.make_async_remote_copy(
                src_ref=part_ref.at[:, pl.ds(pl.multiple_of(to * share, LANES), share)],
                dst_ref=shares_ref.at[tensor - step - 1],
                send_sem=send.at[step], recv_sem=recv.at[step],
                device_id={"tensor": to}, device_id_type=MESH,
            )
        )
        copies[-1].start()
    return copies


def exchange_kernel(
    message_ref, part_ref, landed_ref, shares_ref, send, recv, send_t, recv_t, local, *, ranks
):
    heads = message_ref.shape[0]
    place = lax.axis_index("dp")
    head = place // ranks
    rank = lax.rem(place, ranks)
    greet(heads, ranks, head, rank, False, shares_ref.shape[0] + 1)
    copies = []
    for step in reversed(range(1, heads)):
        to = peer(head, step, heads)
        copies.append(
            remote(
                message_ref.at[to], landed_ref.at[head], send.at[step], recv.at[step],
                to * ranks + rank,
            )
        )
        copies[-1].start()
    copies.append(pltpu.make_async_copy(message_ref.at[head], landed_ref.at[head], local))
    copies[-1].start()
    copies += send_shares(part_ref, shares_ref, send_t, recv_t)
    for copy in copies:
        copy.wait()


def exchange(message, part, ranks, tensor):
    heads = message.shape[0]
    rows, depth = part.shape
    dma = pltpu.SemaphoreType.DMA
    return pl.pallas_call(
        functools.partial(exchange_kernel, ranks=ranks),
        in_specs=[ANYWHERE] * 2,
        out_specs=(ANYWHERE,) * 2,
        out_shape=(
            jax.ShapeDtypeStruct(message.shape, message.dtype),
            jax.ShapeDtypeStruct((tensor - 1, rows, depth // tensor), low),
        ),
        scratch_shapes=[dma((heads,))] * 2 + [dma((tensor,))] * 2 + [dma],
        compiler_params=params(collective_id=2, has_side_effects=True),
    )(message, part)


def share_out_kernel(message_ref, landed_ref, send, recv, send_t, recv_t, local, *, ranks, tensor):
    heads = message_ref.shape[0]
    place = lax.axis_index("dp")
    side = lax.axis_index("tensor")
    head = place // ranks
    rank = lax.rem(place, ranks)
    barrier = pltpu.get_barrier_semaphore()
    for step in range(1, tensor):
        to = lax.rem(side + step, tensor)
        pl.semaphore_signal(barrier, inc=1, device_id={"tensor": to}, device_id_type=MESH)
    for step in range(1, heads):
        to = peer(head, step, heads) * ranks + rank
        pl.semaphore_signal(barrier, inc=1, device_id={"dp": to}, device_id_type=MESH)
    pl.semaphore_wait(barrier, heads + tensor - 2)
    copies = []
    for step in range(1, heads):
        to = peer(head, step, heads)
        copies.append(
            remote(
                message_ref.at[to], landed_ref.at[0, head], send.at[step], recv.at[step],
                to * ranks + rank,
            )
        )
        copies[-1].start()
    mine = pltpu.make_async_copy(message_ref.at[head], landed_ref.at[0, head], local)
    mine.start()
    onward = []

    def relay(step, source, src):
        for other in range(1, tensor):
            copy = pltpu.make_async_remote_copy(
                src_ref=src, dst_ref=landed_ref.at[tensor - other, source],
                send_sem=send_t.at[step, other], recv_sem=recv_t.at[step, other],
                device_id={"tensor": lax.rem(side + other, tensor)}, device_id_type=MESH,
            )
            copy.start()
            onward.append(copy)

    relay(0, head, message_ref.at[head])
    for step in range(1, heads):
        source = origin(head, step, heads)
        copies[step - 1].wait_recv()
        relay(step, source, landed_ref.at[0, source])
    for copy in copies:
        copy.wait_send()
    mine.wait()
    for copy in onward:
        copy.wait()


def share_out(message, ranks, tensor):
    heads = message.shape[0]
    dma = pltpu.SemaphoreType.DMA
    return pl.pallas_call(
        functools.partial(share_out_kernel, ranks=ranks, tensor=tensor),
        in_specs=[ANYWHERE],
        out_specs=ANYWHERE,
        out_shape=jax.ShapeDtypeStruct((tensor,) + message.shape, message.dtype),
        scratch_shapes=[dma((heads,))] * 2 + [dma((heads, tensor))] * 2 + [dma],
        compiler_params=params(collective_id=1, has_side_effects=True),
    )(message)


def total_kernel(*refs, arrays, chunks, zs, tensor):
    ins, part_ref, refs = refs[: arrays + 1], refs[arrays + 1], refs[arrays + 2 :]
    outs, shares_ref, refs = refs[: arrays + 1], refs[arrays + 1], refs[arrays + 2 :]
    count = len(chunks)
    scratch, refs = refs[: 5 * count], refs[5 * count :]
    near_ref, far_ref, line_ref, side_ref, send, recv, send_z, recv_z, send_s, recv_s, send_t, recv_t = refs
    place = lax.axis_index("dp")
    side = lax.axis_index("tensor")
    core = lax.rem(place, 2)
    x = lax.rem(place // 2, 2)
    z = place // 4
    base = place - core
    core_mate = base + 1 - core
    x_mate = z * 4 + (1 - x) * 2 + core
    z_mates = [lax.rem(z + step, zs) * 4 + x * 2 + core for step in range(1, zs)]

    barrier = pltpu.get_barrier_semaphore()
    for to in [core_mate, x_mate] + z_mates:
        pl.semaphore_signal(barrier, inc=1, device_id={"dp": to}, device_id_type=MESH)
    for step in range(1, tensor):
        to = lax.rem(side + step, tensor)
        pl.semaphore_signal(barrier, inc=1, device_id={"tensor": to}, device_id_type=MESH)
    pl.semaphore_wait(barrier, zs + tensor)
    shares = send_shares(part_ref, shares_ref, send_t, recv_t)
    sent = []
    waits = {}

    def rows_at(at, size):
        return pl.ds(pl.multiple_of(at, 16), size)

    def pieces(chunk):
        index, lead, begin, size = chunks[chunk]
        source = ins[index] if lead is None else ins[index].at[lead]
        target = outs[index] if lead is None else outs[index].at[lead]
        source, target = (ref.at[pl.ds(begin, size)] for ref in (source, target))
        return source, target, size, scratch[5 * chunk : 5 * chunk + 5]

    def go(copy, key):
        copy.start()
        sent.append(copy)
        waits.setdefault(key, []).append(copy)

    def arrived(key):
        for copy in waits[key]:
            copy.wait_recv()

    def halve_core(chunk):
        source, _, size, (first, _, _, _, _) = pieces(chunk)
        go(
            remote(
                source.at[rows_at((1 - core) * (size // 2), size // 2)], first,
                send.at[chunk, 0], recv.at[chunk, 0], core_mate,
            ),
            (chunk, 0),
        )

    def halve_x(chunk):
        source, _, size, (first, half, second, _, _) = pieces(chunk)
        arrived((chunk, 0))
        mine = source[rows_at(core * (size // 2), size // 2), :].astype(wide)
        half[...] = (mine + first[...].astype(wide)).astype(low)
        go(
            remote(
                half.at[rows_at((1 - x) * (size // 4), size // 4)], second,
                send.at[chunk, 1], recv.at[chunk, 1], x_mate,
            ),
            (chunk, 1),
        )

    def part_z(chunk):
        _, _, size, (_, half, second, quarter, third) = pieces(chunk)
        arrived((chunk, 1))
        mine = half[rows_at(x * (size // 4), size // 4), :].astype(wide)
        quarter[...] = (mine + second[...].astype(wide)).astype(low)
        part = size // (4 * zs)
        for step in range(1, zs):
            to = lax.rem(z + step, zs)
            go(
                remote(
                    quarter.at[rows_at(to * part, part)], third.at[step],
                    send_z.at[chunk, 0, step], recv_z.at[chunk, 0, step], z_mates[step - 1],
                ),
                (chunk, 2),
            )

    def spread_z(chunk):
        _, target, size, (_, _, _, quarter, third) = pieces(chunk)
        arrived((chunk, 2))
        part = size // (4 * zs)
        total = quarter[rows_at(z * part, part), :].astype(wide)
        for step in range(1, zs):
            total = total + third[step].astype(wide)
        span = rows_at(core * (size // 2) + x * (size // 4) + z * part, part)
        target[span, :] = total.astype(low)
        for step in range(1, zs):
            go(
                remote(
                    target.at[span], target.at[span],
                    send_z.at[chunk, 1, step], recv_z.at[chunk, 1, step], z_mates[step - 1],
                ),
                (chunk, 3),
            )

    def spread_x(chunk):
        _, target, size, _ = pieces(chunk)
        arrived((chunk, 3))
        span = rows_at(core * (size // 2) + x * (size // 4), size // 4)
        go(
            remote(target.at[span], target.at[span], send.at[chunk, 2], recv.at[chunk, 2], x_mate),
            (chunk, 4),
        )

    def spread_core(chunk):
        _, target, size, _ = pieces(chunk)
        arrived((chunk, 4))
        span = rows_at(core * (size // 2), size // 2)
        go(
            remote(target.at[span], target.at[span], send.at[chunk, 3], recv.at[chunk, 3], core_mate),
            (chunk, 5),
        )

    small = ins[arrays]

    def small_core():
        near_ref[0] = small[...]
        go(remote(near_ref.at[0], near_ref.at[1], send_s.at[0, 0], recv_s.at[0, 0], core_mate), "c")

    def small_x():
        arrived("c")
        far_ref[0] = near_ref[0] + near_ref[1]
        go(remote(far_ref.at[0], far_ref.at[1], send_s.at[1, 0], recv_s.at[1, 0], x_mate), "x")

    def small_z():
        arrived("x")
        line_ref[z] = far_ref[0] + far_ref[1]
        for step in range(1, zs):
            go(
                remote(
                    line_ref.at[z], line_ref.at[z], send_s.at[2, step], recv_s.at[2, step],
                    z_mates[step - 1],
                ),
                "z",
            )

    def small_side():
        arrived("z")
        total = line_ref[0]
        for at in range(1, zs):
            total = total + line_ref[at]
        side_ref[side] = total
        for step in range(1, tensor):
            copy = pltpu.make_async_remote_copy(
                src_ref=side_ref.at[side], dst_ref=side_ref.at[side],
                send_sem=send_s.at[3, step], recv_sem=recv_s.at[3, step],
                device_id={"tensor": lax.rem(side + step, tensor)}, device_id_type=MESH,
            )
            go(copy, "s")

    def small_end():
        if tensor > 1:
            arrived("s")
        total = side_ref[0]
        for at in range(1, tensor):
            total = total + side_ref[at]
        outs[arrays][...] = total

    stages = [halve_core, halve_x, part_z, spread_z, spread_x, spread_core]
    smalls = [small_core, small_x, small_z, small_side, small_end]
    for tick in range(max(count + LAGS[-1], len(smalls))):
        for stage in range(len(stages)):
            if 0 <= tick - LAGS[stage] < count:
                stages[stage](tick - LAGS[stage])
        if tick < len(smalls):
            smalls[tick]()
    for chunk in range(count):
        arrived((chunk, 5))
    for copy in sent:
        copy.wait_send()
    for copy in shares:
        copy.wait()


def total_sums(arrays, small, part, dp, tensor):
    zs = dp // 4
    chunks = []
    scratch = []
    for index, array in enumerate(arrays):
        leads = [None] if array.ndim == 2 else list(range(array.shape[0]))
        size, width = array.shape[-2:]
        total, size = size, min(size, max(64 * zs, FEWEST))
        for lead, begin in [(a, b) for a in leads for b in range(0, total, size)]:
            chunks.append((index, lead, begin, size))
            scratch += [
                pltpu.VMEM((size // 2, width), low),
                pltpu.VMEM((size // 2, width), low),
                pltpu.VMEM((size // 4, width), low),
                pltpu.VMEM((size // 4, width), low),
                pltpu.VMEM((zs, size // (4 * zs), width), low),
            ]
    dma = pltpu.SemaphoreType.DMA
    count = len(chunks)
    return pl.pallas_call(
        functools.partial(
            total_kernel, arrays=len(arrays), chunks=tuple(chunks), zs=zs, tensor=tensor
        ),
        in_specs=[WHOLE] * (len(arrays) + 1) + [ANYWHERE],
        out_specs=(WHOLE,) * (len(arrays) + 1) + (ANYWHERE,),
        out_shape=tuple(jax.ShapeDtypeStruct(a.shape, a.dtype) for a in [*arrays, small])
        + (jax.ShapeDtypeStruct((tensor - 1, part.shape[0], part.shape[1] // tensor), low),),
        scratch_shapes=scratch
        + [
            pltpu.VMEM((2,) + small.shape, wide),
            pltpu.VMEM((2,) + small.shape, wide),
            pltpu.VMEM((zs,) + small.shape, wide),
            pltpu.VMEM((tensor,) + small.shape, wide),
        ]
        + [dma((count, 4))] * 2
        + [dma((count, 2, zs))] * 2
        + [dma((4, max(zs, tensor)))] * 2
        + [dma((tensor,))] * 2,
        compiler_params=params(collective_id=4, has_side_effects=True),
    )(*arrays, small, part)


def collect_kernel(
    kv_ref, query_ref, landed_ref, piece_ref, sum_ref,
    send_p, recv_p, send_a, recv_a, send_b, recv_b, local, *, ranks,
):
    heads, rows = kv_ref.shape[1:3]
    half = query_ref.shape[1]
    place = lax.axis_index("dp")
    head = place // ranks
    rank = lax.rem(place, ranks)
    greet(heads, ranks, head, rank, True)
    order = list(reversed(range(heads)))
    pieces = {}
    copies = []
    for step in order:
        to = peer(head, step, heads)
        for other in range(1, ranks):
            partner = lax.rem(rank + other, ranks)
            pieces[step, other] = remote(
                kv_ref.at[partner, to], piece_ref.at[other, to],
                send_p.at[step, other], recv_p.at[step, other], head * ranks + partner,
            )
            pieces[step, other].start()
        if step:
            copies.append(
                remote(
                    query_ref.at[to], landed_ref.at[head, pl.ds(rows, half)],
                    send_b.at[step], recv_b.at[step], to * ranks + rank,
                )
            )
        else:
            copies.append(
                pltpu.make_async_copy(
                    query_ref.at[head], landed_ref.at[head, pl.ds(rows, half)], local.at[0]
                )
            )
        copies[-1].start()
    for step in order:
        to = peer(head, step, heads)
        total = kv_ref[rank, to].astype(wide)
        for other in range(1, ranks):
            pieces[step, other].wait_recv()
            total = total + piece_ref[other, to].astype(wide)
        sum_ref[to] = total.astype(low)
        if step:
            copies.append(
                remote(
                    sum_ref.at[to], landed_ref.at[head, pl.ds(0, rows)],
                    send_a.at[step], recv_a.at[step], to * ranks + rank,
                )
            )
        else:
            copies.append(
                pltpu.make_async_copy(
                    sum_ref.at[head], landed_ref.at[head, pl.ds(0, rows)], local.at[1]
                )
            )
        copies[-1].start()
    for piece in pieces.values():
        piece.wait_send()
    for copy in copies:
        copy.wait()


def collect(kv, query):
    ranks, heads, rows = kv.shape[:3]
    dma = pltpu.SemaphoreType.DMA
    return pl.pallas_call(
        functools.partial(collect_kernel, ranks=ranks),
        in_specs=[WHOLE, WHOLE],
        out_specs=ANYWHERE,
        out_shape=jax.ShapeDtypeStruct((heads, rows + rows // 2, LANES), low),
        scratch_shapes=[
            pltpu.VMEM((ranks, heads, rows, LANES), low),
            pltpu.VMEM((heads, rows, LANES), low),
        ]
        + [dma((heads, ranks))] * 2
        + [dma((heads,))] * 4
        + [dma((2,))],
        compiler_params=params(collective_id=3, has_side_effects=True),
    )(kv, query)


def tables(times):
    half = HD // 2
    lane = np.arange(LANES)
    inverse = (10000.0 ** (-2.0 * (lane % half) / HD)).astype(np.float32)
    sign = np.where(lane % HD < half, -1.0, 1.0).astype(np.float32)
    angles = times.astype(wide)[:, None] * inverse[None, :]
    return jnp.cos(angles), jnp.sin(angles) * sign[None, :]


def keep_order(x):
    return with_layout_constraint(x, Layout(major_to_minor=tuple(range(x.ndim))))


def id_rows(x):
    rows = x.reshape(-1, LANES).astype(low)
    return jnp.pad(rows, ((0, IDS // 2 - rows.shape[0]), (0, 0)))


def shards(
    tokens,
    cotangent,
    segment,
    variate,
    time,
    w_qkv,
    w_out,
    w_gateup,
    w_down,
    attn_gain,
    mlp_gain,
    query_gain,
    key_gain,
    var_bias,
):
    rows = tokens.shape[0]
    local_width = w_qkv.shape[2]
    heads = local_width // HD
    dp = lax.axis_size("dp")
    tensor = lax.axis_size("tensor")
    ranks = dp // heads
    place = lax.axis_index("dp")
    rank_here = lax.rem(place, ranks)
    width_share = tokens.shape[1] // tensor
    tensor_start = lax.axis_index("tensor") * width_share

    def tensor_sum(x, x_low):
        if tensor == 2:
            return x + lax.ppermute(x_low, "tensor", [(0, 1), (1, 0)]).astype(wide)
        return lax.psum(x_low, "tensor").astype(wide)

    def share_of(x):
        return lax.dynamic_slice_in_dim(x, tensor_start, width_share, 1).astype(wide)

    def share_sum(x, others):
        return share_of(x) + jnp.sum(others.astype(wide), axis=0)

    depth = tokens.shape[1]
    cosine, sine = tables(time)
    message, raw_query, raw_key, normed_one = project(
        tokens, w_qkv, attn_gain[None, :], query_gain[None, :], key_gain[None, :], cosine, sine,
        segment.reshape(-1, LANES), variate.reshape(-1, LANES),
    )
    kv, query_in, w_others = spread(message, w_out, ranks, rows, tensor)
    key_op, value_op, query_op, exact, out_message, runs = forward_attention(var_bias, kv, query_in)
    landed = share_out(out_message, ranks, tensor)
    heads_out, middle, normed_two, hidden, grad_gu, middle_part, middle_low, mlp_gain_part = out_and_mlp(
        landed, tokens, cotangent, mlp_gain[None, :], w_out, w_others, w_gateup, w_down
    )
    grad_down = jnp.einsum("tf,te->fe", hidden, cotangent, preferred_element_type=wide)
    grad_gateup = jnp.einsum("td,ktf->kdf", normed_two, grad_gu, preferred_element_type=wide)
    early = (keep_order(grad_gateup.astype(low)), grad_down.astype(low))
    mlp_part = jnp.dot(hidden, w_down, preferred_element_type=wide).astype(low)
    normed_turned = normed_one.T
    grad_middle = cotangent.astype(wide) + tensor_sum(middle_part, middle_low)
    grad_middle_low = grad_middle.astype(low)
    grad_middle_low, mlp_part, normed_turned = lax.optimization_barrier(
        (grad_middle_low, mlp_part, normed_turned)
    )
    grad_out = jnp.einsum("tc,td->cd", heads_out, grad_middle_low, preferred_element_type=wide)
    early = lax.psum((*early, grad_out.astype(low)), "dp")
    out_sum = early[2]
    grad_landed, mlp_others = exchange(
        grad_heads_of(grad_middle_low, w_out), mlp_part, ranks, tensor
    )
    output = (share_of(middle) + share_sum(mlp_part, mlp_others)).astype(low)
    own_ids = lax.dynamic_index_in_dim(kv[:, :, rows:], rank_here, 0, False)
    back_kv, back_query, bias_tiles = backward_attention(
        runs, key_op, value_op, query_op, exact, grad_landed, own_ids
    )
    grad_qkv, input_part, small = tail(
        collect(back_kv, back_query), raw_query, raw_key, query_gain[None, :], key_gain[None, :],
        cosine, sine, tokens, attn_gain[None, :], normed_turned, w_qkv, mlp_gain_part, bias_tiles, ranks,
    )
    qkv_sum, small, input_others = total_sums([grad_qkv], small, input_part, dp, tensor)
    grad_input = share_of(grad_middle) + share_sum(input_part, input_others)
    flat = lambda x: x.reshape(-1, x.shape[-1])
    (qkv_wide,) = widen([flat(qkv_sum)])
    gateup_wide, out_wide, down_wide = widen([flat(early[0]), out_sum, early[1]])
    count = 2 * depth // LANES
    gains = small[:count].reshape(2, depth)
    head_gains = small[count : count + 2, :HD] + small[count : count + 2, HD:]
    bias_sum = lax.dynamic_slice_in_dim(
        small[count + 2 : count + 4], lax.axis_index("tensor") * heads, heads, 1
    )
    return (
        output,
        grad_input,
        qkv_wide.reshape(w_qkv.shape),
        out_wide,
        gateup_wide.reshape(w_gateup.shape),
        down_wide,
        gains[0],
        gains[1],
        head_gains[0],
        head_gains[1],
        bias_sum,
    )


def solution(mesh):
    placed = (
        P("dp", None),
        P("dp", None),
        P("dp"),
        P("dp"),
        P("dp"),
        P(None, None, "tensor"),
        P("tensor", None),
        P(None, None, "tensor"),
        P("tensor", None),
        P(),
        P(),
        P(),
        P(),
        P(None, "tensor"),
    )
    return jax.shard_map(
        shards,
        mesh=mesh,
        in_specs=placed,
        out_specs=(
            P("dp", "tensor"),
            P("dp", "tensor"),
            P(None, None, "tensor"),
            P("tensor", None),
            P(None, None, "tensor"),
            P("tensor", None),
            P(),
            P(),
            P(),
            P(),
            P(None, "tensor"),
        ),
        check_vma=False,
    )
```
